128 devices in a mesh: section: 2 (over core), context: 2 (over x_lo), expert: 8 (over x_hi, y), dp: 4 (over z).
Axes of the slice: x: 4 (x_hi: 2, x_lo: 2; x = x_hi * 2 + x_lo), y: 4, z: 4, core: 2. Of those that a mesh axis runs over, the one named last changes fastest.
Arguments:
- tokens: bfloat16 [2, 32, 320, 768], P(None, ('expert', 'dp'), 'context'), may hold values from -6 to 6
- cotangent: bfloat16 [2, 32, 320, 768], P(None, ('expert', 'dp'), 'context'), may hold values from -6 to 6
- expert_route: int32 [2, 2, 32, 320], P('section', None, ('expert', 'dp'), 'context'), may hold values from 0 to 7, as said below
- capacity_slot: int32 [2, 2, 32, 320], P('section', None, ('expert', 'dp'), 'context'), may hold values from 0 to 30, as said below
- buckets: int32 [639], replicated, may hold values from 0 to 31
- qkv_weight: bfloat16 [2, 768, 2304], P('section'), may hold values from -0.21875 to 0.21875
- attention_out: bfloat16 [2, 768, 768], P('section'), may hold values from -1.25 to 1.25
- relative_bias: float32 [2, 32, 12], P('section'), may hold values from -4 to 4
- attention_gain: float32 [2, 768], P('section'), may hold values from 0.5 to 1.5
- mixture_gain: float32 [2, 768], P('section'), may hold values from 0.5 to 1.5
- router: float32 [2, 768, 8], P('section'), may hold values from -0.15625 to 0.15625
- expert_in: bfloat16 [2, 8, 768, 3072], P('section', 'expert'), may hold values from -0.21875 to 0.21875
- expert_out: bfloat16 [2, 8, 3072, 768], P('section', 'expert'), may hold values from -0.875 to 0.875
Outputs:
- hidden_states: bfloat16 [2, 2, 32, 320, 768], P('section', None, ('expert', 'dp'), 'context')
- input_grads: float32 [2, 2, 32, 320, 768], P('section', None, ('expert', 'dp'), 'context')
- qkv_grad: float32 [2, 768, 2304], P('section', ('context', 'expert', 'dp'))
- attention_grad: float32 [2, 768, 768], P('section', ('context', 'expert', 'dp'))
- relative_grad: float32 [2, 32, 12], P('section')
- attention_gain_grad: float32 [2, 768], P('section')
- mixture_gain_grad: float32 [2, 768], P('section')
- router_grad: float32 [2, 768, 8], P('section')
- expert_in_grad: float32 [2, 8, 768, 3072], P('section', 'expert', None, ('context', 'dp'))
- expert_out_grad: float32 [2, 8, 3072, 768], P('section', 'expert', ('context', 'dp'))
The draws below stay inside these ranges and needn't reach their ends.
Inputs may be any that keep to these rules, and one draw needn't show every extreme that they name: `expert_route`: within each block of 160 consecutive positions of one sequence and layer, one expert drawn from the seed receives exactly 31 tokens at positions drawn from the seed; the other tokens of the block are spread as evenly as possible over the other experts. `capacity_slot`: for each block of 160 positions and each expert, the tokens routed there carry the slots 0, 1, 2, ... once each, in an order drawn from the seed; those with slot 25 or more are dropped by the expert.
All inputs are finite; a program needn't handle non-finite values.
Results may differ from the reference program's by a relative error of at most 0.024.
Values may be sent and summed in bfloat16 or wider, within the bound.
No kernel may reach another device: no remote copies, remote signals or barrier semaphores. Data moves between devices by JAX's collectives and lax.ppermute only.
A program may use at most 192 MiB of HBM per device.

```python
import math
import jax
import jax.numpy as jnp
from jax import lax

D = 768
H = 12
HD = 64
FF = 3072
NB = 32
SEQ_DEV = 160
MICRO = 2
EXPERTS = 8
CAP = 25
SEQ = 320
BATCH = 32


def routing_pair(key):
    key = jax.random.fold_in(key, 7)
    block_count = 2 * MICRO * BATCH * SEQ // SEQ_DEV
    forced = CAP + 1 + SEQ_DEV // (4 * EXPERTS)
    key_heavy, key_order, key_rank = jax.random.split(key, 3)
    heavy_expert = jax.random.randint(key_heavy, (block_count, 1), 0, EXPERTS).astype(jnp.int32)
    order_rank = jax.vmap(lambda subkey: jax.random.permutation(subkey, SEQ_DEV))(jax.random.split(key_order, block_count)).astype(jnp.int32)
    ranking = jax.vmap(lambda subkey: jax.random.permutation(subkey, SEQ_DEV))(jax.random.split(key_rank, block_count)).astype(jnp.int32)
    others = (heavy_expert + 1 + jnp.maximum(order_rank - forced, 0) % (EXPERTS - 1)) % EXPERTS
    routes = jnp.where(order_rank < forced, heavy_expert, others).astype(jnp.int32)
    same_expert = routes[:, :, None] == routes[:, None, :]
    before = ranking[:, None, :] < ranking[:, :, None]
    slot_rank = jnp.sum((same_expert & before).astype(jnp.int32), axis=2).astype(jnp.int32)
    full_shape = (2, MICRO, BATCH, SEQ)
    return (routes.reshape(full_shape), slot_rank.reshape(full_shape))


def draw_expert_route(key, part):
    return routing_pair(key)[0]


def draw_capacity_slot(key, part):
    return routing_pair(key)[1]


def touch_ends(result, stream_key, least, high):
    index_at = [jax.random.randint(jax.random.fold_in(stream_key, axis), (), 0, length) for axis, length in enumerate(result.shape)]
    longest = result.shape.index(max(result.shape))
    beside = index_at[:longest] + [(index_at[longest] + 1) % result.shape[longest]] + index_at[longest + 1:]
    return result.at[tuple(index_at)].set(least).at[tuple(beside)].set(high)


def levels(own_key, extent, shards, least, top_value):
    loudness = 1.0
    for dim, blocks in shards:
        draws = jax.random.uniform(jax.random.fold_in(jax.random.fold_in(own_key, 6), dim), (blocks,), jnp.float32, least / len(shards), top_value / len(shards))
        loudness = loudness * jnp.repeat(jnp.exp(draws), extent[dim] // blocks).reshape((-1,) + (1,) * (len(extent) - 1 - dim))
    return loudness


def gaussian(own_key, shape, spread, reach, shards=(), kind=jnp.bfloat16):
    values = spread * jax.random.normal(own_key, shape, jnp.float32)
    if shards:
        values = values * levels(own_key, shape, shards, -0.22, 0.18)
    return jnp.clip(values, -reach, reach).astype(kind)


def setup_inputs(seed: int = 0) -> dict:
    streams_of = jax.random.split(jax.random.key(seed), 14)
    tokens = gaussian(streams_of[0], (MICRO, BATCH, SEQ, D), 1.0, 6.0, ((1, 32), (2, 2)))
    cotangent = gaussian(streams_of[1], (MICRO, BATCH, SEQ, D), 1.0, 6.0, ((1, 32), (2, 2)))
    expert_route = draw_expert_route(jax.random.fold_in(streams_of[13], 71), 0)
    capacity_slot = draw_capacity_slot(jax.random.fold_in(streams_of[13], 71), 0)
    buckets = touch_ends(jax.random.randint(streams_of[4], (2 * SEQ - 1,), 0, NB), jax.random.fold_in(streams_of[4], 1), 0, NB - 1).astype(jnp.int32)
    qkv_weight = gaussian(streams_of[5], (2, D, 3 * D), D ** -0.5, 0.21875, ((0, 2),))
    attention_out = gaussian(streams_of[6], (2, D, D), (D // 32) ** -0.5, 1.25, ((0, 2),))
    relative_bias = gaussian(streams_of[7], (2, NB, H), 1.0, 4.0, ((0, 2),), jnp.float32)
    attention_gain = jnp.clip(1.0 + 0.1 * jax.random.normal(streams_of[8], (2, D), jnp.float32), 0.5, 1.5)
    mixture_gain = jnp.clip(1.0 + 0.1 * jax.random.normal(streams_of[9], (2, D), jnp.float32), 0.5, 1.5)
    router = gaussian(streams_of[10], (2, D, EXPERTS), (2 * D) ** -0.5, 0.15625, ((0, 2),), jnp.float32)
    expert_in = gaussian(streams_of[11], (2, EXPERTS, D, FF), D ** -0.5, 0.21875, ((0, 2), (1, 8)))
    expert_out = gaussian(streams_of[12], (2, EXPERTS, FF, D), (FF // (8 * EXPERTS)) ** -0.5, 0.875, ((0, 2), (1, 8)))
    return dict(tokens=tokens, cotangent=cotangent, expert_route=expert_route, capacity_slot=capacity_slot, buckets=buckets, qkv_weight=qkv_weight, attention_out=attention_out, relative_bias=relative_bias, attention_gain=attention_gain, mixture_gain=mixture_gain, router=router, expert_in=expert_in, expert_out=expert_out)


@jax.custom_vjp
def low(v):
    return lax.optimization_barrier(v.astype(jnp.bfloat16)).astype(jnp.float32)

@jax.custom_vjp
def low_back(v):
    return v

def low_keep(v):
    return (low(v), None)

def low_pass(kept, grad):
    return (grad,)

def back_keep(v):
    return (v, None)

def back_low(kept, grad):
    return (low(grad),)
low.defvjp(low_keep, low_pass)
low_back.defvjp(back_keep, back_low)
largest_logit = lax.Precision.HIGHEST
eps = 1e-06

def rms_scale(values):
    return lax.rsqrt(lax.optimization_barrier(jnp.mean(values * values, axis=-1, keepdims=True)) + eps)

def attention_part(hidden, qkv_weight, attention_out, relative_offset, attention_gain, buckets):
    seq_count = hidden.shape[0]
    normed = low(hidden * rms_scale(hidden) * attention_gain)
    projected = low_back(low(jnp.einsum('nsd,de->nse', normed, qkv_weight, precision=largest_logit)))
    positions = jnp.arange(SEQ, dtype=jnp.int32)
    offsets = positions[None, :] - positions[:, None] + (SEQ - 1)
    bias = jnp.transpose(relative_offset[buckets[offsets]], (2, 0, 1))
    group_size = math.gcd(max(1, 4096 // SEQ), seq_count)

    def attend(block):
        queries = block[..., :D].reshape(group_size, SEQ, H, HD)
        keys = block[..., D:2 * D].reshape(group_size, SEQ, H, HD)
        values = block[..., 2 * D:].reshape(group_size, SEQ, H, HD)
        attention_scores = jnp.einsum('nqhd,nkhd->nhqk', queries, keys, precision=largest_logit) * 0.125 + bias[None]
        probs_all = jax.nn.softmax(low_back(attention_scores), axis=-1)
        attended = jnp.einsum('nhqk,nkhd->nqhd', low(probs_all), values, precision=largest_logit)
        return low_back(low(attended.reshape(group_size, SEQ, D)))
    attended = lax.map(jax.checkpoint(attend), projected.reshape(seq_count // group_size, group_size, SEQ, 3 * D))
    attended = attended.reshape(seq_count, SEQ, D)
    branch = low_back(jnp.einsum('nsd,de->nse', attended, attention_out, precision=largest_logit))
    return hidden + branch

def mixture_part(hidden, mixture_gain, router, expert_in, expert_out, expert_route, capacity_slot):
    seq_count = hidden.shape[0]
    normed = hidden * rms_scale(hidden) * mixture_gain
    logits = jnp.einsum('nsd,de->nse', normed, router, precision=largest_logit)
    router_probs = jax.nn.softmax(logits, axis=-1)
    chosen = (expert_route[..., None] == jnp.arange(EXPERTS, dtype=jnp.int32)).astype(jnp.float32)
    gate_value = lax.optimization_barrier(jnp.sum(router_probs * chosen, axis=-1, keepdims=True))
    sent = low_back(low(normed))
    block_count = seq_count * SEQ // SEQ_DEV
    target = jnp.where(capacity_slot < CAP, expert_route * CAP + capacity_slot, -1).reshape(block_count, SEQ_DEV)
    slot_map = (target[:, None, :] == jnp.arange(EXPERTS * CAP, dtype=jnp.int32)[None, :, None]).astype(jnp.float32)
    rows_in = jnp.einsum('bjt,btd->bjd', slot_map, sent.reshape(block_count, SEQ_DEV, D), precision=largest_logit)
    rows_in = jnp.transpose(rows_in.reshape(block_count, EXPERTS, CAP, D), (1, 0, 2, 3)).reshape(EXPERTS, block_count * CAP, D)

    def expert(operands):
        received, weight_in, weight_out = operands
        inner_act = low_back(jnp.dot(received, weight_in, precision=largest_logit))
        active = low(jax.nn.gelu(inner_act))
        return low_back(low(jnp.dot(active, weight_out, precision=largest_logit)))
    rows_out = lax.map(jax.checkpoint(expert), (rows_in, expert_in, expert_out))
    rows_out = jnp.transpose(rows_out.reshape(EXPERTS, block_count, CAP, D), (1, 0, 2, 3)).reshape(block_count, EXPERTS * CAP, D)
    combined = jnp.einsum('bjt,bjd->btd', slot_map, rows_out, precision=largest_logit).reshape(hidden.shape)
    return hidden + gate_value * combined

def layer(hidden, layer_index, weights, expert_route, capacity_slot, buckets):
    qkv_all, out_all, relative_all, gain_attn, gain_mix, router_all, in_all, out_experts = weights
    seq_count = hidden.shape[0]
    middle = attention_part(hidden, qkv_all[layer_index], out_all[layer_index], relative_all[layer_index], gain_attn[layer_index], buckets)
    return mixture_part(middle, gain_mix[layer_index], router_all[layer_index], in_all[layer_index], out_experts[layer_index], expert_route[layer_index].reshape(seq_count, SEQ), capacity_slot[layer_index].reshape(seq_count, SEQ))

def reference(tokens, cotangent, expert_route, capacity_slot, buckets, qkv_weight, attention_out, relative_bias, attention_gain, mixture_gain, router, expert_in, expert_out):
    seq_count = MICRO * BATCH

    def forward(inputs, zero_shift, *weights):
        first_out = low(layer(inputs, 0, weights, expert_route, capacity_slot, buckets))
        second_in = low_back(first_out + zero_shift)
        return (layer(second_in, 1, weights, expert_route, capacity_slot, buckets), first_out)
    inputs = tokens.astype(jnp.float32).reshape(seq_count, SEQ, D)
    zero_shift = jnp.zeros_like(inputs)
    weights = tuple((array.astype(jnp.float32) for array in (qkv_weight, attention_out, relative_bias, attention_gain, mixture_gain, router, expert_in, expert_out)))
    second_out, pullback, first_out = jax.vjp(forward, inputs, zero_shift, *weights, has_aux=True)
    grads = pullback(cotangent.astype(jnp.float32).reshape(seq_count, SEQ, D))
    hidden_states = jnp.stack([first_out, second_out]).reshape(2, MICRO, BATCH, SEQ, D).astype(jnp.bfloat16)
    input_grads = jnp.stack([grads[0], grads[1]]).reshape(2, MICRO, BATCH, SEQ, D)
    return (hidden_states, input_grads, grads[2], grads[3], grads[4], grads[5], grads[6], grads[7], grads[8], grads[9])
```

```python
import functools

import jax
import jax.numpy as jnp
from jax import lax
from jax.experimental import pallas as pl
from jax.experimental.pallas import tpu as pltpu
from jax.sharding import PartitionSpec as P

BF = jnp.bfloat16
F32 = jnp.float32
HIGH = lax.Precision.HIGHEST
EPS = 1e-06
HEAD = 64
PAIR = 2 * HEAD
SLOTS = 32
SHIFT = 512
SWAP = [(0, 1), (1, 0)]
NN = (((1,), (0,)), ((), ()))
NT = (((1,), (1,)), ((), ()))
TN = (((0,), (0,)), ((), ()))


def mm(a, b, dims=NN, precision=None):
    return lax.dot_general(a, b, dims, precision=precision, preferred_element_type=F32)


def full(shape):
    return pl.BlockSpec(shape, lambda: (0,) * len(shape))


VM = pl.BlockSpec(memory_space=pltpu.VMEM)
SM = pl.BlockSpec(memory_space=pltpu.SMEM)
ANY = pl.BlockSpec(memory_space=pl.ANY)


def params(mib):
    return pltpu.CompilerParams(vmem_limit_bytes=mib * 1024 * 1024)


def cost(flops, size):
    return pl.CostEstimate(flops=int(flops), bytes_accessed=int(size), transcendentals=0)


def col_cuts(width, step):
    return [(slice(None), pl.ds(at, step)) for at in range(0, width, step)]


def row_cuts(height, step):
    return [(pl.ds(at, step), slice(None)) for at in range(0, height, step)]


def fetch(sec, layer, own, other, dst, sems, cuts, base=0):
    def go(src):
        for index, cut in enumerate(cuts):
            pltpu.make_async_copy(src.at[cut], dst.at[cut], sems.at[base + index]).start()

    pl.when(sec == layer)(lambda: go(own))
    pl.when(sec != layer)(lambda: go(other))


def arrive(own, dst, sems, cuts, index, base=0):
    cut = cuts[index]
    pltpu.make_async_copy(own.at[cut], dst.at[cut], sems.at[base + index]).wait()


def rms(values):
    return lax.rsqrt(jnp.mean(values * values, axis=-1, keepdims=True) + EPS)


def slot_rows(code_row, rows, capacity):
    target = jnp.where((code_row & (SLOTS - 1)) < capacity, code_row, -1)
    return (
        lax.broadcasted_iota(jnp.int32, (rows, code_row.shape[1]), 0) == target
    ).astype(F32).astype(BF)


def slot_cols(code_col, rows, capacity):
    target = jnp.where((code_col & (SLOTS - 1)) < capacity, code_col, -1)
    return (
        lax.broadcasted_iota(jnp.int32, (code_col.shape[0], rows), 1) == target
    ).astype(F32).astype(BF)


def project(normed, w_own, w_scr, sems, cuts, qkv_ref, base=0):
    step = w_scr.shape[1] // len(cuts)
    for index in range(len(cuts)):
        arrive(w_own, w_scr, sems, cuts, index, base)
        part = slice(index * step, (index + 1) * step)
        qkv_ref[:, part] = mm(normed, w_scr[:, part]).astype(BF)


def bias_kernel(vec_ref, out_ref):
    layers, heads, rows, width = out_ref.shape
    lanes = vec_ref.shape[2]
    sub = lax.broadcasted_iota(jnp.int32, (8, lanes), 0)
    for layer in range(layers):
        for head in range(heads):
            base = jnp.broadcast_to(vec_ref[layer, head : head + 1, :], (8, lanes))
            for bit in (1, 2, 4):
                base = jnp.where((sub & bit) != 0, pltpu.roll(base, bit, 1), base)
            for block in range(rows // 8):
                moved = pltpu.roll(base, (8 * block - (rows - 1)) % lanes, 1)
                out_ref[layer, head, 8 * block : 8 * block + 8, :] = moved[:, :width]


def bias_table(vectors, rows, width):
    layers, heads, _ = vectors.shape
    return pl.pallas_call(
        bias_kernel,
        out_shape=jax.ShapeDtypeStruct((layers, heads, rows, width), F32),
        in_specs=[VM],
        out_specs=VM,
        compiler_params=params(24),
        name="bias_table",
    )(vectors)


def first_kernel(layer, sec_ref, x_ref, gain_ref, w_own, w_other, normed_ref, qkv_ref, w_scr, sems):
    cuts = col_cuts(w_scr.shape[1], w_scr.shape[1] // 3)
    fetch(sec_ref[0], layer, w_own, w_other, w_scr, sems, cuts)
    x = x_ref[...].astype(F32)
    normed = (x * rms(x) * gain_ref[...]).astype(BF)
    normed_ref[...] = normed
    project(normed, w_own, w_scr, sems, cuts, qkv_ref)


def first_projection(layer, sec, x, gain, w):
    rows, width = x.shape
    wide = w[0].shape[1]
    return pl.pallas_call(
        functools.partial(first_kernel, layer),
        out_shape=(
            jax.ShapeDtypeStruct((rows, width), BF),
            jax.ShapeDtypeStruct((rows, wide), BF),
        ),
        in_specs=[SM, VM, VM, ANY, ANY],
        out_specs=(VM, VM),
        scratch_shapes=[pltpu.VMEM((width, wide), BF), pltpu.SemaphoreType.DMA((3,))],
        compiler_params=params(24),
        cost_estimate=cost(2 * rows * width * wide, 2 * width * wide),
        name="first_projection",
    )(sec, x, gain, *w)


def attend_kernel(
    layer,
    capacity,
    sec_ref,
    x_ref,
    qkv_ref,
    kv_ref,
    gain_ref,
    router_ref,
    row_ref,
    col_ref,
    bias_hbm,
    wo_own,
    wo_other,
    mid_ref,
    probs_ref,
    att_ref,
    p_ref,
    out_ref,
    kv_scr,
    bias_scr,
    wo_scr,
    sems,
):
    sec = sec_ref[0]
    rows, width = x_ref.shape
    total = kv_scr.shape[0]
    pairs = width // PAIR
    for pair in range(pairs):
        pltpu.make_async_copy(
            bias_hbm.at[layer, pl.ds(2 * pair, 2)], bias_scr.at[pl.ds(2 * pair, 2)], sems.at[pair]
        ).start()
    cuts = [(slice(None), slice(None))]
    fetch(sec, layer, wo_own, wo_other, wo_scr, sems, cuts, pairs)
    kv_scr[pl.ds(pl.multiple_of(sec * rows, rows), rows), :] = qkv_ref[:, width:]
    kv_scr[pl.ds(pl.multiple_of((1 - sec) * rows, rows), rows), :] = kv_ref[...]
    low = lax.broadcasted_iota(jnp.int32, (rows, PAIR), 1) < HEAD
    zero = jnp.zeros((rows, PAIR), BF)
    for pair in range(pairs):
        part = slice(pair * PAIR, (pair + 1) * PAIR)
        q = qkv_ref[:, part]
        k = kv_scr[:, part]
        v = kv_scr[:, width + pair * PAIR : width + (pair + 1) * PAIR]
        pltpu.make_async_copy(
            bias_hbm.at[layer, pl.ds(2 * pair, 2)], bias_scr.at[pl.ds(2 * pair, 2)], sems.at[pair]
        ).wait()
        both = []
        for side in range(2):
            head = 2 * pair + side
            masked = jnp.where(low, q, zero) if side == 0 else jnp.where(low, zero, q)
            scores = mm(masked, k, NT) * 0.125 + bias_scr[head, :, :total]
            top = jnp.max(scores, axis=-1, keepdims=True)
            raised = jnp.exp(scores - top)
            share = (raised * (1.0 / jnp.sum(raised, axis=-1, keepdims=True))).astype(BF)
            p_ref[head] = share
            both.append(mm(share, v))
        att_ref[:, part] = jnp.where(low, both[0], both[1]).astype(BF)
    arrive(wo_own, wo_scr, sems, cuts, 0, pairs)
    middle = x_ref[...].astype(F32) + mm(att_ref[...], wo_scr[...])
    mid_ref[...] = middle
    normed = middle * rms(middle) * gain_ref[...]
    logits = mm(normed, router_ref[...], NN, HIGH)
    raised = jnp.exp(logits - jnp.max(logits, axis=-1, keepdims=True))
    probs_ref[...] = raised / jnp.sum(raised, axis=-1, keepdims=True)
    slots = slot_rows(row_ref[...], out_ref.shape[0], capacity)
    out_ref[...] = mm(slots, normed.astype(BF)).astype(BF)


def attend(layer, capacity, sec, x, qkv, kv_other, gain, router, code_row, code_col, bias, wo):
    rows, width = x.shape
    experts = router.shape[1]
    heads = width // HEAD
    wide = bias.shape[3]
    return pl.pallas_call(
        functools.partial(attend_kernel, layer, capacity),
        out_shape=(
            jax.ShapeDtypeStruct((rows, width), F32),
            jax.ShapeDtypeStruct((rows, experts), F32),
            jax.ShapeDtypeStruct((rows, width), BF),
            jax.ShapeDtypeStruct((heads, rows, 2 * rows), BF),
            jax.ShapeDtypeStruct((experts * SLOTS, width), BF),
        ),
        in_specs=[SM] + [VM] * 7 + [ANY] * 3,
        out_specs=(VM,) * 5,
        scratch_shapes=[
            pltpu.VMEM((2 * rows, 2 * width), BF),
            pltpu.VMEM((heads, rows, wide), F32),
            pltpu.VMEM((width, width), BF),
            pltpu.SemaphoreType.DMA((heads // 2 + 1,)),
        ],
        compiler_params=params(40),
        cost_estimate=cost(4e9, 6e6),
        name="attend",
    )(sec, x, qkv, kv_other, gain, router, code_row, code_col, bias, *wo)


def expert_kernel(
    layer, sec_ref, rec_ref, in_own, in_other, out_own, out_other, res_ref, act_ref, slope_ref, win, wout, sems
):
    sec = sec_ref[0]
    hidden = win.shape[1]
    step = 512
    count = hidden // step
    in_cuts = col_cuts(hidden, step)
    out_cuts = row_cuts(hidden, step)
    fetch(sec, layer, in_own, in_other, win, sems, in_cuts)
    fetch(sec, layer, out_own, out_other, wout, sems, out_cuts, count)
    rec = rec_ref[...]
    total = None
    for index in range(count):
        part = slice(index * step, (index + 1) * step)
        arrive(in_own, win, sems, in_cuts, index)
        v = mm(rec, win[:, part])
        square = v * v
        t = jnp.tanh(v * (0.7978845608028654 + 0.035677408136300125 * square))
        half = 0.5 * (1.0 + t)
        active = (v * half).astype(BF)
        act_ref[:, part] = active
        slope = half + 0.5 * v * (1.0 - t * t) * (0.7978845608028654 + 0.10703222440890037 * square)
        slope_ref[:, part] = slope.astype(BF)
        arrive(out_own, wout, sems, out_cuts, index, count)
        fresh = mm(active, wout[part, :])
        total = fresh if total is None else total + fresh
    res_ref[...] = total.astype(BF)


def expert_forward(layer, sec, received, w_in, w_out):
    rows, width = received.shape
    hidden = w_in[0].shape[1]
    return pl.pallas_call(
        functools.partial(expert_kernel, layer),
        out_shape=(
            jax.ShapeDtypeStruct((rows, width), BF),
            jax.ShapeDtypeStruct((rows, hidden), BF),
            jax.ShapeDtypeStruct((rows, hidden), BF),
        ),
        in_specs=[SM, VM] + [ANY] * 4,
        out_specs=(VM,) * 3,
        scratch_shapes=[
            pltpu.VMEM((width, hidden), BF),
            pltpu.VMEM((hidden, width), BF),
            pltpu.SemaphoreType.DMA((2 * (hidden // 512),)),
        ],
        compiler_params=params(40),
        cost_estimate=cost(4 * rows * width * hidden, 4 * width * hidden),
        name="expert_forward",
    )(sec, received, *w_in, *w_out)


def gate_of(probs, code_col):
    lane = lax.broadcasted_iota(jnp.int32, probs.shape, 1)
    chosen = (lane == code_col // SLOTS).astype(F32)
    return chosen, jnp.sum(probs * chosen, axis=-1, keepdims=True)


def join_kernel(
    layer,
    capacity,
    sec_ref,
    mid_ref,
    ret_ref,
    probs_ref,
    col_ref,
    gain_ref,
    w_own,
    w_other,
    comb_ref,
    hid_ref,
    normed_ref,
    qkv_ref,
    w_scr,
    sems,
):
    cuts = col_cuts(w_scr.shape[1], w_scr.shape[1] // 3)
    fetch(sec_ref[0], layer, w_own, w_other, w_scr, sems, cuts)
    col = col_ref[...]
    combined = mm(slot_cols(col, ret_ref.shape[0], capacity), ret_ref[...])
    comb_ref[...] = combined.astype(BF)
    _, gate = gate_of(probs_ref[...], col)
    hidden = (mid_ref[...] + gate * combined).astype(BF)
    hid_ref[...] = hidden
    x = hidden.astype(F32)
    normed = (x * rms(x) * gain_ref[...]).astype(BF)
    normed_ref[...] = normed
    project(normed, w_own, w_scr, sems, cuts, qkv_ref)


def join(layer, capacity, sec, middle, returned, probs, code_col, gain, w):
    rows, width = middle.shape
    wide = w[0].shape[1]
    return pl.pallas_call(
        functools.partial(join_kernel, layer, capacity),
        out_shape=(
            jax.ShapeDtypeStruct((rows, width), BF),
            jax.ShapeDtypeStruct((rows, width), BF),
            jax.ShapeDtypeStruct((rows, width), BF),
            jax.ShapeDtypeStruct((rows, wide), BF),
        ),
        in_specs=[SM] + [VM] * 5 + [ANY] * 2,
        out_specs=(VM,) * 4,
        scratch_shapes=[pltpu.VMEM((width, wide), BF), pltpu.SemaphoreType.DMA((3,))],
        compiler_params=params(24),
        cost_estimate=cost(2 * rows * width * wide, 2 * width * wide),
        name="join",
    )(sec, middle, returned, probs, code_col, gain, *w)


def send_back(g, combined, probs, row, col, rows, capacity):
    _, gate = gate_of(probs, col)
    gate_grad = jnp.sum(g * combined, axis=-1, keepdims=True)
    placed = mm(slot_rows(row, rows, capacity), (gate * g).astype(BF))
    return gate_grad, placed.astype(BF)


def turn_kernel(
    capacity, mid_ref, ret_ref, probs_ref, row_ref, col_ref, cot_ref, hid_ref, gate_grad_ref, out_ref
):
    col = col_ref[...]
    probs = probs_ref[...]
    combined = mm(slot_cols(col, ret_ref.shape[0], capacity), ret_ref[...])
    _, gate = gate_of(probs, col)
    hid_ref[...] = (mid_ref[...] + gate * combined).astype(BF)
    gate_grad_ref[...], out_ref[...] = send_back(
        cot_ref[...].astype(F32), combined, probs, row_ref[...], col, out_ref.shape[0], capacity
    )


def turn(capacity, middle, returned, probs, code_row, code_col, cotangent):
    rows, width = middle.shape
    return pl.pallas_call(
        functools.partial(turn_kernel, capacity),
        out_shape=(
            jax.ShapeDtypeStruct((rows, width), BF),
            jax.ShapeDtypeStruct((rows, 1), F32),
            jax.ShapeDtypeStruct(returned.shape, BF),
        ),
        in_specs=[VM] * 6,
        out_specs=(VM,) * 3,
        compiler_params=params(24),
        cost_estimate=cost(4 * rows * width * returned.shape[0], 3e6),
        name="turn",
    )(middle, returned, probs, code_row, code_col, cotangent)


def expert_back_kernel(
    layer, sec_ref, rec_ref, slope_ref, in_own, in_other, out_own, out_other, sent_ref, grad_ref, win, wout, sems
):
    sec = sec_ref[0]
    hidden = win.shape[1]
    step = 512
    count = hidden // step
    in_cuts = col_cuts(hidden, step)
    out_cuts = row_cuts(hidden, step)
    fetch(sec, layer, out_own, out_other, wout, sems, out_cuts, count)
    fetch(sec, layer, in_own, in_other, win, sems, in_cuts)
    rec = rec_ref[...]
    total = None
    for index in range(count):
        part = slice(index * step, (index + 1) * step)
        arrive(out_own, wout, sems, out_cuts, index, count)
        inner = (mm(rec, wout[part, :], NT) * slope_ref[:, part].astype(F32)).astype(BF)
        grad_ref[:, part] = inner
        arrive(in_own, win, sems, in_cuts, index)
        fresh = mm(inner, win[:, part], NT)
        total = fresh if total is None else total + fresh
    sent_ref[...] = total.astype(BF)


def expert_backward(layer, sec, received, slope, w_in, w_out):
    rows, width = received.shape
    hidden = w_in[0].shape[1]
    return pl.pallas_call(
        functools.partial(expert_back_kernel, layer),
        out_shape=(
            jax.ShapeDtypeStruct((rows, width), BF),
            jax.ShapeDtypeStruct((rows, hidden), BF),
        ),
        in_specs=[SM, VM, VM] + [ANY] * 4,
        out_specs=(VM,) * 2,
        scratch_shapes=[
            pltpu.VMEM((width, hidden), BF),
            pltpu.VMEM((hidden, width), BF),
            pltpu.SemaphoreType.DMA((2 * (hidden // 512),)),
        ],
        compiler_params=params(40),
        cost_estimate=cost(4 * rows * width * hidden, 4 * width * hidden),
        name="expert_backward",
    )(sec, received, slope, *w_in, *w_out)


def expert_weight_kernel(add, half_ref, rec_ref, grad_ref, act_ref, res_ref, *rest):
    out_ref = rest[-1]
    half = rec_ref.shape[1]
    upper = mm(rec_ref[...], grad_ref[...], TN)
    lower = mm(act_ref[...], res_ref[...], TN)
    if add:
        upper = upper + rest[0][0, :half].astype(F32)
        lower = lower + rest[0][0, half:].astype(F32)
    out_ref[0, :half] = upper.astype(BF)
    out_ref[0, half:] = lower.astype(BF)


def expert_weights(half, blocks, received, inner_grad, active, result_grad, addend=None):
    rows, width = received.shape
    hidden = inner_grad.shape[1]
    step = hidden // blocks
    cut = width // 2
    more = [] if addend is None else [addend]
    block = pl.BlockSpec((1, width, step), lambda b, half_ref: (b, 0, 0))
    return pl.pallas_call(
        functools.partial(expert_weight_kernel, addend is not None),
        out_shape=jax.ShapeDtypeStruct((blocks, width, step), BF),
        grid_spec=pltpu.PrefetchScalarGridSpec(
            num_scalar_prefetch=1,
            grid=(blocks,),
            in_specs=[
                pl.BlockSpec((rows, cut), lambda b, half_ref: (0, half_ref[0])),
                pl.BlockSpec((rows, step), lambda b, half_ref: (0, b)),
                pl.BlockSpec((rows, step), lambda b, half_ref: (0, b)),
                pl.BlockSpec((rows, cut), lambda b, half_ref: (0, half_ref[0])),
            ]
            + [block] * len(more),
            out_specs=block,
        ),
        compiler_params=params(24),
        cost_estimate=cost(2 * rows * width * hidden, 4 * width * hidden),
        name="expert_weights",
    )(half, received, inner_grad, active, result_grad, *more)


def attend_back_kernel(
    layer,
    capacity,
    sec_ref,
    g_ref,
    mid_ref,
    sent_ref,
    col_ref,
    probs_ref,
    gate_grad_ref,
    gain_ref,
    router_ref,
    qkv_ref,
    kv_ref,
    p_hbm,
    wo_own,
    wo_other,
    mid_grad_ref,
    branch_ref,
    dq_ref,
    own_ref,
    other_ref,
    diag_ref,
    small_ref,
    kv_scr,
    dkv_scr,
    p_scr,
    wo_scr,
    sems,
):
    sec = sec_ref[0]
    rows, width = mid_ref.shape
    total = kv_scr.shape[0]
    pairs = width // PAIR
    lanes = diag_ref.shape[1]
    cuts = [(slice(None), slice(None))]
    fetch(sec, layer, wo_own, wo_other, wo_scr, sems, cuts, pairs)
    for pair in range(pairs):
        pltpu.make_async_copy(
            p_hbm.at[pl.ds(2 * pair, 2)], p_scr.at[pl.ds(2 * pair, 2)], sems.at[pair]
        ).start()
    kv_scr[pl.ds(pl.multiple_of(sec * rows, rows), rows), :] = qkv_ref[:, width:]
    kv_scr[pl.ds(pl.multiple_of((1 - sec) * rows, rows), rows), :] = kv_ref[...]

    middle = mid_ref[...]
    scale = rms(middle)
    unit = middle * scale
    gain = gain_ref[...]
    col = col_ref[...]
    probs = probs_ref[...]
    chosen, gate = gate_of(probs, col)
    logit_grad = probs * (chosen - gate) * gate_grad_ref[...]
    normed_grad = mm(slot_cols(col, sent_ref.shape[0], capacity), sent_ref[...])
    normed_grad = normed_grad + mm(logit_grad, router_ref[...], NT, HIGH)
    experts = probs.shape[1]
    small_ref[0:experts, :] = mm(logit_grad, unit * gain, TN, HIGH)
    small_ref[experts : experts + 1, :] = jnp.sum(normed_grad * unit, axis=0, keepdims=True)
    unit_grad = normed_grad * gain
    middle_grad = g_ref[...].astype(F32) + scale * (
        unit_grad - unit * jnp.mean(unit_grad * unit, axis=-1, keepdims=True)
    )
    mid_grad_ref[...] = middle_grad
    branch = middle_grad.astype(BF)
    branch_ref[...] = branch
    arrive(wo_own, wo_scr, sems, cuts, 0, pairs)
    att_grad = mm(branch, wo_scr[...], NT).astype(BF)

    low = lax.broadcasted_iota(jnp.int32, (rows, PAIR), 1) < HEAD
    low_wide = lax.broadcasted_iota(jnp.int32, (total, PAIR), 1) < HEAD
    zero = jnp.zeros((rows, PAIR), BF)
    pad = jnp.zeros((rows, lanes - total), F32)
    sub = lax.broadcasted_iota(jnp.int32, (8, lanes), 0)
    for pair in range(pairs):
        part = slice(pair * PAIR, (pair + 1) * PAIR)
        later = slice(width + pair * PAIR, width + (pair + 1) * PAIR)
        q = qkv_ref[:, part]
        k = kv_scr[:, part]
        v = kv_scr[:, later]
        da = att_grad[:, part]
        pltpu.make_async_copy(
            p_hbm.at[pl.ds(2 * pair, 2)], p_scr.at[pl.ds(2 * pair, 2)], sems.at[pair]
        ).wait()
        dqs, dks, dvs = [], [], []
        for side in range(2):
            head = 2 * pair + side
            masked = jnp.where(low, da, zero) if side == 0 else jnp.where(low, zero, da)
            share = p_scr[head]
            wide = share.astype(F32)
            dp = mm(masked, v, NT)
            ds = wide * (dp - jnp.sum(wide * dp, axis=-1, keepdims=True))
            dsb = ds.astype(BF)
            dqs.append(mm(dsb, k))
            dks.append(mm(dsb, q, TN))
            dvs.append(mm(share, da, TN))
            padded = jnp.concatenate([ds, pad], axis=1)
            fold = None
            for block in range(rows // 8):
                moved = pltpu.roll(
                    padded[8 * block : 8 * block + 8], (rows - 1 - 8 * block) % lanes, 1
                )
                fold = moved if fold is None else fold + moved
            for bit in (1, 2, 4):
                fold = jnp.where((sub & bit) != 0, pltpu.roll(fold, lanes - bit, 1), fold)
            diag_ref[head : head + 1, :] = jnp.sum(fold, axis=0, keepdims=True)
        dq_ref[:, part] = (jnp.where(low, dqs[0], dqs[1]) * 0.125).astype(BF)
        dkv_scr[:, part] = (jnp.where(low_wide, dks[0], dks[1]) * 0.125).astype(BF)
        dkv_scr[:, later] = jnp.where(low_wide, dvs[0], dvs[1]).astype(BF)
    own_ref[...] = dkv_scr[pl.ds(pl.multiple_of(sec * rows, rows), rows), :]
    other_ref[...] = dkv_scr[pl.ds(pl.multiple_of((1 - sec) * rows, rows), rows), :]


def attend_backward(
    layer, capacity, sec, g, middle, sent, code_col, probs, gate_grad, gain, router, qkv, kv_other, shares, wo
):
    rows, width = middle.shape
    heads = width // HEAD
    experts = router.shape[1]
    return pl.pallas_call(
        functools.partial(attend_back_kernel, layer, capacity),
        out_shape=(
            jax.ShapeDtypeStruct((rows, width), F32),
            jax.ShapeDtypeStruct((rows, width), BF),
            jax.ShapeDtypeStruct((rows, width), BF),
            jax.ShapeDtypeStruct((rows, 2 * width), BF),
            jax.ShapeDtypeStruct((rows, 2 * width), BF),
            jax.ShapeDtypeStruct((heads, SHIFT), F32),
            jax.ShapeDtypeStruct((experts + 1, width), F32),
        ),
        in_specs=[SM] + [VM] * 10 + [ANY] * 3,
        out_specs=(VM,) * 7,
        scratch_shapes=[
            pltpu.VMEM((2 * rows, 2 * width), BF),
            pltpu.VMEM((2 * rows, 2 * width), BF),
            pltpu.VMEM((heads, rows, 2 * rows), BF),
            pltpu.VMEM((width, width), BF),
            pltpu.SemaphoreType.DMA((heads // 2 + 1,)),
        ],
        compiler_params=params(40),
        cost_estimate=cost(8e9, 6e6),
        name="attend_backward",
    )(
        sec, g, middle, sent, code_col, probs, gate_grad, gain, router, qkv, kv_other, shares, *wo
    )


def project_back_kernel(
    layer, last, capacity, sec_ref, dq_ref, own_ref, come_ref, mid_grad_ref, x_ref, gain_ref, *rest
):
    if last:
        w_own, w_other, rows_ref, grad_ref, gain_grad_ref, w_scr, sems = rest
    else:
        comb_ref, probs_ref, row_ref, col_ref, w_own, w_other = rest[:6]
        rows_ref, grad_ref, gain_grad_ref, gate_grad_ref, out_ref, w_scr, sems = rest[6:]
    width = x_ref.shape[1]
    cuts = col_cuts(w_scr.shape[1], width)
    fetch(sec_ref[0], layer, w_own, w_other, w_scr, sems, cuts)
    rows_ref[:, :width] = dq_ref[...]
    rows_ref[:, width:] = (own_ref[...].astype(F32) + come_ref[...].astype(F32)).astype(BF)
    normed_grad = None
    for index in range(3):
        part = slice(index * width, (index + 1) * width)
        arrive(w_own, w_scr, sems, cuts, index)
        fresh = mm(rows_ref[:, part], w_scr[:, part], NT)
        normed_grad = fresh if normed_grad is None else normed_grad + fresh
    x = x_ref[...].astype(F32)
    scale = rms(x)
    unit = x * scale
    gain_grad_ref[...] = jnp.sum(normed_grad * unit, axis=0, keepdims=True)
    unit_grad = normed_grad * gain_ref[...]
    grad = mid_grad_ref[...] + scale * (
        unit_grad - unit * jnp.mean(unit_grad * unit, axis=-1, keepdims=True)
    )
    rounded = grad.astype(BF)
    grad_ref[...] = rounded
    if not last:
        gate_grad_ref[...], out_ref[...] = send_back(
            rounded.astype(F32),
            comb_ref[...].astype(F32),
            probs_ref[...],
            row_ref[...],
            col_ref[...],
            out_ref.shape[0],
            capacity,
        )


def project_backward(layer, capacity, sec, dq, own, come, middle_grad, x, gain, w, before=None):
    rows, width = x.shape
    wide = w[0].shape[1]
    last = before is None
    outs = [
        jax.ShapeDtypeStruct((rows, wide), BF),
        jax.ShapeDtypeStruct((rows, width), BF),
        jax.ShapeDtypeStruct((1, width), F32),
    ]
    more = []
    if not last:
        more = list(before)
        outs += [
            jax.ShapeDtypeStruct((rows, 1), F32),
            jax.ShapeDtypeStruct((before[1].shape[1] * SLOTS, width), BF),
        ]
    return pl.pallas_call(
        functools.partial(project_back_kernel, layer, last, capacity),
        out_shape=tuple(outs),
        in_specs=[SM] + [VM] * (6 + len(more)) + [ANY] * 2,
        out_specs=(VM,) * len(outs),
        scratch_shapes=[pltpu.VMEM((width, wide), BF), pltpu.SemaphoreType.DMA((3,))],
        compiler_params=params(24),
        cost_estimate=cost(2 * rows * width * wide, 2 * width * wide),
        name="project_backward",
    )(sec, dq, own, come, middle_grad, x, gain, *more, *w)


def projection_weight_kernel(add, half_ref, normed_ref, att_ref, rows_ref, branch_ref, *rest):
    out_ref = rest[-1]
    width = normed_ref.shape[1]
    lanes = out_ref.shape[0]
    step = out_ref.shape[1] // 3
    half = half_ref[0]
    first = half == 0
    normed = normed_ref[...]
    mixed = jnp.where(first, normed, att_ref[...])

    def columns(group):
        late = 4 + group
        upper = rows_ref[:, group * step : (group + 1) * step]
        if late < 6:
            lower = rows_ref[:, late * step : (late + 1) * step]
        else:
            lower = branch_ref[:, (late - 6) * step : (late - 5) * step]
        return jnp.where(first, upper, lower)

    feature = lax.broadcasted_iota(jnp.int32, (width, lanes), 0)
    lane = lax.broadcasted_iota(jnp.int32, (width, lanes), 1)
    block, place = lane // 16, lane % 16

    def spread(values, group=None):
        if group is None:
            hit = (place < 12) & (feature == block * 12 + place)
        else:
            hit = (place >= 12) & (feature == block * 12 + 4 * group + place - 12)
        return mm(values, hit.astype(F32).astype(BF)).astype(BF)

    main = spread(normed)
    late_main = spread(mixed)
    tail = columns(3)
    for group in range(3):
        total = mm(main if group < 2 else late_main, columns(group), TN)
        total = total + mm(spread(mixed, group), tail, TN)
        part = slice(group * step, (group + 1) * step)
        if add:
            total = total + rest[0][:, part].astype(F32)
        out_ref[:, part] = total.astype(BF)


def projection_weights(half, shards, normed, attended, rows_grad, branch_grad, addend=None):
    rows, width = normed.shape
    wide = (rows_grad.shape[1] + width) // 2 // 4 * 3
    more = [] if addend is None else [addend]
    return pl.pallas_call(
        functools.partial(projection_weight_kernel, addend is not None),
        out_shape=jax.ShapeDtypeStruct((shards * 16, wide), BF),
        in_specs=[SM] + [VM] * (4 + len(more)),
        out_specs=VM,
        compiler_params=params(40),
        cost_estimate=cost(4e9, 6e6),
        name="projection_weights",
    )(half, normed, attended, rows_grad, branch_grad, *more)


def unpack_rows(shares):
    total = jnp.sum(shares.astype(F32), axis=0)
    width = total.shape[1]
    left = total[12:].reshape(4, 3, width // 3).transpose(1, 0, 2).reshape(12, width // 3)
    return jnp.concatenate([total[:12], left], axis=1)


def body(
    tokens,
    cotangent,
    expert_route,
    capacity_slot,
    buckets,
    qkv_weight,
    attention_out,
    relative_bias,
    attention_gain,
    mixture_gain,
    router,
    expert_in,
    expert_out,
):
    sec = lax.axis_index("section")
    ctx = lax.axis_index("context")
    sec1 = sec.astype(jnp.int32).reshape(1)
    not1 = 1 - sec1
    rows, width = tokens.shape[2:]
    experts = router.shape[2]
    heads = width // HEAD
    bucket_count = relative_bias.shape[1]
    capacity = (5 * rows + 4 * experts - 1) // (4 * experts)
    local = ("context", "dp")
    section = ("context", "expert", "dp")
    blocks = lax.axis_size(local)
    shards = lax.axis_size(section)
    grid = ("section", "context")
    flat_a = [(0, 0), (1, 2), (2, 1), (3, 3)]

    def swap(value):
        return lax.ppermute(value, "section", SWAP)

    def pick(values, at):
        return jnp.where(at == 0, values[0], values[1])

    def exchange(value):
        spread = value.reshape(experts, SLOTS, width)
        return lax.all_to_all(spread, "expert", 0, 0, tiled=True).reshape(value.shape)

    w_qkv = (qkv_weight[0], swap(qkv_weight[0]))
    foreign = pick(tokens[:, 0], 1 - ctx)
    x0 = jnp.where(sec == ctx, pick(tokens[:, 0], ctx), lax.ppermute(foreign, grid, [(0, 1), (3, 2)]))
    foreign = pick(cotangent[:, 0], 1 - ctx)
    cot = jnp.where(
        sec == ctx, pick(cotangent[:, 0], ctx), lax.ppermute(foreign, grid, [(0, 1), (3, 2)])
    )
    w_out = (attention_out[0], swap(attention_out[0]))
    w_up = (expert_in[0, 0], swap(expert_in[0, 0]))
    w_down = (expert_out[0, 0], swap(expert_out[0, 0]))

    def layered(value):
        other = swap(value)
        return (jnp.where(sec == 0, value, other), jnp.where(sec == 0, other, value))

    gain_a = layered(attention_gain)
    gain_m = layered(mixture_gain)
    routers = layered(router[0])
    relative = layered(relative_bias[0])

    code = (expert_route * SLOTS + capacity_slot)[0, :, 0].astype(F32)
    near = lax.ppermute(pick(code, sec), grid, flat_a)
    far = lax.ppermute(pick(code, 1 - sec), grid, [(0, 1), (1, 3), (2, 0), (3, 2)])
    code_rows = [
        jnp.where(ctx == layer, near, far).astype(jnp.int32).reshape(1, rows) for layer in range(2)
    ]
    code_cols = [item.reshape(rows, 1) for item in code_rows]

    padded = jnp.concatenate([buckets, jnp.full((SHIFT,), -1, jnp.int32)])
    span = lax.dynamic_slice(padded, (rows * (1 - sec),), (SHIFT,))
    span = jnp.where(jnp.arange(SHIFT) < 3 * rows - 1, span, -1)
    onehot = (jnp.arange(bucket_count, dtype=jnp.int32)[:, None] == span[None]).astype(F32)
    vectors = jnp.stack(
        [jnp.einsum("bh,bx->hx", table, onehot, precision=HIGH) for table in relative]
    )
    bias = bias_table(vectors, rows, 384)

    normed0, qkv0 = first_projection(0, sec1, x0, gain_a[0], w_qkv)
    x, normed, qkv = [x0, None], [normed0, None], [qkv0, None]
    kv, middle, probs, attended, shares = ([None, None] for _ in range(5))
    received, active, slope = ([None, None] for _ in range(3))
    hidden = [None, None]
    for layer in range(2):
        kv[layer] = swap(qkv[layer][:, width:])
        middle[layer], probs[layer], attended[layer], shares[layer], outgoing = attend(
            layer,
            capacity,
            sec1,
            x[layer],
            qkv[layer],
            kv[layer],
            gain_m[layer],
            routers[layer],
            code_rows[layer],
            code_cols[layer],
            bias,
            w_out,
        )
        received[layer] = exchange(outgoing)
        result, active[layer], slope[layer] = expert_forward(
            layer, sec1, received[layer], w_up, w_down
        )
        returned = exchange(result)
        if layer == 0:
            combined, hidden[0], normed[1], qkv[1] = join(
                1, capacity, sec1, middle[0], returned, probs[0], code_cols[0], gain_a[1], w_qkv
            )
            x[1] = hidden[0]
        else:
            hidden[1], gate_grad, outgoing = turn(
                capacity, middle[1], returned, probs[1], code_rows[1], code_cols[1], cot
            )

    def spread_out(values):
        one = lax.ppermute(pick(values, ctx), grid, flat_a)
        two = lax.ppermute(pick(values, 1 - ctx), grid, [(0, 2), (1, 0), (2, 3), (3, 1)])
        return jnp.stack([jnp.where(sec == 0, one, two), jnp.where(sec == 0, two, one)])

    hidden_states = spread_out(hidden)

    g = cot
    grads, projections, expert_sums, small = ([None, None] for _ in range(4))
    for layer in (1, 0):
        result_grad = exchange(outgoing)
        sent, inner_grad = expert_backward(
            layer, sec1, result_grad, slope[layer], w_up, w_down
        )
        sent = exchange(sent)
        operands = (received[layer], inner_grad, active[layer], result_grad)
        come = swap(expert_weights(not1, blocks, *operands))
        half = expert_weights(sec1, blocks, *operands, come)
        half = half.reshape(blocks * width, half.shape[2])
        expert_sums[layer] = lax.psum_scatter(half, local, scatter_dimension=0, tiled=True)
        middle_grad, branch, dq, own, other, diag, small_m = attend_backward(
            layer,
            capacity,
            sec1,
            g,
            middle[layer],
            sent,
            code_cols[layer],
            probs[layer],
            gate_grad,
            gain_m[layer],
            routers[layer],
            qkv[layer],
            kv[layer],
            shares[layer],
            w_out,
        )
        before = (combined, probs[0], code_rows[0], code_cols[0]) if layer == 1 else None
        back = project_backward(
            layer,
            capacity,
            sec1,
            dq,
            own,
            swap(other),
            middle_grad,
            x[layer],
            gain_a[layer],
            w_qkv,
            before,
        )
        rows_grad, grads[layer], gain_grad = back[:3]
        if layer == 1:
            g, gate_grad, outgoing = grads[1], back[3], back[4]
        operands = (normed[layer], attended[layer], rows_grad, branch)
        come = swap(projection_weights(not1, shards, *operands))
        projections[layer] = projection_weights(sec1, shards, *operands, come)
        table = jnp.einsum("bx,hx->bh", onehot, diag, precision=HIGH)
        flat = jnp.concatenate(
            [small_m.reshape(-1), gain_grad.reshape(-1), table.reshape(-1)]
        )
        size = -(-flat.shape[0] // (shards * 128)) * shards * 128
        small[layer] = jnp.pad(flat, (0, size - flat.shape[0])).reshape(shards, -1, 128)

    def shared(value):
        return lax.all_to_all(value, section, 0, 0, tiled=True)

    mine = pick(small, sec) + swap(pick(small, 1 - sec))
    mine = jnp.sum(shared(mine), axis=0, keepdims=True)
    mine = shared(jnp.broadcast_to(mine, small[0].shape)).reshape(-1)
    at = 0
    parts = []
    for shape in ((experts, width), (1, width), (1, width), (bucket_count, heads)):
        count = shape[0] * shape[1]
        parts.append(mine[at : at + count].reshape(shape))
        at += count

    halves = [
        unpack_rows(shared(item.reshape(shards, 16, item.shape[1]))) for item in projections
    ]
    whole = (pick(halves, sec), swap(pick(halves, 1 - sec)))
    whole = jnp.concatenate([pick(whole, sec), pick(whole, 1 - sec)], axis=1)
    wide = qkv_weight.shape[2]

    whole_e = (pick(expert_sums, sec), swap(pick(expert_sums, 1 - sec)))
    first, second = pick(whole_e, sec), pick(whole_e, 1 - sec)
    cut = width // 2
    in_grad = jnp.concatenate([first[:cut], second[:cut]], axis=0).astype(F32)
    out_grad = jnp.concatenate([first[cut:], second[cut:]], axis=1).astype(F32)

    input_grads = spread_out(grads).astype(F32)
    return (
        hidden_states[None, :, None],
        input_grads[None, :, None],
        whole[None, :, :wide],
        whole[None, :, wide:],
        parts[3][None],
        parts[2],
        parts[1],
        parts[0].T[None],
        in_grad[None, None],
        out_grad[None, None],
    )


def solution(mesh):
    return jax.shard_map(
        body,
        mesh=mesh,
        in_specs=(
            P(None, ("expert", "dp"), "context", None),
            P(None, ("expert", "dp"), "context", None),
            P("section", None, ("expert", "dp"), "context"),
            P("section", None, ("expert", "dp"), "context"),
            P(),
            P("section", None, None),
            P("section", None, None),
            P("section", None, None),
            P("section", None),
            P("section", None),
            P("section", None, None),
            P("section", "expert", None, None),
            P("section", "expert", None, None),
        ),
        out_specs=(
            P("section", None, ("expert", "dp"), "context", None),
            P("section", None, ("expert", "dp"), "context", None),
            P("section", ("context", "expert", "dp"), None),
            P("section", ("context", "expert", "dp"), None),
            P("section", None, None),
            P("section", None),
            P("section", None),
            P("section", None, None),
            P("section", "expert", None, ("context", "dp")),
            P("section", "expert", ("context", "dp"), None),
        ),
        check_vma=False,
    )
```

```python
import functools

import jax
import jax.numpy as jnp
from jax import lax
from jax.experimental import pallas as pl
from jax.experimental.pallas import tpu as pltpu
from jax.sharding import PartitionSpec as P

BF = jnp.bfloat16
F32 = jnp.float32
HIGH = lax.Precision.HIGHEST
EPS = 1e-06
HEAD = 64
PAIR = 2 * HEAD
SLOTS = 32
SHIFT = 512
SWAP = [(0, 1), (1, 0)]
NN = (((1,), (0,)), ((), ()))
NT = (((1,), (1,)), ((), ()))
TN = (((0,), (0,)), ((), ()))


def mm(a, b, dims=NN, precision=None):
    return lax.dot_general(a, b, dims, precision=precision, preferred_element_type=F32)


SM = pl.BlockSpec(memory_space=pltpu.SMEM)
ANY = pl.BlockSpec(memory_space=pl.ANY)


def call(kernel, name, estimate, operands, outs, scratch=(), deps=(), aliases={}):
    def whole(item):
        if isinstance(item, tuple):
            return item
        rank = len(item.shape)
        return item, pl.BlockSpec(item.shape, lambda step: (0,) * rank)

    operands = [whole(item) for item in operands]
    outs = [whole(item) for item in outs]
    count = len(operands)
    operands += [(item, ANY) for item in deps]

    def inner(*refs):
        kernel(*refs[:count], *refs[count + len(deps) :])

    return pl.pallas_call(
        inner,
        out_shape=tuple(item for item, _ in outs),
        grid=(1,),
        in_specs=[spec for _, spec in operands],
        out_specs=tuple(spec for _, spec in outs),
        scratch_shapes=list(scratch),
        compiler_params=params(),
        cost_estimate=estimate,
        input_output_aliases=aliases,
        name=name,
    )(*[item for item, _ in operands])


def gate(value, *others):
    def kernel(*refs):
        pass

    return pl.pallas_call(
        kernel,
        out_shape=sds(value.shape, value.dtype),
        in_specs=[ANY] * (1 + len(others)),
        out_specs=ANY,
        input_output_aliases={0: 0},
        compiler_params=params(),
        cost_estimate=cost(0, 0),
        name="gate",
    )(value, *others)


def sds(shape, dtype):
    return jax.ShapeDtypeStruct(shape, dtype)


def far(items):
    return [(item, ANY) for item in items]


def params():
    return pltpu.CompilerParams(vmem_limit_bytes=64 * 1024 * 1024)


def cost(flops, size):
    return pl.CostEstimate(flops=int(flops), bytes_accessed=int(size), transcendentals=0)


def col_cuts(width, step):
    return [(slice(None), pl.ds(at, step)) for at in range(0, width, step)]


def row_cuts(height, step):
    return [(pl.ds(at, step), slice(None)) for at in range(0, height, step)]


def fetch(sec, layer, own, other, dst, sems, cuts, base=0):
    def go(src):
        for index, cut in enumerate(cuts):
            pltpu.make_async_copy(src.at[cut], dst.at[cut], sems.at[base + index]).start()

    pl.when(sec == layer)(lambda: go(own))
    pl.when(sec != layer)(lambda: go(other))


def arrive(own, dst, sems, cuts, index, base=0):
    cut = cuts[index]
    pltpu.make_async_copy(own.at[cut], dst.at[cut], sems.at[base + index]).wait()


def depart(src, dst, sems, cuts, index, base=0):
    cut = cuts[index]
    pltpu.make_async_copy(src.at[cut], dst.at[cut], sems.at[base + index]).start()


def rms(values):
    return lax.rsqrt(jnp.mean(values * values, axis=-1, keepdims=True) + EPS)


def slot_rows(code_row, rows, capacity):
    target = jnp.where((code_row & (SLOTS - 1)) < capacity, code_row, -1)
    return (
        lax.broadcasted_iota(jnp.int32, (rows, code_row.shape[1]), 0) == target
    ).astype(F32).astype(BF)


def slot_cols(code_col, rows, capacity):
    target = jnp.where((code_col & (SLOTS - 1)) < capacity, code_col, -1)
    return (
        lax.broadcasted_iota(jnp.int32, (code_col.shape[0], rows), 1) == target
    ).astype(F32).astype(BF)


def project(normed, w_own, w_scr, sems, cuts, q_ref, kv_ref):
    step = q_ref.shape[1]
    for index in range(3):
        arrive(w_own, w_scr, sems, cuts, index)
        part = mm(normed, w_scr[:, index * step : (index + 1) * step]).astype(BF)
        if index == 0:
            q_ref[...] = part
        else:
            kv_ref[:, (index - 1) * step : index * step] = part


def fill_bias(vectors, out_ref, done=None):
    heads, rows, width = out_ref.shape
    lanes = vectors.shape[1]
    sub = lax.broadcasted_iota(jnp.int32, (8, lanes), 0)
    for head in range(heads):
        base = jnp.broadcast_to(vectors[head : head + 1, :], (8, lanes))
        for bit in (1, 2, 4):
            base = jnp.where((sub & bit) != 0, pltpu.roll(base, bit, 1), base)
        for block in range(rows // 8):
            moved = pltpu.roll(base, (8 * block - (rows - 1)) % lanes, 1)
            out_ref[head, 8 * block : 8 * block + 8, :] = moved[:, :width]
        if done is not None:
            done(head)


GAIN_M, ROUTER = 1, 2


def pack_kernel(
    place_ref,
    gain_a,
    gain_m,
    router,
    route,
    slot,
    table,
    tokens,
    cotangent,
    out_ref,
    code_ref,
    tok_ref,
    cot_ref,
):
    ctx = place_ref[1]
    experts = router.shape[0]
    rows = route.shape[2]
    out_ref[...] = jnp.zeros(out_ref.shape, F32)
    out_ref[0:1, :] = gain_a[...]
    out_ref[GAIN_M : GAIN_M + 1, :] = gain_m[...]
    out_ref[ROUTER : ROUTER + experts, :] = router[...]
    at = ROUTER + experts
    code = [(route[micro] * SLOTS + slot[micro]).astype(F32) for micro in range(2)]
    out_ref[at : at + 1, :rows] = code[0]
    out_ref[at + 1 : at + 2, :rows] = code[1]
    at += 2
    out_ref[at : at + table.shape[0], : table.shape[1]] = table[...]
    tok_ref[...] = jnp.where(ctx == 0, tokens[1], tokens[0])
    code_ref[...] = jnp.zeros(code_ref.shape, F32)
    code_ref[0:1, :rows] = jnp.where(ctx == 0, code[1], code[0])
    cot_ref[...] = jnp.where(ctx == 0, cotangent[1], cotangent[0])


def pack(place, gain_a, gain_m, router, route, slot, table, tokens, cotangent):
    rows, width = tokens.shape[1:]
    height = ROUTER + router.shape[0] + route.shape[0] + table.shape[0]
    return call(
        pack_kernel,
        "pack",
        cost(1e6, 2e6),
        [(place, SM), gain_a, gain_m, router, route, slot, table, tokens, cotangent],
        [sds((height, width), F32), sds((8, 256), F32)] + [sds((rows, width), BF)] * 2,
    )


def prepare_kernel(
    place_ref, buckets_ref, packs_ref, come_ref, up_hbm, down_hbm, onehot_ref, bias_hbm, vec_ref, *rest
):
    *outs, up_copy, down_copy, bias_ref, bucket_scr, up_scr, down_scr, leave, enter, moving = rest
    sides = ((up_hbm, up_scr, up_copy), (down_hbm, down_scr, down_copy))

    def pieces():
        for side, item in enumerate(sides):
            step = item[0].shape[0] // 4
            for index in range(4):
                yield side, 4 * side + index, pl.ds(index * step, step)

    for side, index, cut in pieces():
        src, held, _ = sides[side]
        pltpu.make_async_copy(src.at[cut], held.at[cut], enter.at[index]).start()
    sec, ctx = place_ref[0], place_ref[1]
    first = sec == 0
    experts = outs[2].shape[0]
    rows = outs[3].shape[1]
    heads = bias_ref.shape[0]
    bucket_count = onehot_ref.shape[0]
    bucket_scr[...] = jnp.full(bucket_scr.shape, -1, jnp.int32)
    bucket_scr[:, : buckets_ref.shape[1]] = buckets_ref[...]
    wide = bucket_scr[...]
    span = jnp.where(first, pltpu.roll(wide, wide.shape[1] - rows, 1), wide)[:, :SHIFT]
    lane = lax.broadcasted_iota(jnp.int32, span.shape, 1)
    span = jnp.where(lane < 3 * rows - 1, span, -1)
    onehot = lax.broadcasted_iota(jnp.int32, onehot_ref.shape, 0) == span
    onehot = jnp.where(onehot, 1.0, 0.0)
    onehot_ref[...] = onehot
    height = packs_ref.shape[0] // 2
    packs = packs_ref[:height], packs_ref[height:]
    at = ROUTER + experts + 2
    tables = [item[at : at + heads, :bucket_count] for item in packs]

    def copy(head):
        return pltpu.make_async_copy(bias_ref.at[head], bias_hbm.at[head], leave.at[head])

    moves = list(pieces())

    def done(head):
        copy(head).start()
        if head >= heads - len(moves):
            side, index, cut = moves[head - (heads - len(moves))]
            src, held, dst = sides[side]
            pltpu.make_async_copy(src.at[cut], held.at[cut], enter.at[index]).wait()
            pltpu.make_async_copy(held.at[cut], dst.at[cut], moving.at[index]).start()

    fill_bias(mm(tables[0], onehot, NN, HIGH), bias_ref, done)
    vec_ref[...] = mm(tables[1], onehot, NN, HIGH)
    at = ROUTER + experts
    home = sec == ctx
    eye = lax.broadcasted_iota(jnp.int32, (rows, rows), 0) == lax.broadcasted_iota(
        jnp.int32, (rows, rows), 1
    )
    for layer in range(2):
        pair = packs[layer][at : at + 2, :rows]
        row = jnp.where(ctx == 0, pair[0:1], pair[1:2])
        row = jnp.where(home, row, come_ref[8 * layer : 8 * layer + 1, :rows])
        col = jnp.sum(jnp.where(eye, row, 0.0), axis=1, keepdims=True)
        for index, item in enumerate(
            (
                packs[layer][0:1],
                packs[layer][GAIN_M : GAIN_M + 1],
                packs[layer][ROUTER : ROUTER + experts],
                row.astype(jnp.int32),
                col.astype(jnp.int32),
            )
        ):
            outs[5 * layer + index][...] = item
    for head in range(heads):
        copy(head).wait()
    for side, index, cut in pieces():
        _, held, dst = sides[side]
        pltpu.make_async_copy(held.at[cut], dst.at[cut], moving.at[index]).wait()


def prepare(place, buckets, packs, come, up, down, sizes, rows, lanes, deps):
    experts, heads, bucket_count = sizes
    width = packs.shape[1]
    each = [
        sds((1, width), F32),
        sds((1, width), F32),
        sds((experts, width), F32),
        sds((1, rows), jnp.int32),
        sds((rows, 1), jnp.int32),
    ]
    return call(
        prepare_kernel,
        "prepare",
        cost(1e7, 4e6),
        [(place, SM), buckets, packs, come, (up, ANY), (down, ANY)],
        [
            sds((bucket_count, SHIFT), F32),
            (sds((heads, rows, lanes), F32), ANY),
            sds((heads, SHIFT), F32),
            *each,
            *each,
            (sds(up.shape, BF), ANY),
            (sds(down.shape, BF), ANY),
        ],
        [
            pltpu.VMEM((heads, rows, lanes), F32),
            pltpu.VMEM((1, 2 * SHIFT), jnp.int32),
            pltpu.VMEM(up.shape, BF),
            pltpu.VMEM(down.shape, BF),
            pltpu.SemaphoreType.DMA((heads,)),
            pltpu.SemaphoreType.DMA((8,)),
            pltpu.SemaphoreType.DMA((8,)),
        ],
        deps,
    )


def bias_kernel(vec_ref, out_ref):
    fill_bias(vec_ref[...], out_ref)


def bias_table(vectors, rows, width, deps):
    return call(
        bias_kernel,
        "bias_table",
        cost(1e7, 4e6),
        [vectors],
        [sds((vectors.shape[0], rows, width), F32)],
        deps=deps,
    )[0]


def chosen_block(place_ref, both_ref, come_ref):
    sec, ctx = place_ref[0], place_ref[1]
    mine = jnp.where(ctx == 0, both_ref[0], both_ref[1])
    return jnp.where(sec == ctx, mine, come_ref[...])


def first_kernel(
    layer,
    place_ref,
    both_ref,
    come_ref,
    packs_ref,
    w_own,
    w_other,
    x_ref,
    normed_ref,
    q_ref,
    kv_ref,
    w_scr,
    sems,
):
    cuts = col_cuts(w_scr.shape[1], w_scr.shape[1] // 3)
    fetch(place_ref[0], layer, w_own, w_other, w_scr, sems, cuts)
    rounded = chosen_block(place_ref, both_ref, come_ref)
    x_ref[...] = rounded
    x = rounded.astype(F32)
    at = layer * (packs_ref.shape[0] // 2)
    normed = (x * rms(x) * packs_ref[at : at + 1]).astype(BF)
    normed_ref[...] = normed
    project(normed, w_own, w_scr, sems, cuts, q_ref, kv_ref)


def first_projection(layer, place, both, come, packs, w):
    rows, width = both.shape[1:]
    wide = w[0].shape[1]
    return call(
        functools.partial(first_kernel, layer),
        "first_projection",
        cost(2 * rows * width * wide, 2 * width * wide),
        [(place, SM), both, come, packs, *far(w)],
        [sds((rows, width), BF)] * 3 + [sds((rows, 2 * width), BF)],
        [pltpu.VMEM((width, wide), BF), pltpu.SemaphoreType.DMA((3,))],
    )


def attend_kernel(
    layer,
    capacity,
    sec_ref,
    x_ref,
    q_ref,
    kv_ref,
    gain_ref,
    router_ref,
    row_ref,
    bias_hbm,
    wo_own,
    wo_other,
    mid_ref,
    probs_ref,
    att_ref,
    p_ref,
    out_ref,
    bias_scr,
    wo_scr,
    p_scr,
    sems,
    leave,
):
    sec = sec_ref[0]
    rows, width = x_ref.shape
    total = kv_ref.shape[0]
    pairs = width // PAIR
    for pair in range(pairs):
        pltpu.make_async_copy(
            bias_hbm.at[pl.ds(2 * pair, 2)], bias_scr.at[pl.ds(2 * pair, 2)], sems.at[pair]
        ).start()
    cuts = [(slice(None), slice(None))]
    fetch(sec, layer, wo_own, wo_other, wo_scr, sems, cuts, pairs)
    low = lax.broadcasted_iota(jnp.int32, (rows, PAIR), 1) < HEAD
    zero = jnp.zeros((rows, PAIR), BF)
    for pair in range(pairs):
        part = slice(pair * PAIR, (pair + 1) * PAIR)
        q = q_ref[:, part]
        k = kv_ref[:, part]
        v = kv_ref[:, width + pair * PAIR : width + (pair + 1) * PAIR]
        pltpu.make_async_copy(
            bias_hbm.at[pl.ds(2 * pair, 2)], bias_scr.at[pl.ds(2 * pair, 2)], sems.at[pair]
        ).wait()
        both = []
        for side in range(2):
            head = 2 * pair + side
            masked = jnp.where(low, q, zero) if side == 0 else jnp.where(low, zero, q)
            scores = mm(masked, k, NT) * 0.125 + bias_scr[head, :, :total]
            top = jnp.max(scores, axis=-1, keepdims=True)
            raised = jnp.exp(scores - top)
            share = (raised * (1.0 / jnp.sum(raised, axis=-1, keepdims=True))).astype(BF)
            p_scr[head] = share
            both.append(mm(share, v))
        pltpu.make_async_copy(
            p_scr.at[pl.ds(2 * pair, 2)], p_ref.at[pl.ds(2 * pair, 2)], leave.at[pair]
        ).start()
        att_ref[:, part] = jnp.where(low, both[0], both[1]).astype(BF)
    arrive(wo_own, wo_scr, sems, cuts, 0, pairs)
    middle = x_ref[...].astype(F32) + mm(att_ref[...], wo_scr[...])
    mid_ref[...] = middle
    normed = middle * rms(middle) * gain_ref[...]
    logits = mm(normed, router_ref[...], NT, HIGH)
    raised = jnp.exp(logits - jnp.max(logits, axis=-1, keepdims=True))
    probs_ref[...] = raised / jnp.sum(raised, axis=-1, keepdims=True)
    slots = slot_rows(row_ref[...], out_ref.shape[0], capacity)
    out_ref[...] = mm(slots, normed.astype(BF)).astype(BF)
    for pair in range(pairs):
        pltpu.make_async_copy(
            p_scr.at[pl.ds(2 * pair, 2)], p_ref.at[pl.ds(2 * pair, 2)], leave.at[pair]
        ).wait()


def attend(layer, capacity, sec, x, q, kv, gain, router, code_row, bias, wo):
    rows, width = x.shape
    experts = router.shape[0]
    heads = width // HEAD
    wide = bias.shape[2]
    return call(
        functools.partial(attend_kernel, layer, capacity),
        "attend",
        cost(4e9, 6e6),
        [(sec, SM), x, q, kv, gain, router, code_row, (bias, ANY), *far(wo)],
        [
            sds((rows, width), F32),
            sds((rows, experts), F32),
            sds((rows, width), BF),
            (sds((heads, rows, 2 * rows), BF), ANY),
            sds((experts * SLOTS, width), BF),
        ],
        [
            pltpu.VMEM((heads, rows, wide), F32),
            pltpu.VMEM((width, width), BF),
            pltpu.VMEM((heads, rows, 2 * rows), BF),
            pltpu.SemaphoreType.DMA((heads // 2 + 1,)),
            pltpu.SemaphoreType.DMA((heads // 2,)),
        ],
    )


def expert_kernel(
    layer,
    sec_ref,
    rec_ref,
    in_own,
    in_other,
    out_own,
    out_other,
    res_ref,
    act_hbm,
    slope_hbm,
    win,
    wout,
    act_ref,
    slope_ref,
    sems,
    leave,
):
    sec = sec_ref[0]
    hidden = win.shape[1]
    step = 512
    count = hidden // step
    in_cuts = col_cuts(hidden, step)
    out_cuts = row_cuts(hidden, step)
    fetch(sec, layer, in_own, in_other, win, sems, in_cuts)
    fetch(sec, layer, out_own, out_other, wout, sems, out_cuts, count)
    rec = rec_ref[...]
    total = None
    for index in range(count):
        part = slice(index * step, (index + 1) * step)
        arrive(in_own, win, sems, in_cuts, index)
        v = mm(rec, win[:, part])
        square = v * v
        t = jnp.tanh(v * (0.7978845608028654 + 0.035677408136300125 * square))
        half = 0.5 * (1.0 + t)
        active = (v * half).astype(BF)
        act_ref[:, part] = active
        slope = half + 0.5 * v * (1.0 - t * t) * (0.7978845608028654 + 0.10703222440890037 * square)
        slope_ref[:, part] = slope.astype(BF)
        depart(act_ref, act_hbm, leave, in_cuts, index)
        depart(slope_ref, slope_hbm, leave, in_cuts, index, count)
        arrive(out_own, wout, sems, out_cuts, index, count)
        fresh = mm(active, wout[part, :])
        total = fresh if total is None else total + fresh
    res_ref[...] = total.astype(BF)
    for index in range(count):
        arrive(act_ref, act_hbm, leave, in_cuts, index)
        arrive(slope_ref, slope_hbm, leave, in_cuts, index, count)


def expert_forward(layer, sec, received, w_in, w_out, deps=()):
    rows, width = received.shape
    hidden = w_in[0].shape[1]
    count = hidden // 512
    return call(
        functools.partial(expert_kernel, layer),
        "expert_forward",
        cost(4 * rows * width * hidden, 4 * width * hidden),
        [(sec, SM), received, *far(w_in), *far(w_out)],
        [sds((rows, width), BF)] + [(sds((rows, hidden), BF), ANY)] * 2,
        [
            pltpu.VMEM((width, hidden), BF),
            pltpu.VMEM((hidden, width), BF),
            pltpu.VMEM((rows, hidden), BF),
            pltpu.VMEM((rows, hidden), BF),
            pltpu.SemaphoreType.DMA((2 * count,)),
            pltpu.SemaphoreType.DMA((2 * count,)),
        ],
        deps,
    )


def gate_of(probs, code_col):
    lane = lax.broadcasted_iota(jnp.int32, probs.shape, 1)
    chosen = (lane == code_col // SLOTS).astype(F32)
    return chosen, jnp.sum(probs * chosen, axis=-1, keepdims=True)


def join_kernel(
    layer,
    capacity,
    sec_ref,
    mid_ref,
    ret_ref,
    probs_ref,
    col_ref,
    gain_ref,
    w_own,
    w_other,
    comb_ref,
    hid_ref,
    normed_ref,
    q_ref,
    kv_ref,
    w_scr,
    sems,
):
    cuts = col_cuts(w_scr.shape[1], w_scr.shape[1] // 3)
    fetch(sec_ref[0], layer, w_own, w_other, w_scr, sems, cuts)
    col = col_ref[...]
    combined = mm(slot_cols(col, ret_ref.shape[0], capacity), ret_ref[...])
    comb_ref[...] = combined.astype(BF)
    _, gate = gate_of(probs_ref[...], col)
    hidden = (mid_ref[...] + gate * combined).astype(BF)
    hid_ref[...] = hidden
    x = hidden.astype(F32)
    normed = (x * rms(x) * gain_ref[...]).astype(BF)
    normed_ref[...] = normed
    project(normed, w_own, w_scr, sems, cuts, q_ref, kv_ref)


def join(layer, capacity, sec, middle, returned, probs, code_col, gain, w):
    rows, width = middle.shape
    wide = w[0].shape[1]
    return call(
        functools.partial(join_kernel, layer, capacity),
        "join",
        cost(2 * rows * width * wide, 2 * width * wide),
        [(sec, SM), middle, returned, probs, code_col, gain, *far(w)],
        [sds((rows, width), BF)] * 4 + [sds((rows, 2 * width), BF)],
        [pltpu.VMEM((width, wide), BF), pltpu.SemaphoreType.DMA((3,))],
    )


def pack_rows(ref, base, values):
    height, width = values.shape
    for row in range(height):
        for at in range(width // 128):
            place = base + row * (width // 128) + at
            ref[place : place + 1, :] = values[row : row + 1, at * 128 : (at + 1) * 128]


def send_back(g, combined, probs, row, col, rows, capacity):
    _, gate = gate_of(probs, col)
    gate_grad = jnp.sum(g * combined, axis=-1, keepdims=True)
    placed = mm(slot_rows(row, rows, capacity), (gate * g).astype(BF))
    return gate_grad, placed.astype(BF)


def turn_kernel(
    capacity,
    place_ref,
    mid_ref,
    ret_ref,
    probs_ref,
    row_ref,
    col_ref,
    both_ref,
    come_ref,
    hid_ref,
    g_ref,
    gate_grad_ref,
    out_ref,
):
    g = chosen_block(place_ref, both_ref, come_ref)
    g_ref[...] = g
    col = col_ref[...]
    probs = probs_ref[...]
    combined = mm(slot_cols(col, ret_ref.shape[0], capacity), ret_ref[...])
    _, gate = gate_of(probs, col)
    hid_ref[...] = (mid_ref[...] + gate * combined).astype(BF)
    gate_grad_ref[...], out_ref[...] = send_back(
        g.astype(F32), combined, probs, row_ref[...], col, out_ref.shape[0], capacity
    )


def turn(capacity, place, middle, returned, probs, code_row, code_col, both, come):
    rows, width = middle.shape
    return call(
        functools.partial(turn_kernel, capacity),
        "turn",
        cost(4 * rows * width * returned.shape[0], 3e6),
        [(place, SM), middle, returned, probs, code_row, code_col, both, come],
        [
            sds((rows, width), BF),
            sds((rows, width), BF),
            sds((rows, 1), F32),
            sds(returned.shape, BF),
        ],
    )


def expert_back_kernel(
    layer,
    sec_ref,
    rec_ref,
    slope_hbm,
    in_own,
    in_other,
    out_own,
    out_other,
    sent_ref,
    grad_hbm,
    win,
    wout,
    slope_ref,
    grad_ref,
    sems,
    leave,
):
    sec = sec_ref[0]
    hidden = win.shape[1]
    step = 512
    count = hidden // step
    in_cuts = col_cuts(hidden, step)
    out_cuts = row_cuts(hidden, step)
    fetch(sec, layer, out_own, out_other, wout, sems, out_cuts, count)
    for index in range(count):
        depart(slope_hbm, slope_ref, sems, in_cuts, index, 2 * count)
    fetch(sec, layer, in_own, in_other, win, sems, in_cuts)
    rec = rec_ref[...]
    total = None
    for index in range(count):
        part = slice(index * step, (index + 1) * step)
        arrive(out_own, wout, sems, out_cuts, index, count)
        arrive(slope_hbm, slope_ref, sems, in_cuts, index, 2 * count)
        inner = (mm(rec, wout[part, :], NT) * slope_ref[:, part].astype(F32)).astype(BF)
        grad_ref[:, part] = inner
        depart(grad_ref, grad_hbm, leave, in_cuts, index)
        arrive(in_own, win, sems, in_cuts, index)
        fresh = mm(inner, win[:, part], NT)
        total = fresh if total is None else total + fresh
    sent_ref[...] = total.astype(BF)
    for index in range(count):
        arrive(grad_ref, grad_hbm, leave, in_cuts, index)


def expert_backward(layer, sec, received, slope, w_in, w_out, deps=()):
    rows, width = received.shape
    hidden = w_in[0].shape[1]
    count = hidden // 512
    return call(
        functools.partial(expert_back_kernel, layer),
        "expert_backward",
        cost(4 * rows * width * hidden, 4 * width * hidden),
        [(sec, SM), received, (slope, ANY), *far(w_in), *far(w_out)],
        [sds((rows, width), BF), (sds((rows, hidden), BF), ANY)],
        [
            pltpu.VMEM((width, hidden), BF),
            pltpu.VMEM((hidden, width), BF),
            pltpu.VMEM((rows, hidden), BF),
            pltpu.VMEM((rows, hidden), BF),
            pltpu.SemaphoreType.DMA((3 * count,)),
            pltpu.SemaphoreType.DMA((count,)),
        ],
        deps,
    )


def expert_weight_kernel(half_ref, *refs):
    rec, grad, act, res, rec_b, grad_b, act_b, res_b, out_ref = refs
    half = rec.shape[1]
    upper = mm(rec[...], grad[...], TN) + mm(rec_b[...], grad_b[...], TN)
    out_ref[0, :half] = upper.astype(BF)
    lower = mm(act[...], res[...], TN) + mm(act_b[...], res_b[...], TN)
    out_ref[0, half : 2 * half] = lower.astype(BF)


def expert_weights(half, blocks, own, other):
    rows, width = own[0].shape
    hidden = own[1].shape[1]
    step = hidden // blocks
    cut = width // 2
    narrow = pl.BlockSpec((rows, cut), lambda b, half_ref: (0, half_ref[0]))
    moving = pl.BlockSpec((rows, step), lambda b, half_ref: (0, b))
    return pl.pallas_call(
        expert_weight_kernel,
        out_shape=sds((blocks, width, step), BF),
        grid_spec=pltpu.PrefetchScalarGridSpec(
            num_scalar_prefetch=1,
            grid=(blocks,),
            in_specs=[narrow, moving, moving, narrow] * 2,
            out_specs=pl.BlockSpec((1, width, step), lambda b, half_ref: (b, 0, 0)),
        ),
        compiler_params=params(),
        cost_estimate=cost(4 * rows * width * hidden, 4 * width * hidden),
        name="expert_weights",
    )(half, *own, *other)


def attend_back_kernel(
    layer,
    capacity,
    sec_ref,
    g_ref,
    mid_ref,
    sent_ref,
    col_ref,
    probs_ref,
    gate_grad_ref,
    gain_ref,
    router_ref,
    q_ref,
    kv_ref,
    onehot_ref,
    p_hbm,
    wo_own,
    wo_other,
    mid_grad_ref,
    branch_ref,
    dq_ref,
    own_ref,
    other_ref,
    small_ref,
    dkv_scr,
    diag_scr,
    p_scr,
    wo_scr,
    sems,
):
    sec = sec_ref[0]
    rows, width = mid_ref.shape
    total = kv_ref.shape[0]
    pairs = width // PAIR
    lanes = diag_scr.shape[1]
    cuts = [(slice(None), slice(None))]
    fetch(sec, layer, wo_own, wo_other, wo_scr, sems, cuts, pairs)
    for pair in range(pairs):
        pltpu.make_async_copy(
            p_hbm.at[pl.ds(2 * pair, 2)], p_scr.at[pl.ds(2 * pair, 2)], sems.at[pair]
        ).start()

    middle = mid_ref[...]
    scale = rms(middle)
    unit = middle * scale
    gain = gain_ref[...]
    col = col_ref[...]
    probs = probs_ref[...]
    chosen, gate = gate_of(probs, col)
    logit_grad = probs * (chosen - gate) * gate_grad_ref[...]
    normed_grad = mm(slot_cols(col, sent_ref.shape[0], capacity), sent_ref[...])
    normed_grad = normed_grad + mm(logit_grad, router_ref[...], NN, HIGH)
    experts = probs.shape[1]
    router_grad = mm(logit_grad, unit * gain, TN, HIGH)
    gain_grad = jnp.sum(normed_grad * unit, axis=0, keepdims=True)
    pack_rows(small_ref, 0, router_grad)
    pack_rows(small_ref, experts * (width // 128), gain_grad)
    unit_grad = normed_grad * gain
    middle_grad = g_ref[...].astype(F32) + scale * (
        unit_grad - unit * jnp.mean(unit_grad * unit, axis=-1, keepdims=True)
    )
    mid_grad_ref[...] = middle_grad
    branch = middle_grad.astype(BF)
    branch_ref[...] = branch
    arrive(wo_own, wo_scr, sems, cuts, 0, pairs)
    att_grad = mm(branch, wo_scr[...], NT).astype(BF)

    low = lax.broadcasted_iota(jnp.int32, (rows, PAIR), 1) < HEAD
    low_wide = lax.broadcasted_iota(jnp.int32, (total, PAIR), 1) < HEAD
    zero = jnp.zeros((rows, PAIR), BF)
    pad = jnp.zeros((rows, lanes - total), F32)
    sub = lax.broadcasted_iota(jnp.int32, (8, lanes), 0)
    for pair in range(pairs):
        part = slice(pair * PAIR, (pair + 1) * PAIR)
        later = slice(width + pair * PAIR, width + (pair + 1) * PAIR)
        q = q_ref[:, part]
        k = kv_ref[:, part]
        v = kv_ref[:, later]
        da = att_grad[:, part]
        pltpu.make_async_copy(
            p_hbm.at[pl.ds(2 * pair, 2)], p_scr.at[pl.ds(2 * pair, 2)], sems.at[pair]
        ).wait()
        dqs, dks, dvs = [], [], []
        for side in range(2):
            head = 2 * pair + side
            masked = jnp.where(low, da, zero) if side == 0 else jnp.where(low, zero, da)
            share = p_scr[head]
            wide = share.astype(F32)
            dp = mm(masked, v, NT)
            ds = wide * (dp - jnp.sum(wide * dp, axis=-1, keepdims=True))
            dsb = ds.astype(BF)
            dqs.append(mm(dsb, k))
            dks.append(mm(dsb, q, TN))
            dvs.append(mm(share, da, TN))
            padded = jnp.concatenate([ds, pad], axis=1)
            fold = None
            for block in range(rows // 8):
                moved = pltpu.roll(
                    padded[8 * block : 8 * block + 8], (rows - 1 - 8 * block) % lanes, 1
                )
                fold = moved if fold is None else fold + moved
            for bit in (1, 2, 4):
                fold = jnp.where((sub & bit) != 0, pltpu.roll(fold, lanes - bit, 1), fold)
            diag_scr[head : head + 1, :] = jnp.sum(fold, axis=0, keepdims=True)
        dq_ref[:, part] = (jnp.where(low, dqs[0], dqs[1]) * 0.125).astype(BF)
        dkv_scr[:, part] = (jnp.where(low_wide, dks[0], dks[1]) * 0.125).astype(BF)
        dkv_scr[:, later] = jnp.where(low_wide, dvs[0], dvs[1]).astype(BF)
    table = mm(diag_scr[...], onehot_ref[...], NT, HIGH)
    buckets = onehot_ref.shape[0]
    base = (experts + 1) * (width // 128)
    for head in range(2 * pairs):
        at = head * buckets
        small_ref[base + at // 128 : base + at // 128 + 1, at % 128 : at % 128 + buckets] = table[
            head : head + 1, :
        ]
    own_ref[...] = dkv_scr[pl.ds(pl.multiple_of(sec * rows, rows), rows), :]
    other_ref[...] = dkv_scr[pl.ds(pl.multiple_of((1 - sec) * rows, rows), rows), :]


def attend_backward(
    layer,
    capacity,
    sec,
    g,
    middle,
    sent,
    code_col,
    probs,
    gate_grad,
    gain,
    router,
    q,
    kv,
    onehot,
    shares,
    wo,
    deps,
):
    rows, width = middle.shape
    heads = width // HEAD
    experts = router.shape[0]
    packed = (experts + 1) * (width // 128) + heads * onehot.shape[0] // 128
    return call(
        functools.partial(attend_back_kernel, layer, capacity),
        "attend_backward",
        cost(8e9, 6e6),
        [
            (sec, SM),
            g,
            middle,
            sent,
            code_col,
            probs,
            gate_grad,
            gain,
            router,
            q,
            kv,
            onehot,
            (shares, ANY),
            *far(wo),
        ],
        [
            sds((rows, width), F32),
            sds((rows, width), BF),
            sds((rows, width), BF),
            sds((rows, 2 * width), BF),
            sds((rows, 2 * width), BF),
            sds((packed, 128), F32),
        ],
        [
            pltpu.VMEM((2 * rows, 2 * width), BF),
            pltpu.VMEM((heads, SHIFT), F32),
            pltpu.VMEM((heads, rows, 2 * rows), BF),
            pltpu.VMEM((width, width), BF),
            pltpu.SemaphoreType.DMA((heads // 2 + 1,)),
        ],
        deps,
    )


def project_back_kernel(
    layer,
    last,
    capacity,
    sec_ref,
    dq_ref,
    own_ref,
    come_ref,
    mid_grad_ref,
    x_ref,
    gain_ref,
    small_in_ref,
    *rest,
):
    if last:
        late_ref, w_own, w_other, rows_ref, grad_ref, mine_ref, small_ref, w_scr, sems = rest
    else:
        comb_ref, probs_ref, row_ref, col_ref, w_own, w_other = rest[:6]
        rows_ref, grad_ref, small_ref, gate_grad_ref, out_ref, w_scr, sems = rest[6:]
    width = x_ref.shape[1]
    cuts = col_cuts(w_scr.shape[1], width)
    fetch(sec_ref[0], layer, w_own, w_other, w_scr, sems, cuts)
    rows_ref[:, :width] = dq_ref[...]
    rows_ref[:, width:] = (own_ref[...].astype(F32) + come_ref[...].astype(F32)).astype(BF)
    normed_grad = None
    for index in range(3):
        part = slice(index * width, (index + 1) * width)
        arrive(w_own, w_scr, sems, cuts, index)
        fresh = mm(rows_ref[:, part], w_scr[:, part], NT)
        normed_grad = fresh if normed_grad is None else normed_grad + fresh
    x = x_ref[...].astype(F32)
    scale = rms(x)
    unit = x * scale
    held = small_in_ref.shape[0]
    small_ref[:held, :] = small_in_ref[...]
    pack_rows(small_ref, held, jnp.sum(normed_grad * unit, axis=0, keepdims=True))
    held += width // 128
    small_ref[held:, :] = jnp.zeros((small_ref.shape[0] - held, 128), F32)
    if last:
        first = sec_ref[0] == 0
        early, late = small_ref[...], late_ref[...]
        mine_ref[...] = jnp.where(first, early, late)
        small_ref[...] = jnp.where(first, late, early)
    unit_grad = normed_grad * gain_ref[...]
    grad = mid_grad_ref[...] + scale * (
        unit_grad - unit * jnp.mean(unit_grad * unit, axis=-1, keepdims=True)
    )
    rounded = grad.astype(BF)
    grad_ref[...] = rounded
    if not last:
        gate_grad_ref[...], out_ref[...] = send_back(
            rounded.astype(F32),
            comb_ref[...].astype(F32),
            probs_ref[...],
            row_ref[...],
            col_ref[...],
            out_ref.shape[0],
            capacity,
        )


def project_backward(
    layer, capacity, sec, dq, own, come, middle_grad, x, gain, small, w, before
):
    rows, width = x.shape
    wide = w[0].shape[1]
    last = len(before) == 1
    packed = sds((-(-(small.shape[0] + width // 128) // 8) * 8, 128), F32)
    outs = [sds((rows, wide), BF), sds((rows, width), BF), packed]
    more = list(before)
    if last:
        outs += [packed]
    else:
        outs += [sds((rows, 1), F32), sds((before[1].shape[1] * SLOTS, width), BF)]
    return call(
        functools.partial(project_back_kernel, layer, last, capacity),
        "project_backward",
        cost(2 * rows * width * wide, 2 * width * wide),
        [(sec, SM), dq, own, come, middle_grad, x, gain, small, *more, *far(w)],
        outs,
        [pltpu.VMEM((width, wide), BF), pltpu.SemaphoreType.DMA((3,))],
    )


def spread_kernel(place_ref, *refs):
    own, other, out_ref = refs[:2], refs[2:4], refs[4]
    width = own[0].shape[1]
    lanes = out_ref.shape[1]
    normed = jnp.concatenate([own[0][...], other[0][...]], axis=0)
    attended = jnp.concatenate([own[1][...], other[1][...]], axis=0)
    mixed = jnp.where(place_ref[0] == 0, normed, attended)
    feature = lax.broadcasted_iota(jnp.int32, (lanes, width), 1)
    lane = lax.broadcasted_iota(jnp.int32, (lanes, 1), 0)
    block, place = lane // 16, lane % 16
    base = block * 12
    main = jnp.where(place < 12, base + place, -1)
    late = [jnp.where(place < 12, -1, base + 4 * group + place - 12) for group in range(3)]
    for index, (values, source) in enumerate(
        [(normed, main), (mixed, main), (mixed, late[0]), (mixed, late[1]), (mixed, late[2])]
    ):
        hit = jnp.where(feature == source, 1.0, 0.0).astype(BF)
        out_ref[index] = mm(hit, values, NT).astype(BF)


def spread_features(place, shards, own, other):
    rows = own[0].shape[0]
    return call(
        spread_kernel,
        "spread_features",
        cost(3e9, 4e6),
        [(place, SM), *own, *other],
        [sds((5, shards * 16, 2 * rows), BF)],
    )[0]


def projection_weight_kernel(base, place_ref, left_hbm, *refs):
    own, other = refs[:2], refs[2:4]
    out_hbm, left, out_ref, sems, leave = refs[-5:]
    step = out_ref.shape[1] // 3
    first = place_ref[0] == 0
    for index in range(5):
        pltpu.make_async_copy(left_hbm.at[index], left.at[index], sems.at[index]).start()

    def columns(group):
        late = 4 + group
        parts = []
        for rows_ref, branch_ref in (own, other):
            upper = rows_ref[:, group * step : (group + 1) * step]
            if late < 6:
                lower = rows_ref[:, late * step : (late + 1) * step]
            else:
                lower = branch_ref[:, (late - 6) * step : (late - 5) * step]
            parts.append(jnp.where(first, upper, lower))
        return jnp.concatenate(parts, axis=0)

    def copy(group):
        return pltpu.make_async_copy(
            out_ref.at[:, pl.ds(group * step, step)],
            out_hbm.at[:, pl.ds(base + group * step, step)],
            leave.at[group],
        )

    for index in range(5):
        pltpu.make_async_copy(left_hbm.at[index], left.at[index], sems.at[index]).wait()
    tail = columns(3)
    for group in range(3):
        total = mm(left[0 if group < 2 else 1], columns(group)) + mm(left[2 + group], tail)
        out_ref[:, group * step : (group + 1) * step] = total.astype(BF)
        copy(group).start()
    for group in range(3):
        copy(group).wait()


def projection_weights(place, left, own, other, held=None):
    wide = (own[0].shape[1] + own[1].shape[1]) // 8 * 3
    height = left.shape[1]
    more = [] if held is None else [(held, ANY)]
    return call(
        functools.partial(projection_weight_kernel, wide if more else 0),
        "projection_weights",
        cost(2e9, 8e6),
        [(place, SM), (left, ANY), *own, *other, *more],
        [(sds((height, 2 * wide + 128), BF), ANY)],
        [
            pltpu.VMEM(left.shape, BF),
            pltpu.VMEM((height, wide), BF),
            pltpu.SemaphoreType.DMA((5,)),
            pltpu.SemaphoreType.DMA((3,)),
        ],
        aliases={6: 0} if more else {},
    )[0]


def ride_kernel(shares_ref, held_hbm, out_hbm, scr, sem):
    shards = shares_ref.shape[0]
    total = jnp.sum(shares_ref[...], axis=0)
    high = total.astype(BF).astype(F32)
    row = lax.broadcasted_iota(jnp.int32, scr.shape, 0) % 16
    tile = jnp.where(row == 0, high, jnp.where(row == 1, total - high, 0.0))
    scr[...] = tile.astype(BF)
    at = out_hbm.shape[1] - 128
    copy = pltpu.make_async_copy(scr, out_hbm.at[:, pl.ds(at, 128)], sem.at[0])
    copy.start()
    copy.wait()


def ride(shares, held):
    return call(
        ride_kernel,
        "ride",
        cost(1e6, 1e6),
        [shares, (held, ANY)],
        [(sds(held.shape, BF), ANY)],
        [pltpu.VMEM((held.shape[0], 128), BF), pltpu.SemaphoreType.DMA((1,))],
        aliases={1: 0},
    )[0]


def unpack_rows(total):
    width = total.shape[1]
    left = total[12:].reshape(4, 3, width // 3).transpose(1, 0, 2).reshape(12, width // 3)
    return jnp.concatenate([total[:12], left], axis=1)


def body(
    tokens,
    cotangent,
    expert_route,
    capacity_slot,
    buckets,
    qkv_weight,
    attention_out,
    relative_bias,
    attention_gain,
    mixture_gain,
    router,
    expert_in,
    expert_out,
):
    sec = lax.axis_index("section")
    ctx = lax.axis_index("context")
    place = jnp.stack([sec, ctx]).astype(jnp.int32)
    rows, width = tokens.shape[2:]
    experts = router.shape[2]
    heads = width // HEAD
    bucket_count = relative_bias.shape[1]
    capacity = (5 * rows + 4 * experts - 1) // (4 * experts)
    local = ("context", "dp")
    section = ("context", "expert", "dp")
    blocks = lax.axis_size(local)
    contexts = lax.axis_size("context")
    shards = lax.axis_size(section)
    grid = ("section", "context")

    def swap(value):
        return lax.ppermute(value, "section", SWAP)

    def pick(values, at):
        return jnp.where(at == 0, values[0], values[1])

    def come_over(value):
        return lax.ppermute(value, grid, [(0, 1), (3, 2)])

    def exchange(value):
        spread = value.reshape(experts, SLOTS, width)
        return lax.all_to_all(spread, "expert", 0, 0, tiled=True).reshape(value.shape)

    def shared(value):
        return lax.all_to_all(value, section, 0, 0, tiled=True)

    def together(value):
        return lax.all_gather(value, "section", axis=0, tiled=True)

    def both(value):
        return (value, swap(value))

    own, code_leave, tok_leave, cot_leave = pack(
        place,
        attention_gain,
        mixture_gain,
        router[0].T,
        expert_route[0],
        capacity_slot[0],
        relative_bias[0].T,
        tokens[:, 0],
        cotangent[:, 0],
    )
    tok_come = come_over(tok_leave)
    packs = together(gate(own, tok_come))
    codes_come = together(lax.ppermute(code_leave, "context", SWAP))
    w_qkv = both(qkv_weight[0])
    w_out = both(attention_out[0])
    cot_come = come_over(cot_leave)

    x, normed, q, kv, middle, probs, attended, shares = ([None] * 2 for _ in range(8))
    received, active, slope, hidden, left = ([None, None] for _ in range(5))
    x[0], normed[0], q[0], kv[0] = first_projection(
        0, place, tokens[:, 0], tok_come, packs, w_qkv
    )
    for layer in range(2):
        kv[layer] = together(kv[layer])
        if layer == 0:
            prepared = prepare(
                place,
                buckets.reshape(1, -1),
                packs,
                codes_come,
                expert_in[0, 0],
                expert_out[0, 0],
                (experts, heads, bucket_count),
                rows,
                384,
                [kv[0], w_out[1]],
            )
            onehot, bias0, vectors = prepared[:3]
            gain_a, gain_m, routers, code_rows, code_cols = zip(prepared[3:8], prepared[8:13])
            bias = [bias0, None]
            w_up, w_down = ((item, swap(item)) for item in prepared[13:])
        middle[layer], probs[layer], attended[layer], shares[layer], outgoing = attend(
            layer,
            capacity,
            place,
            x[layer],
            q[layer],
            kv[layer],
            gain_m[layer],
            routers[layer],
            code_rows[layer],
            bias[layer],
            w_out,
        )
        received[layer] = exchange(outgoing)
        pair = (normed[layer], attended[layer])
        left[layer] = spread_features(place, shards, pair, [swap(item) for item in pair])
        deps = [left[0]]
        if layer == 0:
            bias[1] = bias_table(vectors, rows, 384, [outgoing])
            deps = [bias[1]]
        result, active[layer], slope[layer] = expert_forward(
            layer, place, received[layer], w_up, w_down, deps
        )
        returned = exchange(result)
        if layer == 0:
            combined, hidden[0], normed[1], q[1], kv[1] = join(
                1, capacity, place, middle[0], returned, probs[0], code_cols[0], gain_a[1], w_qkv
            )
            x[1] = hidden[0]
        else:
            hidden[1], g, gate_grad, outgoing = turn(
                capacity,
                place,
                middle[1],
                returned,
                probs[1],
                code_rows[1],
                code_cols[1],
                cotangent[:, 0],
                cot_come,
            )

    def spread_out(values):
        one = lax.ppermute(pick(values, ctx), grid, [(0, 0), (1, 2), (2, 1), (3, 3)])
        two = lax.ppermute(pick(values, 1 - ctx), grid, [(0, 2), (1, 0), (2, 3), (3, 1)])
        return one, two

    def side_by_side(one, two):
        return jnp.stack([jnp.where(sec == 0, one, two), jnp.where(sec == 0, two, one)])

    hidden_parts = spread_out(hidden)
    hidden_states = side_by_side(*hidden_parts)

    grads, expert_sums, small = ([None, None] for _ in range(3))
    held = None
    for layer in (1, 0):
        result_grad = exchange(outgoing)
        deps = [left[1]] if layer else [held]
        sent, inner_grad = expert_backward(
            layer, place, result_grad, slope[layer], w_up, w_down, deps
        )
        operands = (received[layer], inner_grad, active[layer], result_grad)
        half = expert_weights(place, blocks, operands, [swap(item) for item in operands])
        sent = exchange(sent)
        half = gate(half, sent)
        expert_sums[layer] = lax.psum_scatter(
            half.reshape(-1, half.shape[2]), local, scatter_dimension=0, tiled=True
        )
        middle_grad, branch, dq, own, other, packed = attend_backward(
            layer,
            capacity,
            place,
            g,
            middle[layer],
            sent,
            code_cols[layer],
            probs[layer],
            gate_grad,
            gain_m[layer],
            routers[layer],
            q[layer],
            kv[layer],
            onehot,
            shares[layer],
            w_out,
            [half, *hidden_parts],
        )
        before = (combined, probs[0], code_rows[0], code_cols[0]) if layer == 1 else (small[1],)
        back = project_backward(
            layer,
            capacity,
            place,
            dq,
            own,
            swap(other),
            middle_grad,
            x[layer],
            gain_a[layer],
            packed,
            w_qkv,
            before,
        )
        rows_grad, grads[layer], small[layer] = back[:3]
        if layer == 1:
            g, gate_grad, outgoing = grads[1], back[3], back[4]
        operands = (rows_grad, branch)
        swapped = [swap(item) for item in operands]
        held = projection_weights(place, left[layer], operands, swapped, held)

    mine = small[0] + swap(back[3])
    tail = ride(shared(mine.reshape(shards, 1, 128)), held).reshape(shards, 16, -1)
    tail = shared(tail)
    wide = tail.shape[2] - 128
    mine = jnp.sum(tail[:, 0:2, wide:].astype(F32), axis=1)
    flat = mine.reshape(-1)
    count = experts * width
    router_grad = flat[:count].reshape(experts, width).T
    mixture_gain_grad = flat[count : count + width]
    count += width
    relative_grad = flat[count : count + heads * bucket_count].reshape(heads, bucket_count).T
    count += heads * bucket_count
    attention_gain_grad = flat[count : count + width]

    total = jnp.sum(tail[:, :, :wide].astype(F32), axis=0)
    projections = [unpack_rows(total[:, wide // 2 :]), unpack_rows(total[:, : wide // 2])]
    whole = (pick(projections, sec), swap(pick(projections, 1 - sec)))
    whole = jnp.concatenate([pick(whole, sec), pick(whole, 1 - sec)], axis=1)
    cut = qkv_weight.shape[2]

    whole_e = (pick(expert_sums, sec), swap(pick(expert_sums, 1 - sec)))
    first, second = pick(whole_e, sec), pick(whole_e, 1 - sec)
    mid = width // 2
    in_grad = jnp.concatenate([first[:mid], second[:mid]], axis=0).astype(F32)
    out_grad = jnp.concatenate([first[mid:], second[mid:]], axis=1).astype(F32)

    input_grads = side_by_side(*spread_out(grads)).astype(F32)
    return (
        hidden_states[None, :, None],
        input_grads[None, :, None],
        whole[None, :, :cut],
        whole[None, :, cut:],
        relative_grad[None],
        attention_gain_grad[None],
        mixture_gain_grad[None],
        router_grad[None],
        in_grad[None, None],
        out_grad[None, None],
    )


def solution(mesh):
    return jax.shard_map(
        body,
        mesh=mesh,
        in_specs=(
            P(None, ("expert", "dp"), "context", None),
            P(None, ("expert", "dp"), "context", None),
            P("section", None, ("expert", "dp"), "context"),
            P("section", None, ("expert", "dp"), "context"),
            P(),
            P("section", None, None),
            P("section", None, None),
            P("section", None, None),
            P("section", None),
            P("section", None),
            P("section", None, None),
            P("section", "expert", None, None),
            P("section", "expert", None, None),
        ),
        out_specs=(
            P("section", None, ("expert", "dp"), "context", None),
            P("section", None, ("expert", "dp"), "context", None),
            P("section", ("context", "expert", "dp"), None),
            P("section", ("context", "expert", "dp"), None),
            P("section", None, None),
            P("section", None),
            P("section", None),
            P("section", None, None),
            P("section", "expert", None, ("context", "dp")),
            P("section", "expert", ("context", "dp"), None),
        ),
        check_vma=False,
    )
```

```python
import functools

import jax
import jax.numpy as jnp
from jax import lax
from jax.experimental import pallas as pl
from jax.experimental.pallas import tpu as pltpu
from jax.sharding import PartitionSpec as P

BF = jnp.bfloat16
F32 = jnp.float32
HIGH = lax.Precision.HIGHEST
EPS = 1e-06
HEAD = 64
PAIR = 2 * HEAD
SLOTS = 32
SHIFT = 512
COLUMN = 4
SWAP = [(0, 1), (1, 0)]
NN = (((1,), (0,)), ((), ()))
NT = (((1,), (1,)), ((), ()))
TN = (((0,), (0,)), ((), ()))


def mm(a, b, dims=NN, precision=None):
    return lax.dot_general(a, b, dims, precision=precision, preferred_element_type=F32)


SM = pl.BlockSpec(memory_space=pltpu.SMEM)
ANY = pl.BlockSpec(memory_space=pl.ANY)


def call(kernel, name, estimate, operands, outs, scratch=(), deps=(), aliases={}):
    def whole(item):
        if isinstance(item, tuple):
            return item
        rank = len(item.shape)
        return item, pl.BlockSpec(item.shape, lambda step: (0,) * rank)

    operands = [whole(item) for item in operands]
    outs = [whole(item) for item in outs]
    count = len(operands)
    operands += [(item, ANY) for item in deps]

    def inner(*refs):
        kernel(*refs[:count], *refs[count + len(deps) :])

    return pl.pallas_call(
        inner,
        out_shape=tuple(item for item, _ in outs),
        grid=(1,),
        in_specs=[spec for _, spec in operands],
        out_specs=tuple(spec for _, spec in outs),
        scratch_shapes=list(scratch),
        compiler_params=params(),
        cost_estimate=estimate,
        input_output_aliases=aliases,
        name=name,
    )(*[item for item, _ in operands])


def gate(value, *others):
    def kernel(*refs):
        pass

    return pl.pallas_call(
        kernel,
        out_shape=sds(value.shape, value.dtype),
        in_specs=[ANY] * (1 + len(others)),
        out_specs=ANY,
        input_output_aliases={0: 0},
        compiler_params=params(),
        cost_estimate=cost(0, 0),
        name="gate",
    )(value, *others)


def sds(shape, dtype):
    return jax.ShapeDtypeStruct(shape, dtype)


def far(items):
    return [(item, ANY) for item in items]


def params():
    return pltpu.CompilerParams(vmem_limit_bytes=64 * 1024 * 1024)


def cost(flops, size):
    return pl.CostEstimate(flops=int(flops), bytes_accessed=int(size), transcendentals=0)


def col_cuts(width, step):
    return [(slice(None), pl.ds(at, step)) for at in range(0, width, step)]


def row_cuts(height, step):
    return [(pl.ds(at, step), slice(None)) for at in range(0, height, step)]


def fetch(sec, layer, own, other, dst, sems, cuts, base=0):
    fetch_all(sec, layer, [(own, other, dst, cuts, base)], sems)


def fetch_all(sec, layer, items, sems):
    def go(side):
        for index in range(len(items[0][3])):
            for item in items:
                cut = item[3][index]
                pltpu.make_async_copy(
                    item[side].at[cut], item[2].at[cut], sems.at[item[4] + index]
                ).start()

    pl.when(sec == layer)(lambda: go(0))
    pl.when(sec != layer)(lambda: go(1))


def arrive(own, dst, sems, cuts, index, base=0):
    cut = cuts[index]
    pltpu.make_async_copy(own.at[cut], dst.at[cut], sems.at[base + index]).wait()


def depart(src, dst, sems, cuts, index, base=0):
    cut = cuts[index]
    pltpu.make_async_copy(src.at[cut], dst.at[cut], sems.at[base + index]).start()


def rms(values):
    return lax.rsqrt(jnp.mean(values * values, axis=-1, keepdims=True) + EPS)


def slot_rows(code_row, rows, capacity):
    target = jnp.where((code_row & (SLOTS - 1)) < capacity, code_row, -1)
    return (
        lax.broadcasted_iota(jnp.int32, (rows, code_row.shape[1]), 0) == target
    ).astype(F32).astype(BF)


def slot_cols(code_col, rows, capacity):
    target = jnp.where((code_col & (SLOTS - 1)) < capacity, code_col, -1)
    return (
        lax.broadcasted_iota(jnp.int32, (code_col.shape[0], rows), 1) == target
    ).astype(F32).astype(BF)


def project(normed, w_own, w_scr, sems, cuts, q_ref, kv_ref):
    step = q_ref.shape[1]
    for index in range(3):
        arrive(w_own, w_scr, sems, cuts, index)
        part = mm(normed, w_scr[:, index * step : (index + 1) * step]).astype(BF)
        if index == 0:
            q_ref[...] = part
        else:
            kv_ref[:, (index - 1) * step : index * step] = part


def fill_bias(vectors, out_ref, done=None):
    heads, rows, width = out_ref.shape
    lanes = vectors.shape[1]
    sub = lax.broadcasted_iota(jnp.int32, (8, lanes), 0)
    for head in range(heads):
        base = jnp.broadcast_to(vectors[head : head + 1, :], (8, lanes))
        for bit in (1, 2, 4):
            base = jnp.where((sub & bit) != 0, pltpu.roll(base, bit, 1), base)
        for block in range(rows // 8):
            moved = pltpu.roll(base, (8 * block - (rows - 1)) % lanes, 1)
            out_ref[head, 8 * block : 8 * block + 8, :] = moved[:, :width]
        if done is not None:
            done(head)


GAIN_M, ROUTER = 1, 2


def pack_kernel(
    place_ref,
    gain_a,
    gain_m,
    router,
    route,
    slot,
    table,
    tokens,
    cotangent,
    out_ref,
    code_ref,
    tok_ref,
    cot_ref,
):
    ctx = place_ref[1]
    experts = router.shape[0]
    rows = route.shape[2]
    out_ref[...] = jnp.zeros(out_ref.shape, F32)
    out_ref[0:1, :] = gain_a[...]
    out_ref[GAIN_M : GAIN_M + 1, :] = gain_m[...]
    out_ref[ROUTER : ROUTER + experts, :] = router[...]
    at = ROUTER + experts
    code = [(route[micro] * SLOTS + slot[micro]).astype(F32) for micro in range(2)]
    out_ref[at : at + 1, :rows] = code[0]
    out_ref[at + 1 : at + 2, :rows] = code[1]
    at += 2
    out_ref[at : at + table.shape[0], : table.shape[1]] = table[...]
    tok_ref[...] = jnp.where(ctx == 0, tokens[1], tokens[0])
    code_ref[...] = jnp.zeros(code_ref.shape, F32)
    code_ref[0:1, :rows] = jnp.where(ctx == 0, code[1], code[0])
    cot_ref[...] = jnp.where(ctx == 0, cotangent[1], cotangent[0])


def pack(place, gain_a, gain_m, router, route, slot, table, tokens, cotangent):
    rows, width = tokens.shape[1:]
    height = ROUTER + router.shape[0] + route.shape[0] + table.shape[0]
    return call(
        pack_kernel,
        "pack",
        cost(1e6, 2e6),
        [(place, SM), gain_a, gain_m, router, route, slot, table, tokens, cotangent],
        [sds((height, width), F32), sds((8, 256), F32)] + [sds((rows, width), BF)] * 2,
    )


def prepare_kernel(
    place_ref, buckets_ref, packs_ref, come_ref, up_hbm, onehot_ref, bias_hbm, vec_ref, *rest
):
    *outs, up_copy, bias_ref, bucket_scr, up_scr, leave, enter, moving = rest
    step = up_hbm.shape[0] // 4
    pieces = [pl.ds(index * step, step) for index in range(4)]
    for index, cut in enumerate(pieces):
        pltpu.make_async_copy(up_hbm.at[cut], up_scr.at[cut], enter.at[index]).start()
    sec, ctx = place_ref[0], place_ref[1]
    first = sec == 0
    experts = outs[2].shape[0]
    rows = outs[3].shape[1]
    heads = bias_ref.shape[0]
    bucket_count = onehot_ref.shape[0]
    bucket_scr[...] = jnp.full(bucket_scr.shape, -1, jnp.int32)
    bucket_scr[:, : buckets_ref.shape[1]] = buckets_ref[...]
    wide = bucket_scr[...]
    span = jnp.where(first, pltpu.roll(wide, wide.shape[1] - rows, 1), wide)[:, :SHIFT]
    lane = lax.broadcasted_iota(jnp.int32, span.shape, 1)
    span = jnp.where(lane < 3 * rows - 1, span, -1)
    onehot = lax.broadcasted_iota(jnp.int32, onehot_ref.shape, 0) == span
    onehot = jnp.where(onehot, 1.0, 0.0)
    onehot_ref[...] = onehot
    height = packs_ref.shape[0] // 2
    packs = packs_ref[:height], packs_ref[height:]
    at = ROUTER + experts + 2
    tables = [item[at : at + heads, :bucket_count] for item in packs]

    def copy(head):
        return pltpu.make_async_copy(bias_ref.at[head], bias_hbm.at[head], leave.at[head])


    def done(head):
        copy(head).start()
        if head % 2 == 0 and head // 2 < len(pieces):
            index = head // 2
            cut = pieces[index]
            pltpu.make_async_copy(up_hbm.at[cut], up_scr.at[cut], enter.at[index]).wait()
            pltpu.make_async_copy(up_scr.at[cut], up_copy.at[cut], moving.at[index]).start()

    fill_bias(mm(tables[0], onehot, NN, HIGH), bias_ref, done)
    vec_ref[...] = mm(tables[1], onehot, NN, HIGH)
    at = ROUTER + experts
    home = sec == ctx
    eye = lax.broadcasted_iota(jnp.int32, (rows, rows), 0) == lax.broadcasted_iota(
        jnp.int32, (rows, rows), 1
    )
    for layer in range(2):
        pair = packs[layer][at : at + 2, :rows]
        row = jnp.where(ctx == 0, pair[0:1], pair[1:2])
        row = jnp.where(home, row, come_ref[8 * layer : 8 * layer + 1, :rows])
        col = jnp.sum(jnp.where(eye, row, 0.0), axis=1, keepdims=True)
        for index, item in enumerate(
            (
                packs[layer][0:1],
                packs[layer][GAIN_M : GAIN_M + 1],
                packs[layer][ROUTER : ROUTER + experts],
                row.astype(jnp.int32),
                col.astype(jnp.int32),
            )
        ):
            outs[5 * layer + index][...] = item
    for head in range(heads):
        copy(head).wait()
    for index, cut in enumerate(pieces):
        pltpu.make_async_copy(up_scr.at[cut], up_copy.at[cut], moving.at[index]).wait()


def prepare(place, buckets, packs, come, up, sizes, rows, lanes, deps):
    experts, heads, bucket_count = sizes
    width = packs.shape[1]
    each = [
        sds((1, width), F32),
        sds((1, width), F32),
        sds((experts, width), F32),
        sds((1, rows), jnp.int32),
        sds((rows, 1), jnp.int32),
    ]
    return call(
        prepare_kernel,
        "prepare",
        cost(1e7, 4e6),
        [(place, SM), buckets, packs, come, (up, ANY)],
        [
            sds((bucket_count, SHIFT), F32),
            (sds((heads, rows, lanes), F32), ANY),
            sds((heads, SHIFT), F32),
            *each,
            *each,
            (sds(up.shape, BF), ANY),
        ],
        [
            pltpu.VMEM((heads, rows, lanes), F32),
            pltpu.VMEM((1, 2 * SHIFT), jnp.int32),
            pltpu.VMEM(up.shape, BF),
            pltpu.SemaphoreType.DMA((heads,)),
            pltpu.SemaphoreType.DMA((4,)),
            pltpu.SemaphoreType.DMA((4,)),
        ],
        deps,
    )


def bias_kernel(vec_ref, out_ref):
    fill_bias(vec_ref[...], out_ref)


def bias_table(vectors, rows, width, deps):
    return call(
        bias_kernel,
        "bias_table",
        cost(1e7, 4e6),
        [vectors],
        [sds((vectors.shape[0], rows, width), F32)],
        deps=deps,
    )[0]


def chosen_block(place_ref, both_ref, come_ref):
    sec, ctx = place_ref[0], place_ref[1]
    mine = jnp.where(ctx == 0, both_ref[0], both_ref[1])
    return jnp.where(sec == ctx, mine, come_ref[...])


def first_kernel(
    layer,
    place_ref,
    both_ref,
    come_ref,
    packs_ref,
    w_own,
    w_other,
    x_ref,
    normed_ref,
    q_ref,
    kv_ref,
    w_scr,
    sems,
):
    cuts = col_cuts(w_scr.shape[1], w_scr.shape[1] // 3)
    fetch(place_ref[0], layer, w_own, w_other, w_scr, sems, cuts)
    rounded = chosen_block(place_ref, both_ref, come_ref)
    x_ref[...] = rounded
    x = rounded.astype(F32)
    at = layer * (packs_ref.shape[0] // 2)
    normed = (x * rms(x) * packs_ref[at : at + 1]).astype(BF)
    normed_ref[...] = normed
    project(normed, w_own, w_scr, sems, cuts, q_ref, kv_ref)


def first_projection(layer, place, both, come, packs, w):
    rows, width = both.shape[1:]
    wide = w[0].shape[1]
    return call(
        functools.partial(first_kernel, layer),
        "first_projection",
        cost(2 * rows * width * wide, 2 * width * wide),
        [(place, SM), both, come, packs, *far(w)],
        [sds((rows, width), BF)] * 3 + [sds((rows, 2 * width), BF)],
        [pltpu.VMEM((width, wide), BF), pltpu.SemaphoreType.DMA((3,))],
    )


def attend_kernel(
    layer,
    capacity,
    sec_ref,
    x_ref,
    q_ref,
    kv_ref,
    gain_ref,
    router_ref,
    row_ref,
    bias_hbm,
    wo_own,
    wo_other,
    *rest,
):
    if layer == 0:
        move_hbm, mid_ref, probs_ref, att_ref, p_ref, out_ref, moved_hbm, *rest, moving = rest
        bias_scr, wo_scr, p_scr, sems, leave, move_scr = rest
        pltpu.make_async_copy(move_hbm, move_scr, moving.at[0]).start()
    else:
        mid_ref, probs_ref, att_ref, p_ref, out_ref, bias_scr, wo_scr, p_scr, sems, leave = rest

    sec = sec_ref[0]
    rows, width = x_ref.shape
    total = kv_ref.shape[0]
    pairs = width // PAIR
    for pair in range(pairs):
        pltpu.make_async_copy(
            bias_hbm.at[pl.ds(2 * pair, 2)], bias_scr.at[pl.ds(2 * pair, 2)], sems.at[pair]
        ).start()
    cuts = [(slice(None), slice(None))]
    fetch(sec, layer, wo_own, wo_other, wo_scr, sems, cuts, pairs)
    low = lax.broadcasted_iota(jnp.int32, (rows, PAIR), 1) < HEAD
    zero = jnp.zeros((rows, PAIR), BF)
    for pair in range(pairs):
        pltpu.make_async_copy(
            bias_hbm.at[pl.ds(2 * pair, 2)], bias_scr.at[pl.ds(2 * pair, 2)], sems.at[pair]
        ).wait()
    for pair in range(pairs):
        part = slice(pair * PAIR, (pair + 1) * PAIR)
        q = q_ref[:, part]
        k = kv_ref[:, part]
        v = kv_ref[:, width + pair * PAIR : width + (pair + 1) * PAIR]
        both = []
        for side in range(2):
            head = 2 * pair + side
            masked = jnp.where(low, q, zero) if side == 0 else jnp.where(low, zero, q)
            scores = mm(masked, k, NT) * 0.125 + bias_scr[head, :, :total]
            top = jnp.max(scores, axis=-1, keepdims=True)
            raised = jnp.exp(scores - top)
            share = (raised * (1.0 / jnp.sum(raised, axis=-1, keepdims=True))).astype(BF)
            p_scr[head] = share
            both.append(mm(share, v))
        att_ref[:, part] = jnp.where(low, both[0], both[1]).astype(BF)
    for pair in range(pairs):
        pltpu.make_async_copy(
            p_scr.at[pl.ds(2 * pair, 2)], p_ref.at[pl.ds(2 * pair, 2)], leave.at[pair]
        ).start()
    if layer == 0:
        pltpu.make_async_copy(move_hbm, move_scr, moving.at[0]).wait()
        pltpu.make_async_copy(move_scr, moved_hbm, moving.at[1]).start()
    arrive(wo_own, wo_scr, sems, cuts, 0, pairs)
    middle = x_ref[...].astype(F32) + mm(att_ref[...], wo_scr[...])
    mid_ref[...] = middle
    normed = middle * rms(middle) * gain_ref[...]
    logits = mm(normed, router_ref[...], NT, HIGH)
    raised = jnp.exp(logits - jnp.max(logits, axis=-1, keepdims=True))
    probs_ref[...] = raised / jnp.sum(raised, axis=-1, keepdims=True)
    slots = slot_rows(row_ref[...], out_ref.shape[0], capacity)
    out_ref[...] = mm(slots, normed.astype(BF)).astype(BF)
    for pair in range(pairs):
        pltpu.make_async_copy(
            p_scr.at[pl.ds(2 * pair, 2)], p_ref.at[pl.ds(2 * pair, 2)], leave.at[pair]
        ).wait()
    if layer == 0:
        pltpu.make_async_copy(move_scr, moved_hbm, moving.at[1]).wait()


def attend(layer, capacity, sec, x, q, kv, gain, router, code_row, bias, wo, move=()):
    rows, width = x.shape
    experts = router.shape[0]
    heads = width // HEAD
    wide = bias.shape[2]
    return call(
        functools.partial(attend_kernel, layer, capacity),
        "attend",
        cost(4e9, 6e6),
        [(sec, SM), x, q, kv, gain, router, code_row, (bias, ANY), *far(wo), *far(move)],
        [
            sds((rows, width), F32),
            sds((rows, experts), F32),
            sds((rows, width), BF),
            (sds((heads, rows, 2 * rows), BF), ANY),
            sds((experts * SLOTS, width), BF),
            *[(sds(item.shape, BF), ANY) for item in move],
        ],
        [
            pltpu.VMEM((heads, rows, wide), F32),
            pltpu.VMEM((width, width), BF),
            pltpu.VMEM((heads, rows, 2 * rows), BF),
            pltpu.SemaphoreType.DMA((heads // 2 + 1,)),
            pltpu.SemaphoreType.DMA((heads // 2,)),
            *[pltpu.VMEM(item.shape, BF) for item in move],
            *[pltpu.SemaphoreType.DMA((2,)) for item in move],
        ],
    )


def expert_kernel(
    layer,
    sec_ref,
    rec_ref,
    in_own,
    in_other,
    out_own,
    out_other,
    res_ref,
    act_hbm,
    slope_hbm,
    win,
    wout,
    act_ref,
    slope_ref,
    sems,
    leave,
):
    sec = sec_ref[0]
    hidden = win.shape[1]
    step = 512
    count = hidden // step
    in_cuts = col_cuts(hidden, step)
    out_cuts = row_cuts(hidden, step)
    items = [(in_own, in_other, win, in_cuts, 0), (out_own, out_other, wout, out_cuts, count)]
    fetch_all(sec, layer, items, sems)
    rec = rec_ref[...]
    total = None
    arrive(in_own, win, sems, in_cuts, 0)
    later = mm(rec, win[:, :step])
    for index in range(count):
        part = slice(index * step, (index + 1) * step)
        v = later
        if index + 1 < count:
            arrive(in_own, win, sems, in_cuts, index + 1)
        arrive(out_own, wout, sems, out_cuts, index, count)
        if index + 1 < count:
            later = mm(rec, win[:, (index + 1) * step : (index + 2) * step])
        square = v * v
        t = jnp.tanh(v * (0.7978845608028654 + 0.035677408136300125 * square))
        half = 0.5 * t + 0.5
        rising = v * half
        active = rising.astype(BF)
        act_ref[:, part] = active
        slope = half + (rising - rising * half) * (
            1.5957691216057308 + 0.21406444881780074 * square
        )
        slope_ref[:, part] = slope.astype(BF)
        fresh = mm(active, wout[part, :])
        total = fresh if total is None else total + fresh
        depart(act_ref, act_hbm, leave, in_cuts, index)
        depart(slope_ref, slope_hbm, leave, in_cuts, index, count)
    res_ref[...] = total.astype(BF)
    for index in range(count):
        arrive(act_ref, act_hbm, leave, in_cuts, index)
        arrive(slope_ref, slope_hbm, leave, in_cuts, index, count)


def expert_forward(layer, sec, received, w_in, w_out, deps=()):
    rows, width = received.shape
    hidden = w_in[0].shape[1]
    count = hidden // 512
    return call(
        functools.partial(expert_kernel, layer),
        "expert_forward",
        cost(4 * rows * width * hidden, 4 * width * hidden),
        [(sec, SM), received, *far(w_in), *far(w_out)],
        [sds((rows, width), BF)] + [(sds((rows, hidden), BF), ANY)] * 2,
        [
            pltpu.VMEM((width, hidden), BF),
            pltpu.VMEM((hidden, width), BF),
            pltpu.VMEM((rows, hidden), BF),
            pltpu.VMEM((rows, hidden), BF),
            pltpu.SemaphoreType.DMA((2 * count,)),
            pltpu.SemaphoreType.DMA((2 * count,)),
        ],
        deps,
    )


def gate_of(probs, code_col):
    lane = lax.broadcasted_iota(jnp.int32, probs.shape, 1)
    chosen = (lane == code_col // SLOTS).astype(F32)
    return chosen, jnp.sum(probs * chosen, axis=-1, keepdims=True)


def join_kernel(
    layer,
    capacity,
    sec_ref,
    mid_ref,
    ret_ref,
    probs_ref,
    col_ref,
    gain_ref,
    w_own,
    w_other,
    comb_ref,
    hid_ref,
    normed_ref,
    q_ref,
    kv_ref,
    w_scr,
    sems,
):
    cuts = col_cuts(w_scr.shape[1], w_scr.shape[1] // 3)
    fetch(sec_ref[0], layer, w_own, w_other, w_scr, sems, cuts)
    col = col_ref[...]
    combined = mm(slot_cols(col, ret_ref.shape[0], capacity), ret_ref[...])
    comb_ref[...] = combined.astype(BF)
    _, gate = gate_of(probs_ref[...], col)
    hidden = (mid_ref[...] + gate * combined).astype(BF)
    hid_ref[...] = hidden
    x = hidden.astype(F32)
    normed = (x * rms(x) * gain_ref[...]).astype(BF)
    normed_ref[...] = normed
    project(normed, w_own, w_scr, sems, cuts, q_ref, kv_ref)


def join(layer, capacity, sec, middle, returned, probs, code_col, gain, w):
    rows, width = middle.shape
    wide = w[0].shape[1]
    return call(
        functools.partial(join_kernel, layer, capacity),
        "join",
        cost(2 * rows * width * wide, 2 * width * wide),
        [(sec, SM), middle, returned, probs, code_col, gain, *far(w)],
        [sds((rows, width), BF)] * 4 + [sds((rows, 2 * width), BF)],
        [pltpu.VMEM((width, wide), BF), pltpu.SemaphoreType.DMA((3,))],
    )


def pack_rows(ref, base, values):
    height, width = values.shape
    for row in range(height):
        for at in range(width // 128):
            place = base + row * (width // 128) + at
            ref[place : place + 1, :] = values[row : row + 1, at * 128 : (at + 1) * 128]


def send_back(g, combined, probs, row, col, rows, capacity):
    _, gate = gate_of(probs, col)
    gate_grad = jnp.sum(g * combined, axis=-1, keepdims=True)
    placed = mm(slot_rows(row, rows, capacity), (gate * g).astype(BF))
    return gate_grad, placed.astype(BF)


def turn_kernel(
    capacity,
    place_ref,
    mid_ref,
    ret_ref,
    probs_ref,
    row_ref,
    col_ref,
    both_ref,
    come_ref,
    hid_ref,
    g_ref,
    gate_grad_ref,
    out_ref,
):
    g = chosen_block(place_ref, both_ref, come_ref)
    g_ref[...] = g
    col = col_ref[...]
    probs = probs_ref[...]
    combined = mm(slot_cols(col, ret_ref.shape[0], capacity), ret_ref[...])
    _, gate = gate_of(probs, col)
    hid_ref[...] = (mid_ref[...] + gate * combined).astype(BF)
    gate_grad_ref[...], out_ref[...] = send_back(
        g.astype(F32), combined, probs, row_ref[...], col, out_ref.shape[0], capacity
    )


def turn(capacity, place, middle, returned, probs, code_row, code_col, both, come):
    rows, width = middle.shape
    return call(
        functools.partial(turn_kernel, capacity),
        "turn",
        cost(4 * rows * width * returned.shape[0], 3e6),
        [(place, SM), middle, returned, probs, code_row, code_col, both, come],
        [
            sds((rows, width), BF),
            sds((rows, width), BF),
            sds((rows, 1), F32),
            sds(returned.shape, BF),
        ],
    )


def expert_back_kernel(
    layer,
    sec_ref,
    rec_ref,
    slope_hbm,
    in_own,
    in_other,
    out_own,
    out_other,
    sent_ref,
    grad_hbm,
    win,
    wout,
    slope_ref,
    grad_ref,
    sems,
    leave,
):
    sec = sec_ref[0]
    hidden = win.shape[1]
    step = 512
    count = hidden // step
    in_cuts = col_cuts(hidden, step)
    out_cuts = row_cuts(hidden, step)
    items = [(out_own, out_other, wout, out_cuts, count), (in_own, in_other, win, in_cuts, 0)]
    for index in range(count):
        depart(slope_hbm, slope_ref, sems, in_cuts, index, 2 * count)
    fetch_all(sec, layer, items, sems)
    rec = rec_ref[...]
    total = None
    arrive(out_own, wout, sems, out_cuts, 0, count)
    later = mm(rec, wout[:step, :], NT)
    for index in range(count):
        part = slice(index * step, (index + 1) * step)
        now = later
        if index + 1 < count:
            arrive(out_own, wout, sems, out_cuts, index + 1, count)
        arrive(slope_hbm, slope_ref, sems, in_cuts, index, 2 * count)
        arrive(in_own, win, sems, in_cuts, index)
        if index + 1 < count:
            later = mm(rec, wout[(index + 1) * step : (index + 2) * step, :], NT)
        inner = (now * slope_ref[:, part].astype(F32)).astype(BF)
        grad_ref[:, part] = inner
        fresh = mm(inner, win[:, part], NT)
        total = fresh if total is None else total + fresh
        depart(grad_ref, grad_hbm, leave, in_cuts, index)
    sent_ref[...] = total.astype(BF)
    for index in range(count):
        arrive(grad_ref, grad_hbm, leave, in_cuts, index)


def expert_backward(layer, sec, received, slope, w_in, w_out, deps=()):
    rows, width = received.shape
    hidden = w_in[0].shape[1]
    count = hidden // 512
    return call(
        functools.partial(expert_back_kernel, layer),
        "expert_backward",
        cost(4 * rows * width * hidden, 4 * width * hidden),
        [(sec, SM), received, (slope, ANY), *far(w_in), *far(w_out)],
        [sds((rows, width), BF), (sds((rows, hidden), BF), ANY)],
        [
            pltpu.VMEM((width, hidden), BF),
            pltpu.VMEM((hidden, width), BF),
            pltpu.VMEM((rows, hidden), BF),
            pltpu.VMEM((rows, hidden), BF),
            pltpu.SemaphoreType.DMA((3 * count,)),
            pltpu.SemaphoreType.DMA((count,)),
        ],
        deps,
    )


def expert_weight_kernel(half_ref, *refs):
    rec, grad, act, res, rec_b, grad_b, act_b, res_b, out_ref = refs
    half = rec.shape[1]
    upper = mm(rec[...], grad[...], TN) + mm(rec_b[...], grad_b[...], TN)
    out_ref[0, :half] = upper.astype(BF)
    lower = mm(act[...], res[...], TN) + mm(act_b[...], res_b[...], TN)
    out_ref[0, half : 2 * half] = lower.astype(BF)


def expert_weights(half, blocks, own, other):
    rows, width = own[0].shape
    hidden = own[1].shape[1]
    step = hidden // blocks
    cut = width // 2
    narrow = pl.BlockSpec((rows, cut), lambda b, half_ref: (0, half_ref[0]))
    moving = pl.BlockSpec((rows, step), lambda b, half_ref: (0, b))
    return pl.pallas_call(
        expert_weight_kernel,
        out_shape=sds((blocks, width, step), BF),
        grid_spec=pltpu.PrefetchScalarGridSpec(
            num_scalar_prefetch=1,
            grid=(blocks,),
            in_specs=[narrow, moving, moving, narrow] * 2,
            out_specs=pl.BlockSpec((1, width, step), lambda b, half_ref: (b, 0, 0)),
        ),
        compiler_params=params(),
        cost_estimate=cost(4 * rows * width * hidden, 4 * width * hidden),
        name="expert_weights",
    )(half, *own, *other)


def attend_back_kernel(
    layer,
    capacity,
    sec_ref,
    g_ref,
    mid_ref,
    sent_ref,
    col_ref,
    probs_ref,
    gate_grad_ref,
    gain_ref,
    router_ref,
    q_ref,
    kv_ref,
    onehot_ref,
    p_hbm,
    wo_own,
    wo_other,
    mid_grad_ref,
    branch_ref,
    dq_ref,
    own_ref,
    other_ref,
    small_ref,
    dkv_scr,
    diag_scr,
    p_scr,
    wo_scr,
    sems,
):
    sec = sec_ref[0]
    rows, width = mid_ref.shape
    total = kv_ref.shape[0]
    pairs = width // PAIR
    lanes = diag_scr.shape[1]
    cuts = [(slice(None), slice(None))]
    fetch(sec, layer, wo_own, wo_other, wo_scr, sems, cuts, pairs)
    for pair in range(pairs):
        pltpu.make_async_copy(
            p_hbm.at[pl.ds(2 * pair, 2)], p_scr.at[pl.ds(2 * pair, 2)], sems.at[pair]
        ).start()

    middle = mid_ref[...]
    scale = rms(middle)
    unit = middle * scale
    gain = gain_ref[...]
    col = col_ref[...]
    probs = probs_ref[...]
    chosen, gate = gate_of(probs, col)
    logit_grad = probs * (chosen - gate) * gate_grad_ref[...]
    normed_grad = mm(slot_cols(col, sent_ref.shape[0], capacity), sent_ref[...])
    normed_grad = normed_grad + mm(logit_grad, router_ref[...], NN, HIGH)
    experts = probs.shape[1]
    router_grad = mm(logit_grad, unit * gain, TN, HIGH)
    gain_grad = jnp.sum(normed_grad * unit, axis=0, keepdims=True)
    pack_rows(small_ref, 0, router_grad)
    pack_rows(small_ref, experts * (width // 128), gain_grad)
    unit_grad = normed_grad * gain
    middle_grad = g_ref[...].astype(F32) + scale * (
        unit_grad - unit * jnp.mean(unit_grad * unit, axis=-1, keepdims=True)
    )
    mid_grad_ref[...] = middle_grad
    branch = middle_grad.astype(BF)
    branch_ref[...] = branch
    arrive(wo_own, wo_scr, sems, cuts, 0, pairs)
    att_grad = mm(branch, wo_scr[...], NT).astype(BF)

    low = lax.broadcasted_iota(jnp.int32, (rows, PAIR), 1) < HEAD
    low_wide = lax.broadcasted_iota(jnp.int32, (total, PAIR), 1) < HEAD
    zero = jnp.zeros((rows, PAIR), BF)
    pad = jnp.zeros((rows, lanes - total), F32)
    sub = lax.broadcasted_iota(jnp.int32, (8, lanes), 0)
    for pair in range(pairs):
        pltpu.make_async_copy(
            p_hbm.at[pl.ds(2 * pair, 2)], p_scr.at[pl.ds(2 * pair, 2)], sems.at[pair]
        ).wait()
    for pair in range(pairs):
        part = slice(pair * PAIR, (pair + 1) * PAIR)
        later = slice(width + pair * PAIR, width + (pair + 1) * PAIR)
        q = q_ref[:, part]
        k = kv_ref[:, part]
        v = kv_ref[:, later]
        da = att_grad[:, part]
        dqs, dks, dvs = [], [], []
        for side in range(2):
            head = 2 * pair + side
            masked = jnp.where(low, da, zero) if side == 0 else jnp.where(low, zero, da)
            share = p_scr[head]
            wide = share.astype(F32)
            dp = mm(masked, v, NT)
            ds = wide * (dp - jnp.sum(wide * dp, axis=-1, keepdims=True))
            dsb = ds.astype(BF)
            dqs.append(mm(dsb, k))
            dks.append(mm(dsb, q, TN))
            dvs.append(mm(share, da, TN))
            padded = jnp.concatenate([ds, pad], axis=1)
            fold = None
            for block in range(rows // 8):
                moved = pltpu.roll(
                    padded[8 * block : 8 * block + 8], (rows - 1 - 8 * block) % lanes, 1
                )
                fold = moved if fold is None else fold + moved
            for bit in (1, 2, 4):
                fold = jnp.where((sub & bit) != 0, pltpu.roll(fold, lanes - bit, 1), fold)
            diag_scr[head : head + 1, :] = jnp.sum(fold, axis=0, keepdims=True)
        dq_ref[:, part] = (jnp.where(low, dqs[0], dqs[1]) * 0.125).astype(BF)
        dkv_scr[:, part] = (jnp.where(low_wide, dks[0], dks[1]) * 0.125).astype(BF)
        dkv_scr[:, later] = jnp.where(low_wide, dvs[0], dvs[1]).astype(BF)
    table = mm(diag_scr[...], onehot_ref[...], NT, HIGH)
    buckets = onehot_ref.shape[0]
    base = (experts + 1) * (width // 128)
    for head in range(2 * pairs):
        at = head * buckets
        small_ref[base + at // 128 : base + at // 128 + 1, at % 128 : at % 128 + buckets] = table[
            head : head + 1, :
        ]
    own_ref[...] = dkv_scr[pl.ds(pl.multiple_of(sec * rows, rows), rows), :]
    other_ref[...] = dkv_scr[pl.ds(pl.multiple_of((1 - sec) * rows, rows), rows), :]


def attend_backward(
    layer,
    capacity,
    sec,
    g,
    middle,
    sent,
    code_col,
    probs,
    gate_grad,
    gain,
    router,
    q,
    kv,
    onehot,
    shares,
    wo,
    deps,
):
    rows, width = middle.shape
    heads = width // HEAD
    experts = router.shape[0]
    packed = (experts + 1) * (width // 128) + heads * onehot.shape[0] // 128
    return call(
        functools.partial(attend_back_kernel, layer, capacity),
        "attend_backward",
        cost(8e9, 6e6),
        [
            (sec, SM),
            g,
            middle,
            sent,
            code_col,
            probs,
            gate_grad,
            gain,
            router,
            q,
            kv,
            onehot,
            (shares, ANY),
            *far(wo),
        ],
        [
            sds((rows, width), F32),
            sds((rows, width), BF),
            sds((rows, width), BF),
            sds((rows, 2 * width), BF),
            sds((rows, 2 * width), BF),
            sds((packed, 128), F32),
        ],
        [
            pltpu.VMEM((2 * rows, 2 * width), BF),
            pltpu.VMEM((heads, SHIFT), F32),
            pltpu.VMEM((heads, rows, 2 * rows), BF),
            pltpu.VMEM((width, width), BF),
            pltpu.SemaphoreType.DMA((heads // 2 + 1,)),
        ],
        deps,
    )


def project_back_kernel(
    layer,
    last,
    capacity,
    sec_ref,
    dq_ref,
    own_ref,
    come_ref,
    mid_grad_ref,
    x_ref,
    gain_ref,
    small_in_ref,
    *rest,
):
    if last:
        late_ref, w_own, w_other, rows_ref, grad_ref, mine_ref, small_ref, w_scr, sems = rest
    else:
        comb_ref, probs_ref, row_ref, col_ref, w_own, w_other = rest[:6]
        rows_ref, grad_ref, small_ref, gate_grad_ref, out_ref, w_scr, sems = rest[6:]
    width = x_ref.shape[1]
    cuts = col_cuts(w_scr.shape[1], width)
    fetch(sec_ref[0], layer, w_own, w_other, w_scr, sems, cuts)
    rows_ref[:, :width] = dq_ref[...]
    rows_ref[:, width:] = (own_ref[...].astype(F32) + come_ref[...].astype(F32)).astype(BF)
    normed_grad = None
    for index in range(3):
        part = slice(index * width, (index + 1) * width)
        arrive(w_own, w_scr, sems, cuts, index)
        fresh = mm(rows_ref[:, part], w_scr[:, part], NT)
        normed_grad = fresh if normed_grad is None else normed_grad + fresh
    x = x_ref[...].astype(F32)
    scale = rms(x)
    unit = x * scale
    held = small_in_ref.shape[0]
    small_ref[:held, :] = small_in_ref[...]
    pack_rows(small_ref, held, jnp.sum(normed_grad * unit, axis=0, keepdims=True))
    held += width // 128
    small_ref[held:, :] = jnp.zeros((small_ref.shape[0] - held, 128), F32)
    if last:
        first = sec_ref[0] == 0
        early, late = small_ref[...], late_ref[...]
        mine_ref[...] = jnp.where(first, early, late)
        small_ref[...] = jnp.where(first, late, early)
    unit_grad = normed_grad * gain_ref[...]
    grad = mid_grad_ref[...] + scale * (
        unit_grad - unit * jnp.mean(unit_grad * unit, axis=-1, keepdims=True)
    )
    rounded = grad.astype(BF)
    grad_ref[...] = rounded
    if not last:
        gate_grad_ref[...], out_ref[...] = send_back(
            rounded.astype(F32),
            comb_ref[...].astype(F32),
            probs_ref[...],
            row_ref[...],
            col_ref[...],
            out_ref.shape[0],
            capacity,
        )


def project_backward(
    layer, capacity, sec, dq, own, come, middle_grad, x, gain, small, w, before
):
    rows, width = x.shape
    wide = w[0].shape[1]
    last = len(before) == 1
    packed = sds((-(-(small.shape[0] + width // 128) // 8) * 8, 128), F32)
    outs = [sds((rows, wide), BF), sds((rows, width), BF), packed]
    more = list(before)
    if last:
        outs += [packed]
    else:
        outs += [sds((rows, 1), F32), sds((before[1].shape[1] * SLOTS, width), BF)]
    return call(
        functools.partial(project_back_kernel, layer, last, capacity),
        "project_backward",
        cost(2 * rows * width * wide, 2 * width * wide),
        [(sec, SM), dq, own, come, middle_grad, x, gain, small, *more, *far(w)],
        outs,
        [pltpu.VMEM((width, wide), BF), pltpu.SemaphoreType.DMA((3,))],
    )


def spread_kernel(order, place_ref, *refs):
    own, other, out_ref = refs[:2], refs[2:4], refs[4]
    width = own[0].shape[1]
    lanes = out_ref.shape[1]
    normed = jnp.concatenate([own[0][...], other[0][...]], axis=0)
    attended = jnp.concatenate([own[1][...], other[1][...]], axis=0)
    mixed = jnp.where(place_ref[0] == 0, normed, attended)
    feature = lax.broadcasted_iota(jnp.int32, (lanes, width), 1)
    lane = lax.broadcasted_iota(jnp.int32, (lanes, 1), 0)
    block, place = lane // 16, lane % 16
    if order is not None:
        experts, copies = order
        rest = lanes // 16 // COLUMN
        column, place_in = block // rest, block % rest
        lines = experts // COLUMN
        line = place_in // copies % lines * COLUMN + column
        block = place_in // (lines * copies) * experts * copies + line * copies + place_in % copies
    base = block * 12
    main = jnp.where(place < 12, base + place, -1)
    late = [jnp.where(place < 12, -1, base + 4 * group + place - 12) for group in range(3)]
    for index, (values, source) in enumerate(
        [(normed, main), (mixed, main), (mixed, late[0]), (mixed, late[1]), (mixed, late[2])]
    ):
        hit = jnp.where(feature == source, 1.0, 0.0).astype(BF)
        out_ref[index] = mm(hit, values, NT).astype(BF)


def spread_features(place, shards, own, other, order=None):
    rows = own[0].shape[0]
    return call(
        functools.partial(spread_kernel, order),
        "spread_features",
        cost(3e9, 4e6),
        [(place, SM), *own, *other],
        [sds((5, shards * 16, 2 * rows), BF)],
    )[0]


def projection_weight_kernel(place_ref, left_hbm, *refs):
    own, other = refs[:2], refs[2:4]
    out_hbm, left, out_ref, sems, leave = refs[-5:]
    step = out_ref.shape[1] // 3
    first = place_ref[0] == 0
    for index in range(5):
        pltpu.make_async_copy(left_hbm.at[index], left.at[index], sems.at[index]).start()

    def columns(group):
        late = 4 + group
        parts = []
        for rows_ref, branch_ref in (own, other):
            upper = rows_ref[:, group * step : (group + 1) * step]
            if late < 6:
                lower = rows_ref[:, late * step : (late + 1) * step]
            else:
                lower = branch_ref[:, (late - 6) * step : (late - 5) * step]
            parts.append(jnp.where(first, upper, lower))
        return jnp.concatenate(parts, axis=0)

    def copy(group):
        return pltpu.make_async_copy(
            out_ref.at[:, pl.ds(group * step, step)],
            out_hbm.at[:, pl.ds(group * step, step)],
            leave.at[group],
        )

    for index in range(5):
        pltpu.make_async_copy(left_hbm.at[index], left.at[index], sems.at[index]).wait()
    tail = columns(3)
    for group in range(3):
        total = mm(left[0 if group < 2 else 1], columns(group)) + mm(left[2 + group], tail)
        out_ref[:, group * step : (group + 1) * step] = total.astype(BF)
        copy(group).start()
    for group in range(3):
        copy(group).wait()


def projection_weights(place, left, own, other, spare, deps=()):
    wide = (own[0].shape[1] + own[1].shape[1]) // 8 * 3
    height = left.shape[1]
    return call(
        projection_weight_kernel,
        "projection_weights",
        cost(2e9, 8e6),
        [(place, SM), (left, ANY), *own, *other],
        [(sds((height, wide + spare), BF), ANY)],
        [
            pltpu.VMEM(left.shape, BF),
            pltpu.VMEM((height, wide), BF),
            pltpu.SemaphoreType.DMA((5,)),
            pltpu.SemaphoreType.DMA((3,)),
        ],
        deps,
    )[0]


def ride_kernel(shares_ref, held_hbm, out_hbm, scr, sem):
    shards = shares_ref.shape[0]
    total = jnp.sum(shares_ref[...], axis=0)
    high = total.astype(BF).astype(F32)
    row = lax.broadcasted_iota(jnp.int32, scr.shape, 0) % 16
    tile = jnp.where(row == 0, high, jnp.where(row == 1, total - high, 0.0))
    scr[...] = tile.astype(BF)
    at = out_hbm.shape[1] - 128
    copy = pltpu.make_async_copy(scr, out_hbm.at[:, pl.ds(at, 128)], sem.at[0])
    copy.start()
    copy.wait()


def ride(shares, held):
    return call(
        ride_kernel,
        "ride",
        cost(1e6, 1e6),
        [shares, (held, ANY)],
        [(sds(held.shape, BF), ANY)],
        [pltpu.VMEM((held.shape[0], 128), BF), pltpu.SemaphoreType.DMA((1,))],
        aliases={1: 0},
    )[0]


def unpack_rows(total):
    width = total.shape[1]
    left = total[12:].reshape(4, 3, width // 3).transpose(1, 0, 2).reshape(12, width // 3)
    return jnp.concatenate([total[:12], left], axis=1)


def body(
    tokens,
    cotangent,
    expert_route,
    capacity_slot,
    buckets,
    qkv_weight,
    attention_out,
    relative_bias,
    attention_gain,
    mixture_gain,
    router,
    expert_in,
    expert_out,
):
    sec = lax.axis_index("section")
    ctx = lax.axis_index("context")
    place = jnp.stack([sec, ctx]).astype(jnp.int32)
    rows, width = tokens.shape[2:]
    experts = router.shape[2]
    heads = width // HEAD
    bucket_count = relative_bias.shape[1]
    capacity = (5 * rows + 4 * experts - 1) // (4 * experts)
    local = ("context", "dp")
    section = ("context", "expert", "dp")
    blocks = lax.axis_size(local)
    contexts = lax.axis_size("context")
    shards = lax.axis_size(section)
    grid = ("section", "context")

    def swap(value):
        return lax.ppermute(value, "section", SWAP)

    def pick(values, at):
        return jnp.where(at == 0, values[0], values[1])

    def come_over(value):
        return lax.ppermute(value, grid, [(0, 1), (3, 2)])

    def exchange(value):
        spread = value.reshape(experts, SLOTS, width)
        return lax.all_to_all(spread, "expert", 0, 0, tiled=True).reshape(value.shape)

    def shared(value):
        return lax.all_to_all(value, section, 0, 0, tiled=True)

    def together(value):
        return lax.all_gather(value, "section", axis=0, tiled=True)

    def both(value):
        return (value, swap(value))

    own, code_leave, tok_leave, cot_leave = pack(
        place,
        attention_gain,
        mixture_gain,
        router[0].T,
        expert_route[0],
        capacity_slot[0],
        relative_bias[0].T,
        tokens[:, 0],
        cotangent[:, 0],
    )
    tok_come = come_over(tok_leave)
    packs = together(gate(own, tok_come))
    codes_come = together(lax.ppermute(code_leave, "context", SWAP))
    w_qkv = both(qkv_weight[0])
    w_out = both(attention_out[0])
    cot_come = come_over(cot_leave)

    x, normed, q, kv, middle, probs, attended, shares = ([None] * 2 for _ in range(8))
    received, active, slope, hidden, left = ([None, None] for _ in range(5))
    x[0], normed[0], q[0], kv[0] = first_projection(
        0, place, tokens[:, 0], tok_come, packs, w_qkv
    )
    for layer in range(2):
        kv[layer] = together(kv[layer])
        if layer == 0:
            prepared = prepare(
                place,
                buckets.reshape(1, -1),
                packs,
                codes_come,
                expert_in[0, 0],
                (experts, heads, bucket_count),
                rows,
                384,
                [kv[0], w_out[1]],
            )
            onehot, bias0, vectors = prepared[:3]
            gain_a, gain_m, routers, code_rows, code_cols = zip(prepared[3:8], prepared[8:13])
            bias = [bias0, None]
            w_up = both(prepared[13])
        middle[layer], probs[layer], attended[layer], shares[layer], outgoing, *moved = attend(
            layer,
            capacity,
            place,
            x[layer],
            q[layer],
            kv[layer],
            gain_m[layer],
            routers[layer],
            code_rows[layer],
            bias[layer],
            w_out,
            () if layer else (expert_out[0, 0],),
        )
        if layer == 0:
            w_down = both(moved[0])
        received[layer] = exchange(outgoing)
        pair = (normed[layer], attended[layer])
        order = (experts, lax.axis_size("dp")) if layer else None
        left[layer] = spread_features(place, shards, pair, [swap(item) for item in pair], order)
        deps = [left[0]]
        if layer == 0:
            bias[1] = bias_table(vectors, rows, 384, [outgoing])
            deps = [bias[1]]
        result, active[layer], slope[layer] = expert_forward(
            layer, place, received[layer], w_up, w_down, deps
        )
        returned = exchange(result)
        if layer == 0:
            combined, hidden[0], normed[1], q[1], kv[1] = join(
                1, capacity, place, middle[0], returned, probs[0], code_cols[0], gain_a[1], w_qkv
            )
            x[1] = hidden[0]
        else:
            hidden[1], g, gate_grad, outgoing = turn(
                capacity,
                place,
                middle[1],
                returned,
                probs[1],
                code_rows[1],
                code_cols[1],
                cotangent[:, 0],
                cot_come,
            )

    def spread_out(values):
        one = lax.ppermute(pick(values, ctx), grid, [(0, 0), (1, 2), (2, 1), (3, 3)])
        two = lax.ppermute(pick(values, 1 - ctx), grid, [(0, 2), (1, 0), (2, 3), (3, 1)])
        return one, two

    def side_by_side(one, two):
        return jnp.stack([jnp.where(sec == 0, one, two), jnp.where(sec == 0, two, one)])

    hidden_parts = spread_out(hidden)
    hidden_states = side_by_side(*hidden_parts)

    grads, expert_sums, small = ([None, None] for _ in range(3))
    held = None
    for layer in (1, 0):
        result_grad = exchange(outgoing)
        deps = [left[1]] if layer else [held]
        sent, inner_grad = expert_backward(
            layer, place, result_grad, slope[layer], w_up, w_down, deps
        )
        operands = (received[layer], inner_grad, active[layer], result_grad)
        half = expert_weights(place, blocks, operands, [swap(item) for item in operands])
        sent = exchange(sent)
        half = gate(half, sent)
        expert_sums[layer] = lax.psum_scatter(
            half.reshape(-1, half.shape[2]), local, scatter_dimension=0, tiled=True
        )
        if layer == 0:
            late = gate(held, half).reshape(COLUMN, -1, held.shape[1])
            lines = [list(range(at, at + COLUMN)) for at in range(0, experts, COLUMN)]
            late = lax.all_to_all(late, "expert", 0, 0, axis_index_groups=lines, tiled=True)
        middle_grad, branch, dq, own, other, packed = attend_backward(
            layer,
            capacity,
            place,
            g,
            middle[layer],
            sent,
            code_cols[layer],
            probs[layer],
            gate_grad,
            gain_m[layer],
            routers[layer],
            q[layer],
            kv[layer],
            onehot,
            shares[layer],
            w_out,
            [half, *hidden_parts],
        )
        before = (combined, probs[0], code_rows[0], code_cols[0]) if layer == 1 else (small[1],)
        back = project_backward(
            layer,
            capacity,
            place,
            dq,
            own,
            swap(other),
            middle_grad,
            x[layer],
            gain_a[layer],
            packed,
            w_qkv,
            before,
        )
        rows_grad, grads[layer], small[layer] = back[:3]
        if layer == 1:
            g, gate_grad, outgoing = grads[1], back[3], back[4]
        operands = (rows_grad, branch)
        swapped = [swap(item) for item in operands]
        if layer == 1:
            held = projection_weights(place, left[1], operands, swapped, 0)
        else:
            late = jnp.sum(late.astype(F32), axis=0).astype(BF)
            held = projection_weights(place, left[0], operands, swapped, 128, [late])

    mine = small[0] + swap(back[3])
    tail = ride(shared(mine.reshape(shards, 1, 128)), held).reshape(shards, 16, -1)
    tail = shared(tail)
    late = gate(late, tail).reshape(shards // COLUMN, 16, -1)
    copies = lax.axis_size("dp")
    planes = [
        [at for at in range(shards) if at // copies % COLUMN == column] for column in range(COLUMN)
    ]
    late = lax.all_to_all(late, section, 0, 0, axis_index_groups=planes, tiled=True)
    late = jnp.sum(late.astype(F32), axis=0)
    wide = tail.shape[2] - 128
    mine = jnp.sum(tail[:, 0:2, wide:].astype(F32), axis=1)
    flat = mine.reshape(-1)
    count = experts * width
    router_grad = flat[:count].reshape(experts, width).T
    mixture_gain_grad = flat[count : count + width]
    count += width
    relative_grad = flat[count : count + heads * bucket_count].reshape(heads, bucket_count).T
    count += heads * bucket_count
    attention_gain_grad = flat[count : count + width]

    total = jnp.sum(tail[:, :, :wide].astype(F32), axis=0)
    projections = [unpack_rows(total), unpack_rows(late)]
    whole = (pick(projections, sec), swap(pick(projections, 1 - sec)))
    whole = jnp.concatenate([pick(whole, sec), pick(whole, 1 - sec)], axis=1)
    cut = qkv_weight.shape[2]

    whole_e = (pick(expert_sums, sec), swap(pick(expert_sums, 1 - sec)))
    first, second = pick(whole_e, sec), pick(whole_e, 1 - sec)
    mid = width // 2
    in_grad = jnp.concatenate([first[:mid], second[:mid]], axis=0).astype(F32)
    out_grad = jnp.concatenate([first[mid:], second[mid:]], axis=1).astype(F32)

    input_grads = side_by_side(*spread_out(grads)).astype(F32)
    return (
        hidden_states[None, :, None],
        input_grads[None, :, None],
        whole[None, :, :cut],
        whole[None, :, cut:],
        relative_grad[None],
        attention_gain_grad[None],
        mixture_gain_grad[None],
        router_grad[None],
        in_grad[None, None],
        out_grad[None, None],
    )


def solution(mesh):
    return jax.shard_map(
        body,
        mesh=mesh,
        in_specs=(
            P(None, ("expert", "dp"), "context", None),
            P(None, ("expert", "dp"), "context", None),
            P("section", None, ("expert", "dp"), "context"),
            P("section", None, ("expert", "dp"), "context"),
            P(),
            P("section", None, None),
            P("section", None, None),
            P("section", None, None),
            P("section", None),
            P("section", None),
            P("section", None, None),
            P("section", "expert", None, None),
            P("section", "expert", None, None),
        ),
        out_specs=(
            P("section", None, ("expert", "dp"), "context", None),
            P("section", None, ("expert", "dp"), "context", None),
            P("section", ("context", "expert", "dp"), None),
            P("section", ("context", "expert", "dp"), None),
            P("section", None, None),
            P("section", None),
            P("section", None),
            P("section", None, None),
            P("section", "expert", None, ("context", "dp")),
            P("section", "expert", ("context", "dp"), None),
        ),
        check_vma=False,
    )
```

```python
import functools

import jax
import jax.numpy as jnp
from jax import lax
from jax.experimental import pallas as pl
from jax.experimental.pallas import tpu as pltpu
from jax.sharding import PartitionSpec as P

BF = jnp.bfloat16
F32 = jnp.float32
HIGH = lax.Precision.HIGHEST
EPS = 1e-06
HEAD = 64
PAIR = 2 * HEAD
SLOTS = 32
SHIFT = 512
COLUMN = 4
SWAP = [(0, 1), (1, 0)]
NN = (((1,), (0,)), ((), ()))
NT = (((1,), (1,)), ((), ()))
TN = (((0,), (0,)), ((), ()))


def mm(a, b, dims=NN, precision=None):
    return lax.dot_general(a, b, dims, precision=precision, preferred_element_type=F32)


SM = pl.BlockSpec(memory_space=pltpu.SMEM)
ANY = pl.BlockSpec(memory_space=pl.ANY)


def call(kernel, name, estimate, operands, outs, scratch=(), deps=(), aliases={}):
    def whole(item):
        if isinstance(item, tuple):
            return item
        rank = len(item.shape)
        return item, pl.BlockSpec(item.shape, lambda step: (0,) * rank)

    operands = [whole(item) for item in operands]
    outs = [whole(item) for item in outs]
    count = len(operands)
    operands += [(item, ANY) for item in deps]

    def inner(*refs):
        kernel(*refs[:count], *refs[count + len(deps) :])

    return pl.pallas_call(
        inner,
        out_shape=tuple(item for item, _ in outs),
        grid=(1,),
        in_specs=[spec for _, spec in operands],
        out_specs=tuple(spec for _, spec in outs),
        scratch_shapes=list(scratch),
        compiler_params=params(),
        cost_estimate=estimate,
        input_output_aliases=aliases,
        name=name,
    )(*[item for item, _ in operands])


def gate(value, *others):
    def kernel(*refs):
        pass

    return pl.pallas_call(
        kernel,
        out_shape=sds(value.shape, value.dtype),
        in_specs=[ANY] * (1 + len(others)),
        out_specs=ANY,
        input_output_aliases={0: 0},
        compiler_params=params(),
        cost_estimate=cost(0, 0),
        name="gate",
    )(value, *others)


def sds(shape, dtype):
    return jax.ShapeDtypeStruct(shape, dtype)


def far(items):
    return [(item, ANY) for item in items]


def params():
    return pltpu.CompilerParams(vmem_limit_bytes=64 * 1024 * 1024)


def cost(flops, size):
    return pl.CostEstimate(flops=int(flops), bytes_accessed=int(size), transcendentals=0)


def col_cuts(width, step):
    return [(slice(None), pl.ds(at, step)) for at in range(0, width, step)]


def row_cuts(height, step):
    return [(pl.ds(at, step), slice(None)) for at in range(0, height, step)]


def fetch(sec, layer, own, other, dst, sems, cuts, base=0):
    fetch_all(sec, layer, [(own, other, dst, cuts, base)], sems)


def fetch_all(sec, layer, items, sems):
    def go(side):
        for index in range(len(items[0][3])):
            for item in items:
                cut = item[3][index]
                pltpu.make_async_copy(
                    item[side].at[cut], item[2].at[cut], sems.at[item[4] + index]
                ).start()

    pl.when(sec == layer)(lambda: go(0))
    pl.when(sec != layer)(lambda: go(1))


def arrive(own, dst, sems, cuts, index, base=0):
    cut = cuts[index]
    pltpu.make_async_copy(own.at[cut], dst.at[cut], sems.at[base + index]).wait()


def depart(src, dst, sems, cuts, index, base=0):
    cut = cuts[index]
    pltpu.make_async_copy(src.at[cut], dst.at[cut], sems.at[base + index]).start()


def rms(values):
    return lax.rsqrt(jnp.mean(values * values, axis=-1, keepdims=True) + EPS)


def slot_rows(code_row, rows, capacity):
    target = jnp.where((code_row & (SLOTS - 1)) < capacity, code_row, -1)
    return (
        lax.broadcasted_iota(jnp.int32, (rows, code_row.shape[1]), 0) == target
    ).astype(F32).astype(BF)


def slot_cols(code_col, rows, capacity):
    target = jnp.where((code_col & (SLOTS - 1)) < capacity, code_col, -1)
    return (
        lax.broadcasted_iota(jnp.int32, (code_col.shape[0], rows), 1) == target
    ).astype(F32).astype(BF)


def project(normed, w_own, w_scr, sems, cuts, q_ref, kv_ref):
    step = q_ref.shape[1]
    for index in range(3):
        arrive(w_own, w_scr, sems, cuts, index)
        part = mm(normed, w_scr[:, index * step : (index + 1) * step]).astype(BF)
        if index == 0:
            q_ref[...] = part
        else:
            kv_ref[:, (index - 1) * step : index * step] = part


def fill_bias(vectors, out_ref, done=None):
    heads, rows, width = out_ref.shape
    lanes = vectors.shape[1]
    sub = lax.broadcasted_iota(jnp.int32, (8, lanes), 0)
    for head in range(heads):
        base = jnp.broadcast_to(vectors[head : head + 1, :], (8, lanes))
        for bit in (1, 2, 4):
            base = jnp.where((sub & bit) != 0, pltpu.roll(base, bit, 1), base)
        for block in range(rows // 8):
            moved = pltpu.roll(base, (8 * block - (rows - 1)) % lanes, 1)
            out_ref[head, 8 * block : 8 * block + 8, :] = moved[:, :width]
        if done is not None:
            done(head)


GAIN_M, ROUTER = 1, 2


def pack_kernel(
    place_ref,
    gain_a,
    gain_m,
    router,
    route,
    slot,
    table,
    tokens,
    cotangent,
    out_ref,
    code_ref,
    tok_ref,
    cot_ref,
):
    ctx = place_ref[1]
    experts = router.shape[0]
    rows = route.shape[2]
    out_ref[...] = jnp.zeros(out_ref.shape, F32)
    out_ref[0:1, :] = gain_a[...]
    out_ref[GAIN_M : GAIN_M + 1, :] = gain_m[...]
    out_ref[ROUTER : ROUTER + experts, :] = router[...]
    at = ROUTER + experts
    code = [(route[micro] * SLOTS + slot[micro]).astype(F32) for micro in range(2)]
    out_ref[at : at + 1, :rows] = code[0]
    out_ref[at + 1 : at + 2, :rows] = code[1]
    at += 2
    out_ref[at : at + table.shape[0], : table.shape[1]] = table[...]
    tok_ref[...] = jnp.where(ctx == 0, tokens[1], tokens[0])
    code_ref[...] = jnp.zeros(code_ref.shape, F32)
    code_ref[0:1, :rows] = jnp.where(ctx == 0, code[1], code[0])
    cot_ref[...] = jnp.where(ctx == 0, cotangent[1], cotangent[0])


def pack(place, gain_a, gain_m, router, route, slot, table, tokens, cotangent):
    rows, width = tokens.shape[1:]
    height = ROUTER + router.shape[0] + route.shape[0] + table.shape[0]
    return call(
        pack_kernel,
        "pack",
        cost(1e6, 2e6),
        [(place, SM), gain_a, gain_m, router, route, slot, table, tokens, cotangent],
        [sds((height, width), F32), sds((8, 256), F32)] + [sds((rows, width), BF)] * 2,
    )


def prepare_kernel(
    place_ref, buckets_ref, packs_ref, come_ref, up_hbm, onehot_ref, bias_hbm, vec_ref, *rest
):
    *outs, up_copy, bias_ref, bucket_scr, up_scr, leave, enter, moving = rest
    step = up_hbm.shape[0] // 4
    pieces = [pl.ds(index * step, step) for index in range(4)]
    for index, cut in enumerate(pieces):
        pltpu.make_async_copy(up_hbm.at[cut], up_scr.at[cut], enter.at[index]).start()
    sec, ctx = place_ref[0], place_ref[1]
    first = sec == 0
    experts = outs[2].shape[0]
    rows = outs[3].shape[1]
    heads = bias_ref.shape[0]
    bucket_count = onehot_ref.shape[0]
    bucket_scr[...] = jnp.full(bucket_scr.shape, -1, jnp.int32)
    bucket_scr[:, : buckets_ref.shape[1]] = buckets_ref[...]
    wide = bucket_scr[...]
    span = jnp.where(first, pltpu.roll(wide, wide.shape[1] - rows, 1), wide)[:, :SHIFT]
    lane = lax.broadcasted_iota(jnp.int32, span.shape, 1)
    span = jnp.where(lane < 3 * rows - 1, span, -1)
    onehot = lax.broadcasted_iota(jnp.int32, onehot_ref.shape, 0) == span
    onehot = jnp.where(onehot, 1.0, 0.0)
    onehot_ref[...] = onehot
    height = packs_ref.shape[0] // 2
    packs = packs_ref[:height], packs_ref[height:]
    at = ROUTER + experts + 2
    tables = [item[at : at + heads, :bucket_count] for item in packs]

    def copy(head):
        return pltpu.make_async_copy(bias_ref.at[head], bias_hbm.at[head], leave.at[head])


    def done(head):
        copy(head).start()
        if head % 2 == 0 and head // 2 < len(pieces):
            index = head // 2
            cut = pieces[index]
            pltpu.make_async_copy(up_hbm.at[cut], up_scr.at[cut], enter.at[index]).wait()
            pltpu.make_async_copy(up_scr.at[cut], up_copy.at[cut], moving.at[index]).start()

    fill_bias(mm(tables[0], onehot, NN, HIGH), bias_ref, done)
    vec_ref[...] = mm(tables[1], onehot, NN, HIGH)
    at = ROUTER + experts
    home = sec == ctx
    eye = lax.broadcasted_iota(jnp.int32, (rows, rows), 0) == lax.broadcasted_iota(
        jnp.int32, (rows, rows), 1
    )
    for layer in range(2):
        pair = packs[layer][at : at + 2, :rows]
        row = jnp.where(ctx == 0, pair[0:1], pair[1:2])
        row = jnp.where(home, row, come_ref[8 * layer : 8 * layer + 1, :rows])
        col = jnp.sum(jnp.where(eye, row, 0.0), axis=1, keepdims=True)
        for index, item in enumerate(
            (
                packs[layer][0:1],
                packs[layer][GAIN_M : GAIN_M + 1],
                packs[layer][ROUTER : ROUTER + experts],
                row.astype(jnp.int32),
                col.astype(jnp.int32),
            )
        ):
            outs[5 * layer + index][...] = item
    for head in range(heads):
        copy(head).wait()
    for index, cut in enumerate(pieces):
        pltpu.make_async_copy(up_scr.at[cut], up_copy.at[cut], moving.at[index]).wait()


def prepare(place, buckets, packs, come, up, sizes, rows, lanes, deps):
    experts, heads, bucket_count = sizes
    width = packs.shape[1]
    each = [
        sds((1, width), F32),
        sds((1, width), F32),
        sds((experts, width), F32),
        sds((1, rows), jnp.int32),
        sds((rows, 1), jnp.int32),
    ]
    return call(
        prepare_kernel,
        "prepare",
        cost(1e7, 4e6),
        [(place, SM), buckets, packs, come, (up, ANY)],
        [
            sds((bucket_count, SHIFT), F32),
            (sds((heads, rows, lanes), F32), ANY),
            sds((heads, SHIFT), F32),
            *each,
            *each,
            (sds(up.shape, BF), ANY),
        ],
        [
            pltpu.VMEM((heads, rows, lanes), F32),
            pltpu.VMEM((1, 2 * SHIFT), jnp.int32),
            pltpu.VMEM(up.shape, BF),
            pltpu.SemaphoreType.DMA((heads,)),
            pltpu.SemaphoreType.DMA((4,)),
            pltpu.SemaphoreType.DMA((4,)),
        ],
        deps,
    )


def bias_kernel(vec_ref, out_ref):
    fill_bias(vec_ref[...], out_ref)


def bias_table(vectors, rows, width, deps):
    return call(
        bias_kernel,
        "bias_table",
        cost(1e7, 4e6),
        [vectors],
        [sds((vectors.shape[0], rows, width), F32)],
        deps=deps,
    )[0]


def chosen_block(place_ref, both_ref, come_ref):
    sec, ctx = place_ref[0], place_ref[1]
    mine = jnp.where(ctx == 0, both_ref[0], both_ref[1])
    return jnp.where(sec == ctx, mine, come_ref[...])


def first_kernel(
    layer,
    place_ref,
    both_ref,
    come_ref,
    packs_ref,
    w_own,
    w_other,
    x_ref,
    normed_ref,
    q_ref,
    kv_ref,
    w_scr,
    sems,
):
    cuts = col_cuts(w_scr.shape[1], w_scr.shape[1] // 3)
    fetch(place_ref[0], layer, w_own, w_other, w_scr, sems, cuts)
    rounded = chosen_block(place_ref, both_ref, come_ref)
    x_ref[...] = rounded
    x = rounded.astype(F32)
    at = layer * (packs_ref.shape[0] // 2)
    normed = (x * rms(x) * packs_ref[at : at + 1]).astype(BF)
    normed_ref[...] = normed
    project(normed, w_own, w_scr, sems, cuts, q_ref, kv_ref)


def first_projection(layer, place, both, come, packs, w):
    rows, width = both.shape[1:]
    wide = w[0].shape[1]
    return call(
        functools.partial(first_kernel, layer),
        "first_projection",
        cost(2 * rows * width * wide, 2 * width * wide),
        [(place, SM), both, come, packs, *far(w)],
        [sds((rows, width), BF)] * 3 + [sds((rows, 2 * width), BF)],
        [pltpu.VMEM((width, wide), BF), pltpu.SemaphoreType.DMA((3,))],
    )


def attend_kernel(
    layer,
    capacity,
    sec_ref,
    x_ref,
    q_ref,
    kv_ref,
    gain_ref,
    router_ref,
    row_ref,
    bias_hbm,
    wo_own,
    wo_other,
    *rest,
):
    if layer == 0:
        move_hbm, mid_ref, probs_ref, att_ref, p_ref, out_ref, moved_hbm, *rest, moving = rest
        bias_scr, wo_scr, p_scr, sems, leave, move_scr = rest
        pltpu.make_async_copy(move_hbm, move_scr, moving.at[0]).start()
    else:
        mid_ref, probs_ref, att_ref, p_ref, out_ref, bias_scr, wo_scr, p_scr, sems, leave = rest

    sec = sec_ref[0]
    rows, width = x_ref.shape
    total = kv_ref.shape[0]
    pairs = width // PAIR
    for pair in range(pairs):
        pltpu.make_async_copy(
            bias_hbm.at[pl.ds(2 * pair, 2)], bias_scr.at[pl.ds(2 * pair, 2)], sems.at[pair]
        ).start()
    cuts = [(slice(None), slice(None))]
    fetch(sec, layer, wo_own, wo_other, wo_scr, sems, cuts, pairs)
    low = lax.broadcasted_iota(jnp.int32, (rows, PAIR), 1) < HEAD
    zero = jnp.zeros((rows, PAIR), BF)
    for pair in range(pairs):
        pltpu.make_async_copy(
            bias_hbm.at[pl.ds(2 * pair, 2)], bias_scr.at[pl.ds(2 * pair, 2)], sems.at[pair]
        ).wait()
    for pair in range(pairs):
        part = slice(pair * PAIR, (pair + 1) * PAIR)
        q = q_ref[:, part]
        k = kv_ref[:, part]
        v = kv_ref[:, width + pair * PAIR : width + (pair + 1) * PAIR]
        both = []
        for side in range(2):
            head = 2 * pair + side
            masked = jnp.where(low, q, zero) if side == 0 else jnp.where(low, zero, q)
            scores = mm(masked, k, NT) * 0.125 + bias_scr[head, :, :total]
            top = jnp.max(scores, axis=-1, keepdims=True)
            raised = jnp.exp(scores - top)
            share = (raised * (1.0 / jnp.sum(raised, axis=-1, keepdims=True))).astype(BF)
            p_scr[head] = share
            both.append(mm(share, v))
        att_ref[:, part] = jnp.where(low, both[0], both[1]).astype(BF)
    for pair in range(pairs):
        pltpu.make_async_copy(
            p_scr.at[pl.ds(2 * pair, 2)], p_ref.at[pl.ds(2 * pair, 2)], leave.at[pair]
        ).start()
    if layer == 0:
        pltpu.make_async_copy(move_hbm, move_scr, moving.at[0]).wait()
        pltpu.make_async_copy(move_scr, moved_hbm, moving.at[1]).start()
    arrive(wo_own, wo_scr, sems, cuts, 0, pairs)
    middle = x_ref[...].astype(F32) + mm(att_ref[...], wo_scr[...])
    mid_ref[...] = middle
    normed = middle * rms(middle) * gain_ref[...]
    logits = mm(normed, router_ref[...], NT, HIGH)
    raised = jnp.exp(logits - jnp.max(logits, axis=-1, keepdims=True))
    probs_ref[...] = raised / jnp.sum(raised, axis=-1, keepdims=True)
    slots = slot_rows(row_ref[...], out_ref.shape[0], capacity)
    out_ref[...] = mm(slots, normed.astype(BF)).astype(BF)
    for pair in range(pairs):
        pltpu.make_async_copy(
            p_scr.at[pl.ds(2 * pair, 2)], p_ref.at[pl.ds(2 * pair, 2)], leave.at[pair]
        ).wait()
    if layer == 0:
        pltpu.make_async_copy(move_scr, moved_hbm, moving.at[1]).wait()


def attend(layer, capacity, sec, x, q, kv, gain, router, code_row, bias, wo, move=()):
    rows, width = x.shape
    experts = router.shape[0]
    heads = width // HEAD
    wide = bias.shape[2]
    return call(
        functools.partial(attend_kernel, layer, capacity),
        "attend",
        cost(4e9, 6e6),
        [(sec, SM), x, q, kv, gain, router, code_row, (bias, ANY), *far(wo), *far(move)],
        [
            sds((rows, width), F32),
            sds((rows, experts), F32),
            sds((rows, width), BF),
            (sds((heads, rows, 2 * rows), BF), ANY),
            sds((experts * SLOTS, width), BF),
            *[(sds(item.shape, BF), ANY) for item in move],
        ],
        [
            pltpu.VMEM((heads, rows, wide), F32),
            pltpu.VMEM((width, width), BF),
            pltpu.VMEM((heads, rows, 2 * rows), BF),
            pltpu.SemaphoreType.DMA((heads // 2 + 1,)),
            pltpu.SemaphoreType.DMA((heads // 2,)),
            *[pltpu.VMEM(item.shape, BF) for item in move],
            *[pltpu.SemaphoreType.DMA((2,)) for item in move],
        ],
    )


def expert_kernel(
    layer,
    sec_ref,
    rec_ref,
    in_own,
    in_other,
    out_own,
    out_other,
    res_ref,
    act_hbm,
    slope_hbm,
    win,
    wout,
    act_ref,
    slope_ref,
    sems,
    leave,
):
    sec = sec_ref[0]
    hidden = win.shape[1]
    step = 512
    count = hidden // step
    in_cuts = col_cuts(hidden, step)
    out_cuts = row_cuts(hidden, step)
    items = [(in_own, in_other, win, in_cuts, 0), (out_own, out_other, wout, out_cuts, count)]
    fetch_all(sec, layer, items, sems)
    rec = rec_ref[...]
    total = None
    arrive(in_own, win, sems, in_cuts, 0)
    later = mm(rec, win[:, :step])
    for index in range(count):
        part = slice(index * step, (index + 1) * step)
        v = later
        if index + 1 < count:
            arrive(in_own, win, sems, in_cuts, index + 1)
        arrive(out_own, wout, sems, out_cuts, index, count)
        if index + 1 < count:
            later = mm(rec, win[:, (index + 1) * step : (index + 2) * step])
        square = v * v
        t = jnp.tanh(v * (0.7978845608028654 + 0.035677408136300125 * square))
        half = 0.5 * t + 0.5
        rising = v * half
        active = rising.astype(BF)
        act_ref[:, part] = active
        slope = half + (rising - rising * half) * (
            1.5957691216057308 + 0.21406444881780074 * square
        )
        slope_ref[:, part] = slope.astype(BF)
        fresh = mm(active, wout[part, :])
        total = fresh if total is None else total + fresh
        depart(act_ref, act_hbm, leave, in_cuts, index)
        depart(slope_ref, slope_hbm, leave, in_cuts, index, count)
    res_ref[...] = total.astype(BF)
    for index in range(count):
        arrive(act_ref, act_hbm, leave, in_cuts, index)
        arrive(slope_ref, slope_hbm, leave, in_cuts, index, count)


def expert_forward(layer, sec, received, w_in, w_out, deps=()):
    rows, width = received.shape
    hidden = w_in[0].shape[1]
    count = hidden // 512
    return call(
        functools.partial(expert_kernel, layer),
        "expert_forward",
        cost(4 * rows * width * hidden, 4 * width * hidden),
        [(sec, SM), received, *far(w_in), *far(w_out)],
        [sds((rows, width), BF)] + [(sds((rows, hidden), BF), ANY)] * 2,
        [
            pltpu.VMEM((width, hidden), BF),
            pltpu.VMEM((hidden, width), BF),
            pltpu.VMEM((rows, hidden), BF),
            pltpu.VMEM((rows, hidden), BF),
            pltpu.SemaphoreType.DMA((2 * count,)),
            pltpu.SemaphoreType.DMA((2 * count,)),
        ],
        deps,
    )


def gate_of(probs, code_col):
    lane = lax.broadcasted_iota(jnp.int32, probs.shape, 1)
    chosen = (lane == code_col // SLOTS).astype(F32)
    return chosen, jnp.sum(probs * chosen, axis=-1, keepdims=True)


def join_kernel(
    layer,
    capacity,
    sec_ref,
    mid_ref,
    ret_ref,
    probs_ref,
    col_ref,
    gain_ref,
    w_own,
    w_other,
    comb_ref,
    hid_ref,
    normed_ref,
    q_ref,
    kv_ref,
    w_scr,
    sems,
):
    cuts = col_cuts(w_scr.shape[1], w_scr.shape[1] // 3)
    fetch(sec_ref[0], layer, w_own, w_other, w_scr, sems, cuts)
    col = col_ref[...]
    combined = mm(slot_cols(col, ret_ref.shape[0], capacity), ret_ref[...])
    comb_ref[...] = combined.astype(BF)
    _, gate = gate_of(probs_ref[...], col)
    hidden = (mid_ref[...] + gate * combined).astype(BF)
    hid_ref[...] = hidden
    x = hidden.astype(F32)
    normed = (x * rms(x) * gain_ref[...]).astype(BF)
    normed_ref[...] = normed
    project(normed, w_own, w_scr, sems, cuts, q_ref, kv_ref)


def join(layer, capacity, sec, middle, returned, probs, code_col, gain, w):
    rows, width = middle.shape
    wide = w[0].shape[1]
    return call(
        functools.partial(join_kernel, layer, capacity),
        "join",
        cost(2 * rows * width * wide, 2 * width * wide),
        [(sec, SM), middle, returned, probs, code_col, gain, *far(w)],
        [sds((rows, width), BF)] * 4 + [sds((rows, 2 * width), BF)],
        [pltpu.VMEM((width, wide), BF), pltpu.SemaphoreType.DMA((3,))],
    )


def pack_rows(ref, base, values):
    height, width = values.shape
    for row in range(height):
        for at in range(width // 128):
            place = base + row * (width // 128) + at
            ref[place : place + 1, :] = values[row : row + 1, at * 128 : (at + 1) * 128]


def send_back(g, combined, probs, row, col, rows, capacity):
    _, gate = gate_of(probs, col)
    gate_grad = jnp.sum(g * combined, axis=-1, keepdims=True)
    placed = mm(slot_rows(row, rows, capacity), (gate * g).astype(BF))
    return gate_grad, placed.astype(BF)


def turn_kernel(
    capacity,
    place_ref,
    mid_ref,
    ret_ref,
    probs_ref,
    row_ref,
    col_ref,
    both_ref,
    come_ref,
    hid_ref,
    g_ref,
    gate_grad_ref,
    out_ref,
):
    g = chosen_block(place_ref, both_ref, come_ref)
    g_ref[...] = g
    col = col_ref[...]
    probs = probs_ref[...]
    combined = mm(slot_cols(col, ret_ref.shape[0], capacity), ret_ref[...])
    _, gate = gate_of(probs, col)
    hid_ref[...] = (mid_ref[...] + gate * combined).astype(BF)
    gate_grad_ref[...], out_ref[...] = send_back(
        g.astype(F32), combined, probs, row_ref[...], col, out_ref.shape[0], capacity
    )


def turn(capacity, place, middle, returned, probs, code_row, code_col, both, come):
    rows, width = middle.shape
    return call(
        functools.partial(turn_kernel, capacity),
        "turn",
        cost(4 * rows * width * returned.shape[0], 3e6),
        [(place, SM), middle, returned, probs, code_row, code_col, both, come],
        [
            sds((rows, width), BF),
            sds((rows, width), BF),
            sds((rows, 1), F32),
            sds(returned.shape, BF),
        ],
    )


def expert_back_kernel(
    layer,
    sec_ref,
    rec_ref,
    slope_hbm,
    in_own,
    in_other,
    out_own,
    out_other,
    sent_ref,
    grad_hbm,
    win,
    wout,
    slope_ref,
    grad_ref,
    sems,
    leave,
):
    sec = sec_ref[0]
    hidden = win.shape[1]
    step = 512
    count = hidden // step
    in_cuts = col_cuts(hidden, step)
    out_cuts = row_cuts(hidden, step)
    items = [(out_own, out_other, wout, out_cuts, count), (in_own, in_other, win, in_cuts, 0)]
    for index in range(count):
        depart(slope_hbm, slope_ref, sems, in_cuts, index, 2 * count)
    fetch_all(sec, layer, items, sems)
    rec = rec_ref[...]
    total = None
    arrive(out_own, wout, sems, out_cuts, 0, count)
    later = mm(rec, wout[:step, :], NT)
    for index in range(count):
        part = slice(index * step, (index + 1) * step)
        now = later
        if index + 1 < count:
            arrive(out_own, wout, sems, out_cuts, index + 1, count)
        arrive(slope_hbm, slope_ref, sems, in_cuts, index, 2 * count)
        arrive(in_own, win, sems, in_cuts, index)
        if index + 1 < count:
            later = mm(rec, wout[(index + 1) * step : (index + 2) * step, :], NT)
        inner = (now * slope_ref[:, part].astype(F32)).astype(BF)
        grad_ref[:, part] = inner
        fresh = mm(inner, win[:, part], NT)
        total = fresh if total is None else total + fresh
        depart(grad_ref, grad_hbm, leave, in_cuts, index)
    sent_ref[...] = total.astype(BF)
    for index in range(count):
        arrive(grad_ref, grad_hbm, leave, in_cuts, index)


def expert_backward(layer, sec, received, slope, w_in, w_out, deps=()):
    rows, width = received.shape
    hidden = w_in[0].shape[1]
    count = hidden // 512
    return call(
        functools.partial(expert_back_kernel, layer),
        "expert_backward",
        cost(4 * rows * width * hidden, 4 * width * hidden),
        [(sec, SM), received, (slope, ANY), *far(w_in), *far(w_out)],
        [sds((rows, width), BF), (sds((rows, hidden), BF), ANY)],
        [
            pltpu.VMEM((width, hidden), BF),
            pltpu.VMEM((hidden, width), BF),
            pltpu.VMEM((rows, hidden), BF),
            pltpu.VMEM((rows, hidden), BF),
            pltpu.SemaphoreType.DMA((3 * count,)),
            pltpu.SemaphoreType.DMA((count,)),
        ],
        deps,
    )


def expert_weight_kernel(half_ref, *refs):
    rec, grad, act, res, rec_b, grad_b, act_b, res_b, out_ref, turned = refs
    rows, half = rec.shape

    @pl.when(pl.program_id(0) == 0)
    def _():
        turned[:, :rows] = rec[...].T
        turned[:, rows:] = rec_b[...].T

    upper = mm(turned[:, :rows], grad[...]) + mm(turned[:, rows:], grad_b[...])
    out_ref[0, :half] = upper.astype(BF)
    lower = mm(act[...], res[...], TN) + mm(act_b[...], res_b[...], TN)
    out_ref[0, half : 2 * half] = lower.astype(BF)


def expert_weights(half, blocks, own, other):
    rows, width = own[0].shape
    hidden = own[1].shape[1]
    step = hidden // blocks
    cut = width // 2
    narrow = pl.BlockSpec((rows, cut), lambda b, half_ref: (0, half_ref[0]))
    moving = pl.BlockSpec((rows, step), lambda b, half_ref: (0, b))
    return pl.pallas_call(
        expert_weight_kernel,
        out_shape=sds((blocks, width, step), BF),
        grid_spec=pltpu.PrefetchScalarGridSpec(
            num_scalar_prefetch=1,
            grid=(blocks,),
            in_specs=[narrow, moving, moving, narrow] * 2,
            out_specs=pl.BlockSpec((1, width, step), lambda b, half_ref: (b, 0, 0)),
            scratch_shapes=[pltpu.VMEM((cut, 2 * rows), BF)],
        ),
        compiler_params=params(),
        cost_estimate=cost(4 * rows * width * hidden, 4 * width * hidden),
        name="expert_weights",
    )(half, *own, *other)


def attend_back_kernel(
    layer,
    capacity,
    sec_ref,
    g_ref,
    mid_ref,
    sent_ref,
    col_ref,
    probs_ref,
    gate_grad_ref,
    gain_ref,
    router_ref,
    q_ref,
    kv_ref,
    onehot_ref,
    p_hbm,
    wo_own,
    wo_other,
    mid_grad_ref,
    branch_ref,
    dq_ref,
    own_ref,
    other_ref,
    small_ref,
    dkv_scr,
    diag_scr,
    p_scr,
    wo_scr,
    sems,
):
    sec = sec_ref[0]
    rows, width = mid_ref.shape
    total = kv_ref.shape[0]
    pairs = width // PAIR
    lanes = diag_scr.shape[1]
    cuts = [(slice(None), slice(None))]
    fetch(sec, layer, wo_own, wo_other, wo_scr, sems, cuts, pairs)
    for pair in range(pairs):
        pltpu.make_async_copy(
            p_hbm.at[pl.ds(2 * pair, 2)], p_scr.at[pl.ds(2 * pair, 2)], sems.at[pair]
        ).start()

    middle = mid_ref[...]
    scale = rms(middle)
    unit = middle * scale
    gain = gain_ref[...]
    col = col_ref[...]
    probs = probs_ref[...]
    chosen, gate = gate_of(probs, col)
    logit_grad = probs * (chosen - gate) * gate_grad_ref[...]
    normed_grad = mm(slot_cols(col, sent_ref.shape[0], capacity), sent_ref[...])
    normed_grad = normed_grad + mm(logit_grad, router_ref[...], NN, HIGH)
    experts = probs.shape[1]
    router_grad = mm(logit_grad, unit * gain, TN, HIGH)
    gain_grad = jnp.sum(normed_grad * unit, axis=0, keepdims=True)
    pack_rows(small_ref, 0, router_grad)
    pack_rows(small_ref, experts * (width // 128), gain_grad)
    unit_grad = normed_grad * gain
    middle_grad = g_ref[...].astype(F32) + scale * (
        unit_grad - unit * jnp.mean(unit_grad * unit, axis=-1, keepdims=True)
    )
    mid_grad_ref[...] = middle_grad
    branch = middle_grad.astype(BF)
    branch_ref[...] = branch
    arrive(wo_own, wo_scr, sems, cuts, 0, pairs)
    att_grad = mm(branch, wo_scr[...], NT).astype(BF)

    low = lax.broadcasted_iota(jnp.int32, (rows, PAIR), 1) < HEAD
    low_wide = lax.broadcasted_iota(jnp.int32, (total, PAIR), 1) < HEAD
    zero = jnp.zeros((rows, PAIR), BF)
    pad = jnp.zeros((rows, lanes - total), F32)
    sub = lax.broadcasted_iota(jnp.int32, (8, lanes), 0)
    for pair in range(pairs):
        pltpu.make_async_copy(
            p_hbm.at[pl.ds(2 * pair, 2)], p_scr.at[pl.ds(2 * pair, 2)], sems.at[pair]
        ).wait()
    for pair in range(pairs):
        part = slice(pair * PAIR, (pair + 1) * PAIR)
        later = slice(width + pair * PAIR, width + (pair + 1) * PAIR)
        q = q_ref[:, part]
        k = kv_ref[:, part]
        v = kv_ref[:, later]
        da = att_grad[:, part]
        dqs, dks, dvs = [], [], []
        for side in range(2):
            head = 2 * pair + side
            masked = jnp.where(low, da, zero) if side == 0 else jnp.where(low, zero, da)
            share = p_scr[head]
            wide = share.astype(F32)
            dp = mm(masked, v, NT)
            ds = wide * (dp - jnp.sum(wide * dp, axis=-1, keepdims=True))
            dsb = ds.astype(BF)
            dqs.append(mm(dsb, k))
            dks.append(mm(dsb, q, TN))
            dvs.append(mm(share, da, TN))
            padded = jnp.concatenate([ds, pad], axis=1)
            fold = None
            for block in range(rows // 8):
                moved = pltpu.roll(
                    padded[8 * block : 8 * block + 8], (rows - 1 - 8 * block) % lanes, 1
                )
                fold = moved if fold is None else fold + moved
            for bit in (1, 2, 4):
                fold = jnp.where((sub & bit) != 0, pltpu.roll(fold, lanes - bit, 1), fold)
            diag_scr[head : head + 1, :] = jnp.sum(fold, axis=0, keepdims=True)
        dq_ref[:, part] = (jnp.where(low, dqs[0], dqs[1]) * 0.125).astype(BF)
        dkv_scr[:, part] = (jnp.where(low_wide, dks[0], dks[1]) * 0.125).astype(BF)
        dkv_scr[:, later] = jnp.where(low_wide, dvs[0], dvs[1]).astype(BF)
    table = mm(diag_scr[...], onehot_ref[...], NT, HIGH)
    buckets = onehot_ref.shape[0]
    base = (experts + 1) * (width // 128)
    for head in range(2 * pairs):
        at = head * buckets
        small_ref[base + at // 128 : base + at // 128 + 1, at % 128 : at % 128 + buckets] = table[
            head : head + 1, :
        ]
    own_ref[...] = dkv_scr[pl.ds(pl.multiple_of(sec * rows, rows), rows), :]
    other_ref[...] = dkv_scr[pl.ds(pl.multiple_of((1 - sec) * rows, rows), rows), :]


def attend_backward(
    layer,
    capacity,
    sec,
    g,
    middle,
    sent,
    code_col,
    probs,
    gate_grad,
    gain,
    router,
    q,
    kv,
    onehot,
    shares,
    wo,
    deps,
):
    rows, width = middle.shape
    heads = width // HEAD
    experts = router.shape[0]
    packed = (experts + 1) * (width // 128) + heads * onehot.shape[0] // 128
    return call(
        functools.partial(attend_back_kernel, layer, capacity),
        "attend_backward",
        cost(8e9, 6e6),
        [
            (sec, SM),
            g,
            middle,
            sent,
            code_col,
            probs,
            gate_grad,
            gain,
            router,
            q,
            kv,
            onehot,
            (shares, ANY),
            *far(wo),
        ],
        [
            sds((rows, width), F32),
            sds((rows, width), BF),
            sds((rows, width), BF),
            sds((rows, 2 * width), BF),
            sds((rows, 2 * width), BF),
            sds((packed, 128), F32),
        ],
        [
            pltpu.VMEM((2 * rows, 2 * width), BF),
            pltpu.VMEM((heads, SHIFT), F32),
            pltpu.VMEM((heads, rows, 2 * rows), BF),
            pltpu.VMEM((width, width), BF),
            pltpu.SemaphoreType.DMA((heads // 2 + 1,)),
        ],
        deps,
    )


def project_back_kernel(
    layer,
    last,
    capacity,
    sec_ref,
    dq_ref,
    own_ref,
    come_ref,
    mid_grad_ref,
    x_ref,
    gain_ref,
    small_in_ref,
    *rest,
):
    if last:
        late_ref, w_own, w_other, rows_ref, grad_ref, mine_ref, small_ref, w_scr, sems = rest
    else:
        comb_ref, probs_ref, row_ref, col_ref, w_own, w_other = rest[:6]
        rows_ref, grad_ref, small_ref, gate_grad_ref, out_ref, w_scr, sems = rest[6:]
    width = x_ref.shape[1]
    cuts = col_cuts(w_scr.shape[1], width)
    fetch(sec_ref[0], layer, w_own, w_other, w_scr, sems, cuts)
    rows_ref[:, :width] = dq_ref[...]
    rows_ref[:, width:] = (own_ref[...].astype(F32) + come_ref[...].astype(F32)).astype(BF)
    normed_grad = None
    for index in range(3):
        part = slice(index * width, (index + 1) * width)
        arrive(w_own, w_scr, sems, cuts, index)
        fresh = mm(rows_ref[:, part], w_scr[:, part], NT)
        normed_grad = fresh if normed_grad is None else normed_grad + fresh
    x = x_ref[...].astype(F32)
    scale = rms(x)
    unit = x * scale
    held = small_in_ref.shape[0]
    small_ref[:held, :] = small_in_ref[...]
    pack_rows(small_ref, held, jnp.sum(normed_grad * unit, axis=0, keepdims=True))
    held += width // 128
    small_ref[held:, :] = jnp.zeros((small_ref.shape[0] - held, 128), F32)
    if last:
        first = sec_ref[0] == 0
        early, late = small_ref[...], late_ref[...]
        mine_ref[...] = jnp.where(first, early, late)
        small_ref[...] = jnp.where(first, late, early)
    unit_grad = normed_grad * gain_ref[...]
    grad = mid_grad_ref[...] + scale * (
        unit_grad - unit * jnp.mean(unit_grad * unit, axis=-1, keepdims=True)
    )
    rounded = grad.astype(BF)
    grad_ref[...] = rounded
    if not last:
        gate_grad_ref[...], out_ref[...] = send_back(
            rounded.astype(F32),
            comb_ref[...].astype(F32),
            probs_ref[...],
            row_ref[...],
            col_ref[...],
            out_ref.shape[0],
            capacity,
        )


def project_backward(
    layer, capacity, sec, dq, own, come, middle_grad, x, gain, small, w, before
):
    rows, width = x.shape
    wide = w[0].shape[1]
    last = len(before) == 1
    packed = sds((-(-(small.shape[0] + width // 128) // 8) * 8, 128), F32)
    outs = [sds((rows, wide), BF), sds((rows, width), BF), packed]
    more = list(before)
    if last:
        outs += [packed]
    else:
        outs += [sds((rows, 1), F32), sds((before[1].shape[1] * SLOTS, width), BF)]
    return call(
        functools.partial(project_back_kernel, layer, last, capacity),
        "project_backward",
        cost(2 * rows * width * wide, 2 * width * wide),
        [(sec, SM), dq, own, come, middle_grad, x, gain, small, *more, *far(w)],
        outs,
        [pltpu.VMEM((width, wide), BF), pltpu.SemaphoreType.DMA((3,))],
    )


def spread_kernel(order, place_ref, *refs):
    own, other, out_ref = refs[:2], refs[2:4], refs[4]
    width = own[0].shape[1]
    lanes = out_ref.shape[1]
    normed = jnp.concatenate([own[0][...], other[0][...]], axis=0)
    attended = jnp.concatenate([own[1][...], other[1][...]], axis=0)
    mixed = jnp.where(place_ref[0] == 0, normed, attended)
    feature = lax.broadcasted_iota(jnp.int32, (lanes, width), 1)
    lane = lax.broadcasted_iota(jnp.int32, (lanes, 1), 0)
    block, place = lane // 16, lane % 16
    if order is not None:
        experts, copies = order
        rest = lanes // 16 // COLUMN
        column, place_in = block // rest, block % rest
        lines = experts // COLUMN
        line = place_in // copies % lines * COLUMN + column
        block = place_in // (lines * copies) * experts * copies + line * copies + place_in % copies
    base = block * 12
    main = jnp.where(place < 12, base + place, -1)
    late = [jnp.where(place < 12, -1, base + 4 * group + place - 12) for group in range(3)]
    for index, (values, source) in enumerate(
        [(normed, main), (mixed, main), (mixed, late[0]), (mixed, late[1]), (mixed, late[2])]
    ):
        hit = jnp.where(feature == source, 1.0, 0.0).astype(BF)
        out_ref[index] = mm(hit, values, NT).astype(BF)


def spread_features(place, shards, own, other, order=None):
    rows = own[0].shape[0]
    return call(
        functools.partial(spread_kernel, order),
        "spread_features",
        cost(3e9, 4e6),
        [(place, SM), *own, *other],
        [sds((5, shards * 16, 2 * rows), BF)],
    )[0]


def projection_weight_kernel(place_ref, left_hbm, *refs):
    own, other = refs[:2], refs[2:4]
    out_hbm, left, out_ref, sems, leave = refs[-5:]
    step = out_ref.shape[1] // 3
    first = place_ref[0] == 0
    for index in range(5):
        pltpu.make_async_copy(left_hbm.at[index], left.at[index], sems.at[index]).start()

    def columns(group):
        late = 4 + group
        parts = []
        for rows_ref, branch_ref in (own, other):
            upper = rows_ref[:, group * step : (group + 1) * step]
            if late < 6:
                lower = rows_ref[:, late * step : (late + 1) * step]
            else:
                lower = branch_ref[:, (late - 6) * step : (late - 5) * step]
            parts.append(jnp.where(first, upper, lower))
        return jnp.concatenate(parts, axis=0)

    def copy(group):
        return pltpu.make_async_copy(
            out_ref.at[:, pl.ds(group * step, step)],
            out_hbm.at[:, pl.ds(group * step, step)],
            leave.at[group],
        )

    for index in range(5):
        pltpu.make_async_copy(left_hbm.at[index], left.at[index], sems.at[index]).wait()
    tail = columns(3)
    for group in range(3):
        total = mm(left[0 if group < 2 else 1], columns(group)) + mm(left[2 + group], tail)
        out_ref[:, group * step : (group + 1) * step] = total.astype(BF)
        copy(group).start()
    for group in range(3):
        copy(group).wait()


def projection_weights(place, left, own, other, spare, deps=()):
    wide = (own[0].shape[1] + own[1].shape[1]) // 8 * 3
    height = left.shape[1]
    return call(
        projection_weight_kernel,
        "projection_weights",
        cost(2e9, 8e6),
        [(place, SM), (left, ANY), *own, *other],
        [(sds((height, wide + spare), BF), ANY)],
        [
            pltpu.VMEM(left.shape, BF),
            pltpu.VMEM((height, wide), BF),
            pltpu.SemaphoreType.DMA((5,)),
            pltpu.SemaphoreType.DMA((3,)),
        ],
        deps,
    )[0]


def ride_kernel(shares_ref, held_hbm, out_hbm, scr, sem):
    shards = shares_ref.shape[0]
    total = jnp.sum(shares_ref[...], axis=0)
    high = total.astype(BF).astype(F32)
    row = lax.broadcasted_iota(jnp.int32, scr.shape, 0) % 16
    tile = jnp.where(row == 0, high, jnp.where(row == 1, total - high, 0.0))
    scr[...] = tile.astype(BF)
    at = out_hbm.shape[1] - 128
    copy = pltpu.make_async_copy(scr, out_hbm.at[:, pl.ds(at, 128)], sem.at[0])
    copy.start()
    copy.wait()


def ride(shares, held):
    return call(
        ride_kernel,
        "ride",
        cost(1e6, 1e6),
        [shares, (held, ANY)],
        [(sds(held.shape, BF), ANY)],
        [pltpu.VMEM((held.shape[0], 128), BF), pltpu.SemaphoreType.DMA((1,))],
        aliases={1: 0},
    )[0]


def unpack_rows(total):
    width = total.shape[1]
    left = total[12:].reshape(4, 3, width // 3).transpose(1, 0, 2).reshape(12, width // 3)
    return jnp.concatenate([total[:12], left], axis=1)


def body(
    tokens,
    cotangent,
    expert_route,
    capacity_slot,
    buckets,
    qkv_weight,
    attention_out,
    relative_bias,
    attention_gain,
    mixture_gain,
    router,
    expert_in,
    expert_out,
):
    sec = lax.axis_index("section")
    ctx = lax.axis_index("context")
    place = jnp.stack([sec, ctx]).astype(jnp.int32)
    rows, width = tokens.shape[2:]
    experts = router.shape[2]
    heads = width // HEAD
    bucket_count = relative_bias.shape[1]
    capacity = (5 * rows + 4 * experts - 1) // (4 * experts)
    local = ("context", "dp")
    section = ("context", "expert", "dp")
    blocks = lax.axis_size(local)
    contexts = lax.axis_size("context")
    shards = lax.axis_size(section)
    grid = ("section", "context")

    def swap(value):
        return lax.ppermute(value, "section", SWAP)

    def pick(values, at):
        return jnp.where(at == 0, values[0], values[1])

    def come_over(value):
        return lax.ppermute(value, grid, [(0, 1), (3, 2)])

    def exchange(value):
        spread = value.reshape(experts, SLOTS, width)
        return lax.all_to_all(spread, "expert", 0, 0, tiled=True).reshape(value.shape)

    def shared(value):
        return lax.all_to_all(value, section, 0, 0, tiled=True)

    def together(value):
        return lax.all_gather(value, "section", axis=0, tiled=True)

    def both(value):
        return (value, swap(value))

    own, code_leave, tok_leave, cot_leave = pack(
        place,
        attention_gain,
        mixture_gain,
        router[0].T,
        expert_route[0],
        capacity_slot[0],
        relative_bias[0].T,
        tokens[:, 0],
        cotangent[:, 0],
    )
    tok_come = come_over(tok_leave)
    packs = together(gate(own, tok_come))
    codes_come = together(lax.ppermute(code_leave, "context", SWAP))
    w_qkv = both(qkv_weight[0])
    w_out = both(attention_out[0])
    cot_come = come_over(cot_leave)

    x, normed, q, kv, middle, probs, attended, shares = ([None] * 2 for _ in range(8))
    received, active, slope, hidden, left = ([None, None] for _ in range(5))
    x[0], normed[0], q[0], kv[0] = first_projection(
        0, place, tokens[:, 0], tok_come, packs, w_qkv
    )
    for layer in range(2):
        kv[layer] = together(kv[layer])
        if layer == 0:
            prepared = prepare(
                place,
                buckets.reshape(1, -1),
                packs,
                codes_come,
                expert_in[0, 0],
                (experts, heads, bucket_count),
                rows,
                384,
                [kv[0], w_out[1]],
            )
            onehot, bias0, vectors = prepared[:3]
            gain_a, gain_m, routers, code_rows, code_cols = zip(prepared[3:8], prepared[8:13])
            bias = [bias0, None]
            w_up = both(prepared[13])
        middle[layer], probs[layer], attended[layer], shares[layer], outgoing, *moved = attend(
            layer,
            capacity,
            place,
            x[layer],
            q[layer],
            kv[layer],
            gain_m[layer],
            routers[layer],
            code_rows[layer],
            bias[layer],
            w_out,
            () if layer else (expert_out[0, 0],),
        )
        if layer == 0:
            w_down = both(moved[0])
        received[layer] = exchange(outgoing)
        pair = (normed[layer], attended[layer])
        order = (experts, lax.axis_size("dp")) if layer else None
        left[layer] = spread_features(place, shards, pair, [swap(item) for item in pair], order)
        deps = [left[0]]
        if layer == 0:
            bias[1] = bias_table(vectors, rows, 384, [outgoing])
            deps = [bias[1]]
        result, active[layer], slope[layer] = expert_forward(
            layer, place, received[layer], w_up, w_down, deps
        )
        returned = exchange(result)
        if layer == 0:
            combined, hidden[0], normed[1], q[1], kv[1] = join(
                1, capacity, place, middle[0], returned, probs[0], code_cols[0], gain_a[1], w_qkv
            )
            x[1] = hidden[0]
        else:
            hidden[1], g, gate_grad, outgoing = turn(
                capacity,
                place,
                middle[1],
                returned,
                probs[1],
                code_rows[1],
                code_cols[1],
                cotangent[:, 0],
                cot_come,
            )

    def spread_out(values):
        one = lax.ppermute(pick(values, ctx), grid, [(0, 0), (1, 2), (2, 1), (3, 3)])
        two = lax.ppermute(pick(values, 1 - ctx), grid, [(0, 2), (1, 0), (2, 3), (3, 1)])
        return one, two

    def side_by_side(one, two):
        return jnp.stack([jnp.where(sec == 0, one, two), jnp.where(sec == 0, two, one)])

    hidden_states = side_by_side(*spread_out(hidden))

    grads, expert_sums, small = ([None, None] for _ in range(3))
    held = None
    for layer in (1, 0):
        result_grad = exchange(outgoing)
        deps = [left[1]] if layer else [held]
        sent, inner_grad = expert_backward(
            layer, place, result_grad, slope[layer], w_up, w_down, deps
        )
        operands = (received[layer], inner_grad, active[layer], result_grad)
        half = expert_weights(place, blocks, operands, [swap(item) for item in operands])
        sent = exchange(sent)
        half = gate(half, sent)
        expert_sums[layer] = lax.psum_scatter(
            half.reshape(-1, half.shape[2]), local, scatter_dimension=0, tiled=True
        )
        if layer == 0:
            late = gate(held, half).reshape(COLUMN, -1, held.shape[1])
            lines = [list(range(at, at + COLUMN)) for at in range(0, experts, COLUMN)]
            late = lax.all_to_all(late, "expert", 0, 0, axis_index_groups=lines, tiled=True)
        middle_grad, branch, dq, own, other, packed = attend_backward(
            layer,
            capacity,
            place,
            g,
            middle[layer],
            sent,
            code_cols[layer],
            probs[layer],
            gate_grad,
            gain_m[layer],
            routers[layer],
            q[layer],
            kv[layer],
            onehot,
            shares[layer],
            w_out,
            [half],
        )
        before = (combined, probs[0], code_rows[0], code_cols[0]) if layer == 1 else (small[1],)
        back = project_backward(
            layer,
            capacity,
            place,
            dq,
            own,
            swap(other),
            middle_grad,
            x[layer],
            gain_a[layer],
            packed,
            w_qkv,
            before,
        )
        rows_grad, grads[layer], small[layer] = back[:3]
        if layer == 1:
            g, gate_grad, outgoing = grads[1], back[3], back[4]
        operands = (rows_grad, branch)
        swapped = [swap(item) for item in operands]
        if layer == 1:
            held = projection_weights(place, left[1], operands, swapped, 0)
        else:
            late = jnp.sum(late.astype(F32), axis=0).astype(BF)
            held = projection_weights(place, left[0], operands, swapped, 128, [late])

    mine = small[0] + swap(back[3])
    tail = ride(shared(mine.reshape(shards, 1, 128)), held).reshape(shards, 16, -1)
    tail = shared(tail)
    whole_e = (pick(expert_sums, sec), swap(pick(expert_sums, 1 - sec)))
    first, second = pick(whole_e, sec), pick(whole_e, 1 - sec)
    mid = width // 2
    in_grad = jnp.concatenate([first[:mid], second[:mid]], axis=0).astype(F32)
    out_grad = jnp.concatenate([first[mid:], second[mid:]], axis=1).astype(F32)

    late = gate(late, tail).reshape(shards // COLUMN, 16, -1)
    copies = lax.axis_size("dp")
    planes = [
        [at for at in range(shards) if at // copies % COLUMN == column] for column in range(COLUMN)
    ]
    late = lax.all_to_all(late, section, 0, 0, axis_index_groups=planes, tiled=True)
    late = jnp.sum(late.astype(F32), axis=0)
    wide = tail.shape[2] - 128
    mine = jnp.sum(tail[:, 0:2, wide:].astype(F32), axis=1)
    flat = mine.reshape(-1)
    count = experts * width
    router_grad = flat[:count].reshape(experts, width).T
    mixture_gain_grad = flat[count : count + width]
    count += width
    relative_grad = flat[count : count + heads * bucket_count].reshape(heads, bucket_count).T
    count += heads * bucket_count
    attention_gain_grad = flat[count : count + width]

    total = jnp.sum(tail[:, :, :wide].astype(F32), axis=0)
    projections = [unpack_rows(total), unpack_rows(late)]
    whole = (pick(projections, sec), swap(pick(projections, 1 - sec)))
    whole = jnp.concatenate([pick(whole, sec), pick(whole, 1 - sec)], axis=1)
    cut = qkv_weight.shape[2]

    input_grads = side_by_side(*spread_out(grads)).astype(F32)
    return (
        hidden_states[None, :, None],
        input_grads[None, :, None],
        whole[None, :, :cut],
        whole[None, :, cut:],
        relative_grad[None],
        attention_gain_grad[None],
        mixture_gain_grad[None],
        router_grad[None],
        in_grad[None, None],
        out_grad[None, None],
    )


def solution(mesh):
    return jax.shard_map(
        body,
        mesh=mesh,
        in_specs=(
            P(None, ("expert", "dp"), "context", None),
            P(None, ("expert", "dp"), "context", None),
            P("section", None, ("expert", "dp"), "context"),
            P("section", None, ("expert", "dp"), "context"),
            P(),
            P("section", None, None),
            P("section", None, None),
            P("section", None, None),
            P("section", None),
            P("section", None),
            P("section", None, None),
            P("section", "expert", None, None),
            P("section", "expert", None, None),
        ),
        out_specs=(
            P("section", None, ("expert", "dp"), "context", None),
            P("section", None, ("expert", "dp"), "context", None),
            P("section", ("context", "expert", "dp"), None),
            P("section", ("context", "expert", "dp"), None),
            P("section", None, None),
            P("section", None),
            P("section", None),
            P("section", None, None),
            P("section", "expert", None, ("context", "dp")),
            P("section", "expert", ("context", "dp"), None),
        ),
        check_vma=False,
    )
```

```python
import functools

import jax
import jax.numpy as jnp
from jax import lax
from jax.experimental import pallas as pl
from jax.experimental.pallas import tpu as pltpu
from jax.sharding import PartitionSpec as P

BF = jnp.bfloat16
F32 = jnp.float32
HIGH = lax.Precision.HIGHEST
EPS = 1e-06
HEAD = 64
PAIR = 2 * HEAD
SLOTS = 32
SHIFT = 512
COLUMN = 4
SWAP = [(0, 1), (1, 0)]
NN = (((1,), (0,)), ((), ()))
NT = (((1,), (1,)), ((), ()))
TN = (((0,), (0,)), ((), ()))


def mm(a, b, dims=NN, precision=None):
    return lax.dot_general(a, b, dims, precision=precision, preferred_element_type=F32)


SM = pl.BlockSpec(memory_space=pltpu.SMEM)
ANY = pl.BlockSpec(memory_space=pl.ANY)


def call(kernel, name, estimate, operands, outs, scratch=(), deps=(), aliases={}):
    def whole(item):
        if isinstance(item, tuple):
            return item
        rank = len(item.shape)
        return item, pl.BlockSpec(item.shape, lambda step: (0,) * rank)

    operands = [whole(item) for item in operands]
    outs = [whole(item) for item in outs]
    count = len(operands)
    operands += [(item, ANY) for item in deps]

    def inner(*refs):
        kernel(*refs[:count], *refs[count + len(deps) :])

    return pl.pallas_call(
        inner,
        out_shape=tuple(item for item, _ in outs),
        grid=(1,),
        in_specs=[spec for _, spec in operands],
        out_specs=tuple(spec for _, spec in outs),
        scratch_shapes=list(scratch),
        compiler_params=params(),
        cost_estimate=estimate,
        input_output_aliases=aliases,
        name=name,
    )(*[item for item, _ in operands])


def gate(value, *others):
    def kernel(*refs):
        pass

    return pl.pallas_call(
        kernel,
        out_shape=sds(value.shape, value.dtype),
        in_specs=[ANY] * (1 + len(others)),
        out_specs=ANY,
        input_output_aliases={0: 0},
        compiler_params=params(),
        cost_estimate=cost(0, 0),
        name="gate",
    )(value, *others)


def sds(shape, dtype):
    return jax.ShapeDtypeStruct(shape, dtype)


def far(items):
    return [(item, ANY) for item in items]


def params():
    return pltpu.CompilerParams(vmem_limit_bytes=64 * 1024 * 1024)


def cost(flops, size):
    return pl.CostEstimate(flops=int(flops), bytes_accessed=int(size), transcendentals=0)


def col_cuts(width, step):
    return [(slice(None), pl.ds(at, step)) for at in range(0, width, step)]


def row_cuts(height, step):
    return [(pl.ds(at, step), slice(None)) for at in range(0, height, step)]


def fetch(sec, layer, own, other, dst, sems, cuts, base=0):
    fetch_all(sec, layer, [(own, other, dst, cuts, base)], sems)


def fetch_all(sec, layer, items, sems):
    def go(side):
        for index in range(len(items[0][3])):
            for item in items:
                cut = item[3][index]
                pltpu.make_async_copy(
                    item[side].at[cut], item[2].at[cut], sems.at[item[4] + index]
                ).start()

    pl.when(sec == layer)(lambda: go(0))
    pl.when(sec != layer)(lambda: go(1))


def arrive(own, dst, sems, cuts, index, base=0):
    cut = cuts[index]
    pltpu.make_async_copy(own.at[cut], dst.at[cut], sems.at[base + index]).wait()


def depart(src, dst, sems, cuts, index, base=0):
    cut = cuts[index]
    pltpu.make_async_copy(src.at[cut], dst.at[cut], sems.at[base + index]).start()


def rms(values):
    return lax.rsqrt(jnp.mean(values * values, axis=-1, keepdims=True) + EPS)


def slot_rows(code_row, rows, capacity):
    target = jnp.where((code_row & (SLOTS - 1)) < capacity, code_row, -1)
    return (
        lax.broadcasted_iota(jnp.int32, (rows, code_row.shape[1]), 0) == target
    ).astype(F32).astype(BF)


def slot_cols(code_col, rows, capacity):
    target = jnp.where((code_col & (SLOTS - 1)) < capacity, code_col, -1)
    return (
        lax.broadcasted_iota(jnp.int32, (code_col.shape[0], rows), 1) == target
    ).astype(F32).astype(BF)


def project(normed, w_own, w_scr, sems, cuts, q_ref, kv_ref):
    step = q_ref.shape[1]
    for index in range(3):
        arrive(w_own, w_scr, sems, cuts, index)
        part = mm(normed, w_scr[:, index * step : (index + 1) * step]).astype(BF)
        if index == 0:
            q_ref[...] = part
        else:
            kv_ref[:, (index - 1) * step : index * step] = part


def fill_bias(vectors, out_ref, done=None):
    heads, rows, width = out_ref.shape
    lanes = vectors.shape[1]
    sub = lax.broadcasted_iota(jnp.int32, (8, lanes), 0)
    for head in range(heads):
        base = jnp.broadcast_to(vectors[head : head + 1, :], (8, lanes))
        for bit in (1, 2, 4):
            base = jnp.where((sub & bit) != 0, pltpu.roll(base, bit, 1), base)
        for block in range(rows // 8):
            moved = pltpu.roll(base, (8 * block - (rows - 1)) % lanes, 1)
            out_ref[head, 8 * block : 8 * block + 8, :] = moved[:, :width]
        if done is not None:
            done(head)


GAIN_M, ROUTER = 1, 2


def pack_kernel(
    place_ref,
    gain_a,
    gain_m,
    router,
    route,
    slot,
    table,
    tokens,
    cotangent,
    out_ref,
    code_ref,
    tok_ref,
    cot_ref,
):
    ctx = place_ref[1]
    experts = router.shape[0]
    rows = route.shape[2]
    out_ref[...] = jnp.zeros(out_ref.shape, F32)
    out_ref[0:1, :] = gain_a[...]
    out_ref[GAIN_M : GAIN_M + 1, :] = gain_m[...]
    out_ref[ROUTER : ROUTER + experts, :] = router[...]
    at = ROUTER + experts
    code = [(route[micro] * SLOTS + slot[micro]).astype(F32) for micro in range(2)]
    out_ref[at : at + 1, :rows] = code[0]
    out_ref[at + 1 : at + 2, :rows] = code[1]
    at += 2
    out_ref[at : at + table.shape[0], : table.shape[1]] = table[...]
    tok_ref[...] = jnp.where(ctx == 0, tokens[1], tokens[0])
    code_ref[...] = jnp.zeros(code_ref.shape, F32)
    code_ref[0:1, :rows] = jnp.where(ctx == 0, code[1], code[0])
    cot_ref[...] = jnp.where(ctx == 0, cotangent[1], cotangent[0])


def pack(place, gain_a, gain_m, router, route, slot, table, tokens, cotangent):
    rows, width = tokens.shape[1:]
    height = ROUTER + router.shape[0] + route.shape[0] + table.shape[0]
    return call(
        pack_kernel,
        "pack",
        cost(1e6, 2e6),
        [(place, SM), gain_a, gain_m, router, route, slot, table, tokens, cotangent],
        [sds((height, width), F32), sds((8, 256), F32)] + [sds((rows, width), BF)] * 2,
    )


def prepare_kernel(
    place_ref, buckets_ref, packs_ref, come_ref, up_hbm, onehot_ref, bias_hbm, vec_ref, *rest
):
    *outs, up_copy, bias_ref, bucket_scr, up_scr, leave, enter, moving = rest
    step = up_hbm.shape[0] // 4
    pieces = [pl.ds(index * step, step) for index in range(4)]
    for index, cut in enumerate(pieces):
        pltpu.make_async_copy(up_hbm.at[cut], up_scr.at[cut], enter.at[index]).start()
    sec, ctx = place_ref[0], place_ref[1]
    first = sec == 0
    experts = outs[2].shape[0]
    rows = outs[3].shape[1]
    heads = bias_ref.shape[0]
    bucket_count = onehot_ref.shape[0]
    bucket_scr[...] = jnp.full(bucket_scr.shape, -1, jnp.int32)
    bucket_scr[:, : buckets_ref.shape[1]] = buckets_ref[...]
    wide = bucket_scr[...]
    span = jnp.where(first, pltpu.roll(wide, wide.shape[1] - rows, 1), wide)[:, :SHIFT]
    lane = lax.broadcasted_iota(jnp.int32, span.shape, 1)
    span = jnp.where(lane < 3 * rows - 1, span, -1)
    onehot = lax.broadcasted_iota(jnp.int32, onehot_ref.shape, 0) == span
    onehot = jnp.where(onehot, 1.0, 0.0)
    onehot_ref[...] = onehot
    height = packs_ref.shape[0] // 2
    packs = packs_ref[:height], packs_ref[height:]
    at = ROUTER + experts + 2
    tables = [item[at : at + heads, :bucket_count] for item in packs]

    def copy(head):
        return pltpu.make_async_copy(bias_ref.at[head], bias_hbm.at[head], leave.at[head])


    def done(head):
        copy(head).start()
        if head % 2 == 0 and head // 2 < len(pieces):
            index = head // 2
            cut = pieces[index]
            pltpu.make_async_copy(up_hbm.at[cut], up_scr.at[cut], enter.at[index]).wait()
            pltpu.make_async_copy(up_scr.at[cut], up_copy.at[cut], moving.at[index]).start()

    fill_bias(mm(tables[0], onehot, NN, HIGH), bias_ref, done)
    vec_ref[...] = mm(tables[1], onehot, NN, HIGH)
    at = ROUTER + experts
    home = sec == ctx
    eye = lax.broadcasted_iota(jnp.int32, (rows, rows), 0) == lax.broadcasted_iota(
        jnp.int32, (rows, rows), 1
    )
    for layer in range(2):
        pair = packs[layer][at : at + 2, :rows]
        row = jnp.where(ctx == 0, pair[0:1], pair[1:2])
        row = jnp.where(home, row, come_ref[8 * layer : 8 * layer + 1, :rows])
        col = jnp.sum(jnp.where(eye, row, 0.0), axis=1, keepdims=True)
        for index, item in enumerate(
            (
                packs[layer][0:1],
                packs[layer][GAIN_M : GAIN_M + 1],
                packs[layer][ROUTER : ROUTER + experts],
                row.astype(jnp.int32),
                col.astype(jnp.int32),
            )
        ):
            outs[5 * layer + index][...] = item
    for head in range(heads):
        copy(head).wait()
    for index, cut in enumerate(pieces):
        pltpu.make_async_copy(up_scr.at[cut], up_copy.at[cut], moving.at[index]).wait()


def prepare(place, buckets, packs, come, up, sizes, rows, lanes, deps):
    experts, heads, bucket_count = sizes
    width = packs.shape[1]
    each = [
        sds((1, width), F32),
        sds((1, width), F32),
        sds((experts, width), F32),
        sds((1, rows), jnp.int32),
        sds((rows, 1), jnp.int32),
    ]
    return call(
        prepare_kernel,
        "prepare",
        cost(1e7, 4e6),
        [(place, SM), buckets, packs, come, (up, ANY)],
        [
            sds((bucket_count, SHIFT), F32),
            (sds((heads, rows, lanes), F32), ANY),
            sds((heads, SHIFT), F32),
            *each,
            *each,
            (sds(up.shape, BF), ANY),
        ],
        [
            pltpu.VMEM((heads, rows, lanes), F32),
            pltpu.VMEM((1, 2 * SHIFT), jnp.int32),
            pltpu.VMEM(up.shape, BF),
            pltpu.SemaphoreType.DMA((heads,)),
            pltpu.SemaphoreType.DMA((4,)),
            pltpu.SemaphoreType.DMA((4,)),
        ],
        deps,
    )


def bias_kernel(vec_ref, out_ref):
    fill_bias(vec_ref[...], out_ref)


def bias_table(vectors, rows, width, deps):
    return call(
        bias_kernel,
        "bias_table",
        cost(1e7, 4e6),
        [vectors],
        [sds((vectors.shape[0], rows, width), F32)],
        deps=deps,
    )[0]


def chosen_block(place_ref, both_ref, come_ref):
    sec, ctx = place_ref[0], place_ref[1]
    mine = jnp.where(ctx == 0, both_ref[0], both_ref[1])
    return jnp.where(sec == ctx, mine, come_ref[...])


def first_kernel(
    layer,
    place_ref,
    both_ref,
    come_ref,
    packs_ref,
    w_own,
    w_other,
    x_ref,
    normed_ref,
    q_ref,
    kv_ref,
    w_scr,
    sems,
):
    cuts = col_cuts(w_scr.shape[1], w_scr.shape[1] // 3)
    fetch(place_ref[0], layer, w_own, w_other, w_scr, sems, cuts)
    rounded = chosen_block(place_ref, both_ref, come_ref)
    x_ref[...] = rounded
    x = rounded.astype(F32)
    at = layer * (packs_ref.shape[0] // 2)
    normed = (x * rms(x) * packs_ref[at : at + 1]).astype(BF)
    normed_ref[...] = normed
    project(normed, w_own, w_scr, sems, cuts, q_ref, kv_ref)


def first_projection(layer, place, both, come, packs, w):
    rows, width = both.shape[1:]
    wide = w[0].shape[1]
    return call(
        functools.partial(first_kernel, layer),
        "first_projection",
        cost(2 * rows * width * wide, 2 * width * wide),
        [(place, SM), both, come, packs, *far(w)],
        [sds((rows, width), BF)] * 3 + [sds((rows, 2 * width), BF)],
        [pltpu.VMEM((width, wide), BF), pltpu.SemaphoreType.DMA((3,))],
    )


def attend_kernel(
    layer,
    capacity,
    sec_ref,
    x_ref,
    q_ref,
    kv_ref,
    gain_ref,
    router_ref,
    row_ref,
    bias_hbm,
    wo_own,
    wo_other,
    *rest,
):
    if layer == 0:
        move_hbm, mid_ref, probs_ref, att_ref, p_ref, out_ref, moved_hbm, *rest, moving = rest
        bias_scr, wo_scr, p_scr, sems, leave, move_scr = rest
        pltpu.make_async_copy(move_hbm, move_scr, moving.at[0]).start()
    else:
        mid_ref, probs_ref, att_ref, p_ref, out_ref, bias_scr, wo_scr, p_scr, sems, leave = rest

    sec = sec_ref[0]
    rows, width = x_ref.shape
    total = kv_ref.shape[0]
    pairs = width // PAIR
    for pair in range(pairs):
        pltpu.make_async_copy(
            bias_hbm.at[pl.ds(2 * pair, 2)], bias_scr.at[pl.ds(2 * pair, 2)], sems.at[pair]
        ).start()
    cuts = [(slice(None), slice(None))]
    fetch(sec, layer, wo_own, wo_other, wo_scr, sems, cuts, pairs)
    low = lax.broadcasted_iota(jnp.int32, (rows, PAIR), 1) < HEAD
    zero = jnp.zeros((rows, PAIR), BF)
    for pair in range(pairs):
        pltpu.make_async_copy(
            bias_hbm.at[pl.ds(2 * pair, 2)], bias_scr.at[pl.ds(2 * pair, 2)], sems.at[pair]
        ).wait()
    for pair in range(pairs):
        part = slice(pair * PAIR, (pair + 1) * PAIR)
        q = q_ref[:, part]
        k = kv_ref[:, part]
        v = kv_ref[:, width + pair * PAIR : width + (pair + 1) * PAIR]
        both = []
        for side in range(2):
            head = 2 * pair + side
            masked = jnp.where(low, q, zero) if side == 0 else jnp.where(low, zero, q)
            scores = mm(masked, k, NT) * 0.125 + bias_scr[head, :, :total]
            top = jnp.max(scores, axis=-1, keepdims=True)
            raised = jnp.exp(scores - top)
            share = (raised * (1.0 / jnp.sum(raised, axis=-1, keepdims=True))).astype(BF)
            p_scr[head] = share
            both.append(mm(share, v))
        att_ref[:, part] = jnp.where(low, both[0], both[1]).astype(BF)
    for pair in range(pairs):
        pltpu.make_async_copy(
            p_scr.at[pl.ds(2 * pair, 2)], p_ref.at[pl.ds(2 * pair, 2)], leave.at[pair]
        ).start()
    if layer == 0:
        pltpu.make_async_copy(move_hbm, move_scr, moving.at[0]).wait()
        pltpu.make_async_copy(move_scr, moved_hbm, moving.at[1]).start()
    arrive(wo_own, wo_scr, sems, cuts, 0, pairs)
    middle = x_ref[...].astype(F32) + mm(att_ref[...], wo_scr[...])
    mid_ref[...] = middle
    normed = middle * rms(middle) * gain_ref[...]
    logits = mm(normed, router_ref[...], NT, HIGH)
    raised = jnp.exp(logits - jnp.max(logits, axis=-1, keepdims=True))
    probs_ref[...] = raised / jnp.sum(raised, axis=-1, keepdims=True)
    slots = slot_rows(row_ref[...], out_ref.shape[0], capacity)
    out_ref[...] = mm(slots, normed.astype(BF)).astype(BF)
    for pair in range(pairs):
        pltpu.make_async_copy(
            p_scr.at[pl.ds(2 * pair, 2)], p_ref.at[pl.ds(2 * pair, 2)], leave.at[pair]
        ).wait()
    if layer == 0:
        pltpu.make_async_copy(move_scr, moved_hbm, moving.at[1]).wait()


def attend(layer, capacity, sec, x, q, kv, gain, router, code_row, bias, wo, move=()):
    rows, width = x.shape
    experts = router.shape[0]
    heads = width // HEAD
    wide = bias.shape[2]
    return call(
        functools.partial(attend_kernel, layer, capacity),
        "attend",
        cost(4e9, 6e6),
        [(sec, SM), x, q, kv, gain, router, code_row, (bias, ANY), *far(wo), *far(move)],
        [
            sds((rows, width), F32),
            sds((rows, experts), F32),
            sds((rows, width), BF),
            (sds((heads, rows, 2 * rows), BF), ANY),
            sds((experts * SLOTS, width), BF),
            *[(sds(item.shape, BF), ANY) for item in move],
        ],
        [
            pltpu.VMEM((heads, rows, wide), F32),
            pltpu.VMEM((width, width), BF),
            pltpu.VMEM((heads, rows, 2 * rows), BF),
            pltpu.SemaphoreType.DMA((heads // 2 + 1,)),
            pltpu.SemaphoreType.DMA((heads // 2,)),
            *[pltpu.VMEM(item.shape, BF) for item in move],
            *[pltpu.SemaphoreType.DMA((2,)) for item in move],
        ],
    )


def expert_kernel(
    layer,
    sec_ref,
    rec_ref,
    in_own,
    in_other,
    out_own,
    out_other,
    res_ref,
    act_hbm,
    slope_hbm,
    win,
    wout,
    act_ref,
    slope_ref,
    sems,
    leave,
):
    sec = sec_ref[0]
    hidden = win.shape[1]
    step = 512
    count = hidden // step
    in_cuts = col_cuts(hidden, step)
    out_cuts = row_cuts(hidden, step)
    items = [(in_own, in_other, win, in_cuts, 0), (out_own, out_other, wout, out_cuts, count)]
    fetch_all(sec, layer, items, sems)
    rec = rec_ref[...]
    total = None
    arrive(in_own, win, sems, in_cuts, 0)
    later = mm(rec, win[:, :step])
    for index in range(count):
        part = slice(index * step, (index + 1) * step)
        v = later
        if index + 1 < count:
            arrive(in_own, win, sems, in_cuts, index + 1)
        arrive(out_own, wout, sems, out_cuts, index, count)
        if index + 1 < count:
            later = mm(rec, win[:, (index + 1) * step : (index + 2) * step])
        square = v * v
        t = jnp.tanh(v * (0.7978845608028654 + 0.035677408136300125 * square))
        half = 0.5 * t + 0.5
        rising = v * half
        active = rising.astype(BF)
        act_ref[:, part] = active
        slope = half + (rising - rising * half) * (
            1.5957691216057308 + 0.21406444881780074 * square
        )
        slope_ref[:, part] = slope.astype(BF)
        fresh = mm(active, wout[part, :])
        total = fresh if total is None else total + fresh
        depart(act_ref, act_hbm, leave, in_cuts, index)
        depart(slope_ref, slope_hbm, leave, in_cuts, index, count)
    res_ref[...] = total.astype(BF)
    for index in range(count):
        arrive(act_ref, act_hbm, leave, in_cuts, index)
        arrive(slope_ref, slope_hbm, leave, in_cuts, index, count)


def expert_forward(layer, sec, received, w_in, w_out, deps=()):
    rows, width = received.shape
    hidden = w_in[0].shape[1]
    count = hidden // 512
    return call(
        functools.partial(expert_kernel, layer),
        "expert_forward",
        cost(4 * rows * width * hidden, 4 * width * hidden),
        [(sec, SM), received, *far(w_in), *far(w_out)],
        [sds((rows, width), BF)] + [(sds((rows, hidden), BF), ANY)] * 2,
        [
            pltpu.VMEM((width, hidden), BF),
            pltpu.VMEM((hidden, width), BF),
            pltpu.VMEM((rows, hidden), BF),
            pltpu.VMEM((rows, hidden), BF),
            pltpu.SemaphoreType.DMA((2 * count,)),
            pltpu.SemaphoreType.DMA((2 * count,)),
        ],
        deps,
    )


def gate_of(probs, code_col):
    lane = lax.broadcasted_iota(jnp.int32, probs.shape, 1)
    chosen = (lane == code_col // SLOTS).astype(F32)
    return chosen, jnp.sum(probs * chosen, axis=-1, keepdims=True)


def join_kernel(
    layer,
    capacity,
    sec_ref,
    mid_ref,
    ret_ref,
    probs_ref,
    col_ref,
    gain_ref,
    w_own,
    w_other,
    comb_ref,
    hid_ref,
    normed_ref,
    q_ref,
    kv_ref,
    w_scr,
    sems,
):
    cuts = col_cuts(w_scr.shape[1], w_scr.shape[1] // 3)
    fetch(sec_ref[0], layer, w_own, w_other, w_scr, sems, cuts)
    col = col_ref[...]
    combined = mm(slot_cols(col, ret_ref.shape[0], capacity), ret_ref[...])
    comb_ref[...] = combined.astype(BF)
    _, gate = gate_of(probs_ref[...], col)
    hidden = (mid_ref[...] + gate * combined).astype(BF)
    hid_ref[...] = hidden
    x = hidden.astype(F32)
    normed = (x * rms(x) * gain_ref[...]).astype(BF)
    normed_ref[...] = normed
    project(normed, w_own, w_scr, sems, cuts, q_ref, kv_ref)


def join(layer, capacity, sec, middle, returned, probs, code_col, gain, w):
    rows, width = middle.shape
    wide = w[0].shape[1]
    return call(
        functools.partial(join_kernel, layer, capacity),
        "join",
        cost(2 * rows * width * wide, 2 * width * wide),
        [(sec, SM), middle, returned, probs, code_col, gain, *far(w)],
        [sds((rows, width), BF)] * 4 + [sds((rows, 2 * width), BF)],
        [pltpu.VMEM((width, wide), BF), pltpu.SemaphoreType.DMA((3,))],
    )


def pack_rows(ref, base, values):
    height, width = values.shape
    for row in range(height):
        for at in range(width // 128):
            place = base + row * (width // 128) + at
            ref[place : place + 1, :] = values[row : row + 1, at * 128 : (at + 1) * 128]


def send_back(g, combined, probs, row, col, rows, capacity):
    _, gate = gate_of(probs, col)
    gate_grad = jnp.sum(g * combined, axis=-1, keepdims=True)
    placed = mm(slot_rows(row, rows, capacity), (gate * g).astype(BF))
    return gate_grad, placed.astype(BF)


def turn_kernel(
    capacity,
    place_ref,
    mid_ref,
    ret_ref,
    probs_ref,
    row_ref,
    col_ref,
    both_ref,
    come_ref,
    hid_ref,
    g_ref,
    gate_grad_ref,
    out_ref,
):
    g = chosen_block(place_ref, both_ref, come_ref)
    g_ref[...] = g
    col = col_ref[...]
    probs = probs_ref[...]
    combined = mm(slot_cols(col, ret_ref.shape[0], capacity), ret_ref[...])
    _, gate = gate_of(probs, col)
    hid_ref[...] = (mid_ref[...] + gate * combined).astype(BF)
    gate_grad_ref[...], out_ref[...] = send_back(
        g.astype(F32), combined, probs, row_ref[...], col, out_ref.shape[0], capacity
    )


def turn(capacity, place, middle, returned, probs, code_row, code_col, both, come):
    rows, width = middle.shape
    return call(
        functools.partial(turn_kernel, capacity),
        "turn",
        cost(4 * rows * width * returned.shape[0], 3e6),
        [(place, SM), middle, returned, probs, code_row, code_col, both, come],
        [
            sds((rows, width), BF),
            sds((rows, width), BF),
            sds((rows, 1), F32),
            sds(returned.shape, BF),
        ],
    )


def expert_back_kernel(
    layer,
    sec_ref,
    rec_ref,
    slope_hbm,
    in_own,
    in_other,
    out_own,
    out_other,
    sent_ref,
    grad_hbm,
    win,
    wout,
    slope_ref,
    grad_ref,
    sems,
    leave,
):
    sec = sec_ref[0]
    hidden = win.shape[1]
    step = 512
    count = hidden // step
    in_cuts = col_cuts(hidden, step)
    out_cuts = row_cuts(hidden, step)
    items = [(out_own, out_other, wout, out_cuts, count), (in_own, in_other, win, in_cuts, 0)]
    for index in range(count):
        depart(slope_hbm, slope_ref, sems, in_cuts, index, 2 * count)
    fetch_all(sec, layer, items, sems)
    rec = rec_ref[...]
    total = None
    arrive(out_own, wout, sems, out_cuts, 0, count)
    later = mm(rec, wout[:step, :], NT)
    for index in range(count):
        part = slice(index * step, (index + 1) * step)
        now = later
        if index + 1 < count:
            arrive(out_own, wout, sems, out_cuts, index + 1, count)
        arrive(slope_hbm, slope_ref, sems, in_cuts, index, 2 * count)
        arrive(in_own, win, sems, in_cuts, index)
        if index + 1 < count:
            later = mm(rec, wout[(index + 1) * step : (index + 2) * step, :], NT)
        inner = (now * slope_ref[:, part].astype(F32)).astype(BF)
        grad_ref[:, part] = inner
        fresh = mm(inner, win[:, part], NT)
        total = fresh if total is None else total + fresh
        depart(grad_ref, grad_hbm, leave, in_cuts, index)
    sent_ref[...] = total.astype(BF)
    for index in range(count):
        arrive(grad_ref, grad_hbm, leave, in_cuts, index)


def expert_backward(layer, sec, received, slope, w_in, w_out, deps=()):
    rows, width = received.shape
    hidden = w_in[0].shape[1]
    count = hidden // 512
    return call(
        functools.partial(expert_back_kernel, layer),
        "expert_backward",
        cost(4 * rows * width * hidden, 4 * width * hidden),
        [(sec, SM), received, (slope, ANY), *far(w_in), *far(w_out)],
        [sds((rows, width), BF), (sds((rows, hidden), BF), ANY)],
        [
            pltpu.VMEM((width, hidden), BF),
            pltpu.VMEM((hidden, width), BF),
            pltpu.VMEM((rows, hidden), BF),
            pltpu.VMEM((rows, hidden), BF),
            pltpu.SemaphoreType.DMA((3 * count,)),
            pltpu.SemaphoreType.DMA((count,)),
        ],
        deps,
    )


def expert_weight_kernel(half_ref, *refs):
    rec, grad, act, res, rec_b, grad_b, act_b, res_b, out_ref, turned = refs
    rows, half = rec.shape

    @pl.when(pl.program_id(0) == 0)
    def _():
        turned[:, :rows] = rec[...].T
        turned[:, rows:] = rec_b[...].T

    upper = mm(turned[:, :rows], grad[...]) + mm(turned[:, rows:], grad_b[...])
    out_ref[0, :half] = upper.astype(BF)
    lower = mm(act[...], res[...], TN) + mm(act_b[...], res_b[...], TN)
    out_ref[0, half : 2 * half] = lower.astype(BF)


def expert_weights(half, blocks, own, other):
    rows, width = own[0].shape
    hidden = own[1].shape[1]
    step = hidden // blocks
    cut = width // 2
    narrow = pl.BlockSpec((rows, cut), lambda b, half_ref: (0, half_ref[0]))
    moving = pl.BlockSpec((rows, step), lambda b, half_ref: (0, b))
    return pl.pallas_call(
        expert_weight_kernel,
        out_shape=sds((blocks, width, step), BF),
        grid_spec=pltpu.PrefetchScalarGridSpec(
            num_scalar_prefetch=1,
            grid=(blocks,),
            in_specs=[narrow, moving, moving, narrow] * 2,
            out_specs=pl.BlockSpec((1, width, step), lambda b, half_ref: (b, 0, 0)),
            scratch_shapes=[pltpu.VMEM((cut, 2 * rows), BF)],
        ),
        compiler_params=params(),
        cost_estimate=cost(4 * rows * width * hidden, 4 * width * hidden),
        name="expert_weights",
    )(half, *own, *other)


def attend_back_kernel(
    layer,
    capacity,
    sec_ref,
    g_ref,
    mid_ref,
    sent_ref,
    col_ref,
    probs_ref,
    gate_grad_ref,
    gain_ref,
    router_ref,
    q_ref,
    kv_ref,
    onehot_ref,
    p_hbm,
    wo_own,
    wo_other,
    mid_grad_ref,
    branch_ref,
    dq_ref,
    own_ref,
    other_ref,
    small_ref,
    dkv_scr,
    diag_scr,
    p_scr,
    wo_scr,
    sems,
):
    sec = sec_ref[0]
    rows, width = mid_ref.shape
    total = kv_ref.shape[0]
    pairs = width // PAIR
    lanes = diag_scr.shape[1]
    cuts = [(slice(None), slice(None))]
    fetch(sec, layer, wo_own, wo_other, wo_scr, sems, cuts, pairs)
    for pair in range(pairs):
        pltpu.make_async_copy(
            p_hbm.at[pl.ds(2 * pair, 2)], p_scr.at[pl.ds(2 * pair, 2)], sems.at[pair]
        ).start()

    middle = mid_ref[...]
    scale = rms(middle)
    unit = middle * scale
    gain = gain_ref[...]
    col = col_ref[...]
    probs = probs_ref[...]
    chosen, gate = gate_of(probs, col)
    logit_grad = probs * (chosen - gate) * gate_grad_ref[...]
    normed_grad = mm(slot_cols(col, sent_ref.shape[0], capacity), sent_ref[...])
    normed_grad = normed_grad + mm(logit_grad, router_ref[...], NN, HIGH)
    experts = probs.shape[1]
    router_grad = mm(logit_grad, unit * gain, TN, HIGH)
    gain_grad = jnp.sum(normed_grad * unit, axis=0, keepdims=True)
    pack_rows(small_ref, 0, router_grad)
    pack_rows(small_ref, experts * (width // 128), gain_grad)
    unit_grad = normed_grad * gain
    middle_grad = g_ref[...].astype(F32) + scale * (
        unit_grad - unit * jnp.mean(unit_grad * unit, axis=-1, keepdims=True)
    )
    mid_grad_ref[...] = middle_grad
    branch = middle_grad.astype(BF)
    branch_ref[...] = branch
    arrive(wo_own, wo_scr, sems, cuts, 0, pairs)
    att_grad = mm(branch, wo_scr[...], NT).astype(BF)

    low = lax.broadcasted_iota(jnp.int32, (rows, PAIR), 1) < HEAD
    low_wide = lax.broadcasted_iota(jnp.int32, (total, PAIR), 1) < HEAD
    zero = jnp.zeros((rows, PAIR), BF)
    pad = jnp.zeros((rows, lanes - total), F32)
    sub = lax.broadcasted_iota(jnp.int32, (8, lanes), 0)
    for pair in range(pairs):
        pltpu.make_async_copy(
            p_hbm.at[pl.ds(2 * pair, 2)], p_scr.at[pl.ds(2 * pair, 2)], sems.at[pair]
        ).wait()
    for pair in range(pairs):
        part = slice(pair * PAIR, (pair + 1) * PAIR)
        later = slice(width + pair * PAIR, width + (pair + 1) * PAIR)
        q = q_ref[:, part]
        k = kv_ref[:, part]
        v = kv_ref[:, later]
        da = att_grad[:, part]
        dqs, dks, dvs = [], [], []
        for side in range(2):
            head = 2 * pair + side
            masked = jnp.where(low, da, zero) if side == 0 else jnp.where(low, zero, da)
            share = p_scr[head]
            wide = share.astype(F32)
            dp = mm(masked, v, NT)
            ds = wide * (dp - jnp.sum(wide * dp, axis=-1, keepdims=True))
            dsb = ds.astype(BF)
            dqs.append(mm(dsb, k))
            dks.append(mm(dsb, q, TN))
            dvs.append(mm(share, da, TN))
            padded = jnp.concatenate([ds, pad], axis=1)
            fold = None
            for block in range(rows // 8):
                moved = pltpu.roll(
                    padded[8 * block : 8 * block + 8], (rows - 1 - 8 * block) % lanes, 1
                )
                fold = moved if fold is None else fold + moved
            for bit in (1, 2, 4):
                fold = jnp.where((sub & bit) != 0, pltpu.roll(fold, lanes - bit, 1), fold)
            diag_scr[head : head + 1, :] = jnp.sum(fold, axis=0, keepdims=True)
        dq_ref[:, part] = (jnp.where(low, dqs[0], dqs[1]) * 0.125).astype(BF)
        dkv_scr[:, part] = (jnp.where(low_wide, dks[0], dks[1]) * 0.125).astype(BF)
        dkv_scr[:, later] = jnp.where(low_wide, dvs[0], dvs[1]).astype(BF)
    table = mm(diag_scr[...], onehot_ref[...], NT, HIGH)
    buckets = onehot_ref.shape[0]
    base = (experts + 1) * (width // 128)
    for head in range(2 * pairs):
        at = head * buckets
        small_ref[base + at // 128 : base + at // 128 + 1, at % 128 : at % 128 + buckets] = table[
            head : head + 1, :
        ]
    own_ref[...] = dkv_scr[pl.ds(pl.multiple_of(sec * rows, rows), rows), :]
    other_ref[...] = dkv_scr[pl.ds(pl.multiple_of((1 - sec) * rows, rows), rows), :]


def attend_backward(
    layer,
    capacity,
    sec,
    g,
    middle,
    sent,
    code_col,
    probs,
    gate_grad,
    gain,
    router,
    q,
    kv,
    onehot,
    shares,
    wo,
    deps,
):
    rows, width = middle.shape
    heads = width // HEAD
    experts = router.shape[0]
    packed = (experts + 1) * (width // 128) + heads * onehot.shape[0] // 128
    return call(
        functools.partial(attend_back_kernel, layer, capacity),
        "attend_backward",
        cost(8e9, 6e6),
        [
            (sec, SM),
            g,
            middle,
            sent,
            code_col,
            probs,
            gate_grad,
            gain,
            router,
            q,
            kv,
            onehot,
            (shares, ANY),
            *far(wo),
        ],
        [
            sds((rows, width), F32),
            sds((rows, width), BF),
            sds((rows, width), BF),
            sds((rows, 2 * width), BF),
            sds((rows, 2 * width), BF),
            sds((packed, 128), F32),
        ],
        [
            pltpu.VMEM((2 * rows, 2 * width), BF),
            pltpu.VMEM((heads, SHIFT), F32),
            pltpu.VMEM((heads, rows, 2 * rows), BF),
            pltpu.VMEM((width, width), BF),
            pltpu.SemaphoreType.DMA((heads // 2 + 1,)),
        ],
        deps,
    )


def project_back_kernel(
    layer,
    last,
    capacity,
    sec_ref,
    dq_ref,
    own_ref,
    come_ref,
    mid_grad_ref,
    x_ref,
    gain_ref,
    small_in_ref,
    *rest,
):
    if last:
        late_ref, w_own, w_other, rows_ref, grad_ref, mine_ref, small_ref, w_scr, sems = rest
    else:
        comb_ref, probs_ref, row_ref, col_ref, w_own, w_other = rest[:6]
        rows_ref, grad_ref, small_ref, gate_grad_ref, out_ref, w_scr, sems = rest[6:]
    width = x_ref.shape[1]
    cuts = col_cuts(w_scr.shape[1], width)
    fetch(sec_ref[0], layer, w_own, w_other, w_scr, sems, cuts)
    rows_ref[:, :width] = dq_ref[...]
    rows_ref[:, width:] = (own_ref[...].astype(F32) + come_ref[...].astype(F32)).astype(BF)
    normed_grad = None
    for index in range(3):
        part = slice(index * width, (index + 1) * width)
        arrive(w_own, w_scr, sems, cuts, index)
        fresh = mm(rows_ref[:, part], w_scr[:, part], NT)
        normed_grad = fresh if normed_grad is None else normed_grad + fresh
    x = x_ref[...].astype(F32)
    scale = rms(x)
    unit = x * scale
    held = small_in_ref.shape[0]
    small_ref[:held, :] = small_in_ref[...]
    pack_rows(small_ref, held, jnp.sum(normed_grad * unit, axis=0, keepdims=True))
    held += width // 128
    small_ref[held:, :] = jnp.zeros((small_ref.shape[0] - held, 128), F32)
    if last:
        first = sec_ref[0] == 0
        early, late = small_ref[...], late_ref[...]
        mine_ref[...] = jnp.where(first, early, late)
        small_ref[...] = jnp.where(first, late, early)
    unit_grad = normed_grad * gain_ref[...]
    grad = mid_grad_ref[...] + scale * (
        unit_grad - unit * jnp.mean(unit_grad * unit, axis=-1, keepdims=True)
    )
    rounded = grad.astype(BF)
    grad_ref[...] = rounded
    if not last:
        gate_grad_ref[...], out_ref[...] = send_back(
            rounded.astype(F32),
            comb_ref[...].astype(F32),
            probs_ref[...],
            row_ref[...],
            col_ref[...],
            out_ref.shape[0],
            capacity,
        )


def project_backward(
    layer, capacity, sec, dq, own, come, middle_grad, x, gain, small, w, before
):
    rows, width = x.shape
    wide = w[0].shape[1]
    last = len(before) == 1
    packed = sds((-(-(small.shape[0] + width // 128) // 8) * 8, 128), F32)
    outs = [sds((rows, wide), BF), sds((rows, width), BF), packed]
    more = list(before)
    if last:
        outs += [packed]
    else:
        outs += [sds((rows, 1), F32), sds((before[1].shape[1] * SLOTS, width), BF)]
    return call(
        functools.partial(project_back_kernel, layer, last, capacity),
        "project_backward",
        cost(2 * rows * width * wide, 2 * width * wide),
        [(sec, SM), dq, own, come, middle_grad, x, gain, small, *more, *far(w)],
        outs,
        [pltpu.VMEM((width, wide), BF), pltpu.SemaphoreType.DMA((3,))],
    )


def spread_kernel(order, place_ref, *refs):
    own, other, out_ref = refs[:2], refs[2:4], refs[4]
    width = own[0].shape[1]
    lanes = out_ref.shape[1]
    normed = jnp.concatenate([own[0][...], other[0][...]], axis=0)
    attended = jnp.concatenate([own[1][...], other[1][...]], axis=0)
    mixed = jnp.where(place_ref[0] == 0, normed, attended)
    feature = lax.broadcasted_iota(jnp.int32, (lanes, width), 1)
    lane = lax.broadcasted_iota(jnp.int32, (lanes, 1), 0)
    block, place = lane // 16, lane % 16
    if order is not None:
        experts, copies = order
        rest = lanes // 16 // COLUMN
        column, place_in = block // rest, block % rest
        lines = experts // COLUMN
        line = place_in // copies % lines * COLUMN + column
        block = place_in // (lines * copies) * experts * copies + line * copies + place_in % copies
    base = block * 12
    main = jnp.where(place < 12, base + place, -1)
    late = [jnp.where(place < 12, -1, base + 4 * group + place - 12) for group in range(3)]
    for index, (values, source) in enumerate(
        [(normed, main), (mixed, main), (mixed, late[0]), (mixed, late[1]), (mixed, late[2])]
    ):
        hit = jnp.where(feature == source, 1.0, 0.0).astype(BF)
        out_ref[index] = mm(hit, values, NT).astype(BF)


def spread_features(place, shards, own, other, order=None):
    rows = own[0].shape[0]
    return call(
        functools.partial(spread_kernel, order),
        "spread_features",
        cost(3e9, 4e6),
        [(place, SM), *own, *other],
        [sds((5, shards * 16, 2 * rows), BF)],
    )[0]


def projection_weight_kernel(place_ref, left_hbm, *refs):
    own, other = refs[:2], refs[2:4]
    out_hbm, left, out_ref, sems, leave = refs[-5:]
    step = out_ref.shape[1] // 3
    first = place_ref[0] == 0
    for index in range(5):
        pltpu.make_async_copy(left_hbm.at[index], left.at[index], sems.at[index]).start()

    def columns(group):
        late = 4 + group
        parts = []
        for rows_ref, branch_ref in (own, other):
            upper = rows_ref[:, group * step : (group + 1) * step]
            if late < 6:
                lower = rows_ref[:, late * step : (late + 1) * step]
            else:
                lower = branch_ref[:, (late - 6) * step : (late - 5) * step]
            parts.append(jnp.where(first, upper, lower))
        return jnp.concatenate(parts, axis=0)

    def copy(group):
        return pltpu.make_async_copy(
            out_ref.at[:, pl.ds(group * step, step)],
            out_hbm.at[:, pl.ds(group * step, step)],
            leave.at[group],
        )

    for index in range(5):
        pltpu.make_async_copy(left_hbm.at[index], left.at[index], sems.at[index]).wait()
    tail = columns(3)
    for group in range(3):
        total = mm(left[0 if group < 2 else 1], columns(group)) + mm(left[2 + group], tail)
        out_ref[:, group * step : (group + 1) * step] = total.astype(BF)
        copy(group).start()
    for group in range(3):
        copy(group).wait()


def projection_weights(place, left, own, other, spare, deps=()):
    wide = (own[0].shape[1] + own[1].shape[1]) // 8 * 3
    height = left.shape[1]
    return call(
        projection_weight_kernel,
        "projection_weights",
        cost(2e9, 8e6),
        [(place, SM), (left, ANY), *own, *other],
        [(sds((height, wide + spare), BF), ANY)],
        [
            pltpu.VMEM(left.shape, BF),
            pltpu.VMEM((height, wide), BF),
            pltpu.SemaphoreType.DMA((5,)),
            pltpu.SemaphoreType.DMA((3,)),
        ],
        deps,
    )[0]


def ride_kernel(shares_ref, held_hbm, out_hbm, scr, sem):
    shards = shares_ref.shape[0]
    total = jnp.sum(shares_ref[...], axis=0)
    high = total.astype(BF).astype(F32)
    row = lax.broadcasted_iota(jnp.int32, scr.shape, 0) % 16
    tile = jnp.where(row == 0, high, jnp.where(row == 1, total - high, 0.0))
    scr[...] = tile.astype(BF)
    at = out_hbm.shape[1] - 128
    copy = pltpu.make_async_copy(scr, out_hbm.at[:, pl.ds(at, 128)], sem.at[0])
    copy.start()
    copy.wait()


def ride(shares, held):
    return call(
        ride_kernel,
        "ride",
        cost(1e6, 1e6),
        [shares, (held, ANY)],
        [(sds(held.shape, BF), ANY)],
        [pltpu.VMEM((held.shape[0], 128), BF), pltpu.SemaphoreType.DMA((1,))],
        aliases={1: 0},
    )[0]


def unpack_rows(total):
    width = total.shape[1]
    left = total[12:].reshape(4, 3, width // 3).transpose(1, 0, 2).reshape(12, width // 3)
    return jnp.concatenate([total[:12], left], axis=1)


def body(
    tokens,
    cotangent,
    expert_route,
    capacity_slot,
    buckets,
    qkv_weight,
    attention_out,
    relative_bias,
    attention_gain,
    mixture_gain,
    router,
    expert_in,
    expert_out,
):
    sec = lax.axis_index("section")
    ctx = lax.axis_index("context")
    place = jnp.stack([sec, ctx]).astype(jnp.int32)
    rows, width = tokens.shape[2:]
    experts = router.shape[2]
    heads = width // HEAD
    bucket_count = relative_bias.shape[1]
    capacity = (5 * rows + 4 * experts - 1) // (4 * experts)
    local = ("context", "dp")
    section = ("context", "expert", "dp")
    blocks = lax.axis_size(local)
    contexts = lax.axis_size("context")
    shards = lax.axis_size(section)
    grid = ("section", "context")

    def swap(value):
        return lax.ppermute(value, "section", SWAP)

    def pick(values, at):
        return jnp.where(at == 0, values[0], values[1])

    def come_over(value):
        return lax.ppermute(value, grid, [(0, 1), (3, 2)])

    def exchange(value):
        spread = value.reshape(experts, SLOTS, width)
        return lax.all_to_all(spread, "expert", 0, 0, tiled=True).reshape(value.shape)

    def shared(value):
        return lax.all_to_all(value, section, 0, 0, tiled=True)

    def together(value):
        return lax.all_gather(value, "section", axis=0, tiled=True)

    def both(value):
        return (value, swap(value))

    own, code_leave, tok_leave, cot_leave = pack(
        place,
        attention_gain,
        mixture_gain,
        router[0].T,
        expert_route[0],
        capacity_slot[0],
        relative_bias[0].T,
        tokens[:, 0],
        cotangent[:, 0],
    )
    tok_come = come_over(tok_leave)
    packs = together(gate(own, tok_come))
    codes_come = together(lax.ppermute(code_leave, "context", SWAP))
    w_qkv = both(qkv_weight[0])
    w_out = both(attention_out[0])
    cot_come = come_over(cot_leave)

    x, normed, q, kv, middle, probs, attended, shares = ([None] * 2 for _ in range(8))
    received, active, slope, hidden, left = ([None, None] for _ in range(5))
    x[0], normed[0], q[0], kv[0] = first_projection(
        0, place, tokens[:, 0], tok_come, packs, w_qkv
    )
    for layer in range(2):
        kv[layer] = together(kv[layer])
        if layer == 0:
            prepared = prepare(
                place,
                buckets.reshape(1, -1),
                packs,
                codes_come,
                expert_in[0, 0],
                (experts, heads, bucket_count),
                rows,
                384,
                [kv[0], w_out[1]],
            )
            onehot, bias0, vectors = prepared[:3]
            gain_a, gain_m, routers, code_rows, code_cols = zip(prepared[3:8], prepared[8:13])
            bias = [bias0, None]
            w_up = both(prepared[13])
        middle[layer], probs[layer], attended[layer], shares[layer], outgoing, *moved = attend(
            layer,
            capacity,
            place,
            x[layer],
            q[layer],
            kv[layer],
            gain_m[layer],
            routers[layer],
            code_rows[layer],
            bias[layer],
            w_out,
            () if layer else (expert_out[0, 0],),
        )
        if layer == 0:
            w_down = both(moved[0])
        received[layer] = exchange(outgoing)
        pair = (normed[layer], attended[layer])
        order = (experts, lax.axis_size("dp")) if layer else None
        left[layer] = spread_features(place, shards, pair, [swap(item) for item in pair], order)
        deps = [left[0]]
        if layer == 0:
            bias[1] = bias_table(vectors, rows, 384, [outgoing])
            deps = [bias[1]]
        result, active[layer], slope[layer] = expert_forward(
            layer, place, received[layer], w_up, w_down, deps
        )
        returned = exchange(result)
        if layer == 0:
            combined, hidden[0], normed[1], q[1], kv[1] = join(
                1, capacity, place, middle[0], returned, probs[0], code_cols[0], gain_a[1], w_qkv
            )
            x[1] = hidden[0]
        else:
            hidden[1], g, gate_grad, outgoing = turn(
                capacity,
                place,
                middle[1],
                returned,
                probs[1],
                code_rows[1],
                code_cols[1],
                cotangent[:, 0],
                cot_come,
            )

    def spread_out(values):
        one = lax.ppermute(pick(values, ctx), grid, [(0, 0), (1, 2), (2, 1), (3, 3)])
        two = lax.ppermute(pick(values, 1 - ctx), grid, [(0, 2), (1, 0), (2, 3), (3, 1)])
        return one, two

    def side_by_side(one, two):
        return jnp.stack([jnp.where(sec == 0, one, two), jnp.where(sec == 0, two, one)])

    hidden_states = side_by_side(*spread_out(hidden))

    grads, expert_sums, small = ([None, None] for _ in range(3))
    held = None
    for layer in (1, 0):
        result_grad = exchange(outgoing)
        deps = [left[1]] if layer else [held]
        sent, inner_grad = expert_backward(
            layer, place, result_grad, slope[layer], w_up, w_down, deps
        )
        operands = (received[layer], inner_grad, active[layer], result_grad)
        half = expert_weights(place, blocks, operands, [swap(item) for item in operands])
        sent = exchange(sent)
        half = gate(half, sent)
        expert_sums[layer] = lax.psum_scatter(
            half.reshape(-1, half.shape[2]), local, scatter_dimension=0, tiled=True
        )
        if layer == 0:
            late = gate(held, half).reshape(COLUMN, -1, held.shape[1])
            lines = [list(range(at, at + COLUMN)) for at in range(0, experts, COLUMN)]
            late = lax.all_to_all(late, "expert", 0, 0, axis_index_groups=lines, tiled=True)
        middle_grad, branch, dq, own, other, packed = attend_backward(
            layer,
            capacity,
            place,
            g,
            middle[layer],
            sent,
            code_cols[layer],
            probs[layer],
            gate_grad,
            gain_m[layer],
            routers[layer],
            q[layer],
            kv[layer],
            onehot,
            shares[layer],
            w_out,
            [half],
        )
        before = (combined, probs[0], code_rows[0], code_cols[0]) if layer == 1 else (small[1],)
        back = project_backward(
            layer,
            capacity,
            place,
            dq,
            own,
            swap(other),
            middle_grad,
            x[layer],
            gain_a[layer],
            packed,
            w_qkv,
            before,
        )
        rows_grad, grads[layer], small[layer] = back[:3]
        if layer == 1:
            g, gate_grad, outgoing = grads[1], back[3], back[4]
        operands = (rows_grad, branch)
        swapped = [swap(item) for item in operands]
        if layer == 1:
            held = projection_weights(place, left[1], operands, swapped, 0)
        else:
            late = jnp.sum(late.astype(F32), axis=0).astype(BF)
            held = projection_weights(place, left[0], operands, swapped, 128, [late])

    mine = small[0] + swap(back[3])
    tail = ride(shared(mine.reshape(shards, 1, 128)), held).reshape(shards, 16, -1)
    tail = shared(tail)
    whole_e = (pick(expert_sums, sec), swap(pick(expert_sums, 1 - sec)))
    first, second = pick(whole_e, sec), pick(whole_e, 1 - sec)
    mid = width // 2
    in_grad = jnp.concatenate([first[:mid], second[:mid]], axis=0).astype(F32)
    out_grad = jnp.concatenate([first[mid:], second[mid:]], axis=1).astype(F32)

    late = gate(late, tail).reshape(shards // COLUMN, 16, -1)
    copies = lax.axis_size("dp")
    planes = [
        [at for at in range(shards) if at // copies % COLUMN == column] for column in range(COLUMN)
    ]
    late = lax.all_to_all(late, section, 0, 0, axis_index_groups=planes, tiled=True)
    late = jnp.sum(late.astype(F32), axis=0)
    wide = tail.shape[2] - 128
    mine = jnp.sum(tail[:, 0:2, wide:].astype(F32), axis=1)
    flat = mine.reshape(-1)
    count = experts * width
    router_grad = flat[:count].reshape(experts, width).T
    mixture_gain_grad = flat[count : count + width]
    count += width
    relative_grad = flat[count : count + heads * bucket_count].reshape(heads, bucket_count).T
    count += heads * bucket_count
    attention_gain_grad = flat[count : count + width]

    total = jnp.sum(tail[:, :, :wide].astype(F32), axis=0)
    projections = [unpack_rows(total), unpack_rows(late)]
    whole = (pick(projections, sec), swap(pick(projections, 1 - sec)))
    whole = jnp.concatenate([pick(whole, sec), pick(whole, 1 - sec)], axis=1)
    cut = qkv_weight.shape[2]

    input_grads = side_by_side(*[gate(item, late) for item in spread_out(grads)]).astype(F32)
    return (
        hidden_states[None, :, None],
        input_grads[None, :, None],
        whole[None, :, :cut],
        whole[None, :, cut:],
        relative_grad[None],
        attention_gain_grad[None],
        mixture_gain_grad[None],
        router_grad[None],
        in_grad[None, None],
        out_grad[None, None],
    )


def solution(mesh):
    return jax.shard_map(
        body,
        mesh=mesh,
        in_specs=(
            P(None, ("expert", "dp"), "context", None),
            P(None, ("expert", "dp"), "context", None),
            P("section", None, ("expert", "dp"), "context"),
            P("section", None, ("expert", "dp"), "context"),
            P(),
            P("section", None, None),
            P("section", None, None),
            P("section", None, None),
            P("section", None),
            P("section", None),
            P("section", None, None),
            P("section", "expert", None, None),
            P("section", "expert", None, None),
        ),
        out_specs=(
            P("section", None, ("expert", "dp"), "context", None),
            P("section", None, ("expert", "dp"), "context", None),
            P("section", ("context", "expert", "dp"), None),
            P("section", ("context", "expert", "dp"), None),
            P("section", None, None),
            P("section", None),
            P("section", None),
            P("section", None, None),
            P("section", "expert", None, ("context", "dp")),
            P("section", "expert", ("context", "dp"), None),
        ),
        check_vma=False,
    )
```
